32 devices in a mesh: fs: 4 (over y, x), ctx: 8 (over z, core).
Axes of the slice: x: 2, y: 2, z: 4, core: 2. Of those that a mesh axis runs over, the one named last changes fastest.
Arguments:
- hidden_in: bfloat16 [8, 2048, 2560], P('fs', 'ctx'), may hold values from -6 to 6
- doc_lengths: int32 [8, 4], P('fs'), may hold values from 1 to 2048, as said below
- attn_gain: bfloat16 [2560], P('fs'), may hold values from 0.5 to 1.5
- query_weight: bfloat16 [2560, 2560], P('fs'), may hold values from -0.15625 to 0.15625
- key_matrix: bfloat16 [2560, 640], P('fs'), may hold values from -0.125 to 0.125
- value_matrix: bfloat16 [2560, 640], P('fs'), may hold values from -0.125 to 0.125
- output_weight: bfloat16 [2560, 2560], P('fs'), may hold values from -1 to 1
- mlp_gain: bfloat16 [2560], P('fs'), may hold values from 0.5 to 1.5
- gate_weight: bfloat16 [2560, 7168], P('fs'), may hold values from -0.125 to 0.125
- up_weight: bfloat16 [2560, 7168], P('fs'), may hold values from -0.125 to 0.125
- down_weight: bfloat16 [7168, 2560], P('fs'), may hold values from -0.0625 to 0.0625
- out_grad: bfloat16 [8, 2048, 2560], P('fs', 'ctx'), may hold values from -6 to 6
Outputs:
- hidden_out: float32 [8, 2048, 2560], P('fs', 'ctx')
- hidden_grad: float32 [8, 2048, 2560], P('fs', 'ctx')
- attn_gain_grad: float32 [2560], P('fs')
- query_grad: float32 [2560, 2560], P('fs', 'ctx')
- key_grad: float32 [2560, 640], P('fs', 'ctx')
- value_grad: float32 [2560, 640], P('fs', 'ctx')
- output_grad: float32 [2560, 2560], P('fs', 'ctx')
- mlp_gain_grad: float32 [2560], P('fs')
- gate_grad: float32 [2560, 7168], P('fs', 'ctx')
- up_grad: float32 [2560, 7168], P('fs', 'ctx')
- down_grad: float32 [7168, 2560], P('fs', 'ctx')
The draws below stay inside these ranges and needn't reach their ends.
Inputs may be any that keep to these rules, and one draw needn't show every extreme that they name: `doc_lengths`: each row holds the lengths of the 4 documents of one sequence, in order; they sum to 2048.
All inputs are finite; a program needn't handle non-finite values.
Results may differ from the reference program's by a relative error of at most 0.02.
Values may be sent and summed in bfloat16 or wider, within the bound.
A program may use at most 512 MiB of HBM per device.

```python
import math
import jax
import jax.numpy as jnp
from jax import lax

MODEL_WIDTH = 2560
QUERY_HEADS = 32
KEY_VALUE_HEADS = 8
HEAD_SIZE = 80
FF = 7168
WINDOW = 1024
SEQUENCE_LENGTH = 2048
MB = 2
DOCS = 4
SEQS = 8
BLOCK = 256


def draw_doc_lengths(key, part):
    key = jax.random.fold_in(key, 11)
    key_spread, key_short, key_tail, key_pick = jax.random.split(key, 4)
    segment = SEQUENCE_LENGTH // DOCS
    centers = jnp.arange(1, DOCS, dtype=jnp.int32) * segment
    jitter = jax.random.randint(key_spread, (SEQS, DOCS - 1), 1 - segment // 2, segment // 2, dtype=jnp.int32)
    spread_cuts = centers[None, :] + jitter
    small_steps = jax.random.randint(key_short, (SEQS, DOCS - 2), 1, max(BLOCK // DOCS, 2), dtype=jnp.int32)
    head_cuts = jnp.cumsum(small_steps, axis=1).astype(jnp.int32)
    tail_cut = SEQUENCE_LENGTH - jax.random.randint(key_tail, (SEQS, 1), 1, BLOCK, dtype=jnp.int32)
    long_cuts = jnp.concatenate([head_cuts, tail_cut], axis=1)
    picked = jax.random.randint(key_pick, (SEQS // MB,), 0, MB, dtype=jnp.int32)
    rows_all = jnp.arange(SEQS, dtype=jnp.int32)
    is_long = rows_all % MB == jnp.repeat(picked, MB)
    cut_points = jnp.where(is_long[:, None], long_cuts, spread_cuts)
    borders = jnp.concatenate([jnp.zeros((SEQS, 1), jnp.int32), cut_points, jnp.full((SEQS, 1), SEQUENCE_LENGTH, jnp.int32)], axis=1)
    return borders[:, 1:] - borders[:, :-1]


def steps_of(stream_key, extent, shards, low, largest):
    level, own = 1.0, jax.random.fold_in(stream_key, 6)
    for position, parts in shards:
        draws = jnp.exp(jax.random.uniform(jax.random.fold_in(own, position), (parts,), jnp.float32, low / len(shards), largest / len(shards)))
        level = level * jnp.repeat(draws, extent[position] // parts).reshape([-1 if axis == position else 1 for axis in range(len(extent))])
    return level


def normal_values(stream_key, extent, width, bound, pieces=(), kind=jnp.bfloat16):
    drawn = width * jax.random.normal(stream_key, extent, jnp.float32)
    if pieces:
        drawn = drawn * steps_of(stream_key, extent, pieces, -0.22, 0.18)
    return jnp.clip(drawn, -bound, bound).astype(kind)


def setup_inputs(seed: int = 0) -> dict:
    arg_keys = jax.random.split(jax.random.key(seed), 13)
    return {
        "hidden_in": normal_values(arg_keys[0], (SEQS, SEQUENCE_LENGTH, MODEL_WIDTH), 1.0, 6.0, ((0, 4), (1, 8))),
        "doc_lengths": draw_doc_lengths(jax.random.fold_in(arg_keys[12], 71), 0),
        "attn_gain": jnp.clip(0.5 + 1.0 * jax.random.uniform(arg_keys[2], (MODEL_WIDTH,), jnp.float32) ** steps_of(arg_keys[2], (MODEL_WIDTH,), ((0, 4),), -0.2, 0.2), 0.5, 1.5).astype(jnp.bfloat16),
        "query_weight": normal_values(arg_keys[3], (MODEL_WIDTH, QUERY_HEADS * HEAD_SIZE), (MODEL_WIDTH // 2) ** -0.5, 0.15625, ((0, 4),)),
        "key_matrix": normal_values(arg_keys[4], (MODEL_WIDTH, KEY_VALUE_HEADS * HEAD_SIZE), MODEL_WIDTH ** -0.5, 0.125, ((0, 4),)),
        "value_matrix": normal_values(arg_keys[5], (MODEL_WIDTH, KEY_VALUE_HEADS * HEAD_SIZE), MODEL_WIDTH ** -0.5, 0.125, ((0, 4),)),
        "output_weight": normal_values(arg_keys[6], (QUERY_HEADS * HEAD_SIZE, MODEL_WIDTH), (QUERY_HEADS * HEAD_SIZE // 64) ** -0.5, 1.0, ((0, 4),)),
        "mlp_gain": jnp.clip(0.5 + 1.0 * jax.random.uniform(arg_keys[7], (MODEL_WIDTH,), jnp.float32) ** steps_of(arg_keys[7], (MODEL_WIDTH,), ((0, 4),), -0.2, 0.2), 0.5, 1.5).astype(jnp.bfloat16),
        "gate_weight": normal_values(arg_keys[8], (MODEL_WIDTH, FF), MODEL_WIDTH ** -0.5, 0.125, ((0, 4),)),
        "up_weight": normal_values(arg_keys[9], (MODEL_WIDTH, FF), MODEL_WIDTH ** -0.5, 0.125, ((0, 4),)),
        "down_weight": normal_values(arg_keys[10], (FF, MODEL_WIDTH), FF ** -0.5, 0.0625, ((0, 4),)),
        "out_grad": normal_values(arg_keys[11], (SEQS, SEQUENCE_LENGTH, MODEL_WIDTH), 1.0, 6.0, ((0, 4), (1, 8))),
    }


NORM_EPS = 1e-05
ROPE_THETA = 1000000.0
MASK_VALUE_FILL = -1e+30
HIGHEST_PREC = lax.Precision.HIGHEST

@jax.custom_vjp
def low(v):
    return lax.optimization_barrier(v.astype(jnp.bfloat16)).astype(jnp.float32)

@jax.custom_vjp
def low_back(v):
    return v

def low_keep(v):
    return (low(v), None)

def low_pass(kept, grad):
    return (grad,)

def back_keep(v):
    return (v, None)

def back_low(kept, grad):
    return (low(grad),)
low.defvjp(low_keep, low_pass)
low_back.defvjp(back_keep, back_low)

def matmul_high(left, right):
    return jnp.dot(left, right, precision=HIGHEST_PREC, preferred_element_type=jnp.float32)

def boundaries(lengths, positions):
    cut_points = jnp.cumsum(lengths).astype(jnp.int32)[:-1]
    passed = positions[:, None] >= cut_points[None, :]
    documents = lax.optimization_barrier(jnp.sum(passed.astype(jnp.int32), axis=1))
    starts = lax.optimization_barrier(jnp.max(jnp.where(passed, cut_points[None, :], 0), axis=1))
    return (documents, positions - starts)

def rotate(vectors, rope_places, direction):
    halfway = HEAD_SIZE // 2
    frequency = ROPE_THETA ** (-2.0 * jnp.arange(halfway, dtype=jnp.float32) / HEAD_SIZE)
    angles = rope_places.astype(jnp.float32)[:, None] * frequency[None, :]
    cosine = jnp.cos(angles)[:, None, :]
    sine_part = direction * jnp.sin(angles)[:, None, :]
    shaped = vectors.reshape(vectors.shape[0], vectors.shape[1] // HEAD_SIZE, HEAD_SIZE)
    former = shaped[..., :halfway]
    latter = shaped[..., halfway:]
    turned = jnp.concatenate([former * cosine - latter * sine_part, latter * cosine + former * sine_part], axis=-1)
    return turned.reshape(vectors.shape)

def visible(query_places, query_documents, key_places, key_documents):
    same_doc = query_documents[:, None] == key_documents[None, :]
    earlier = key_places[None, :] <= query_places[:, None]
    inside = query_places[:, None] - key_places[None, :] < WINDOW
    return same_doc & earlier & inside

def block_forward(tokens, lengths, gain_one, query_full, key_full, value_full, output_full, gain_two, gate_full, up_full, down_full):
    positions = jnp.arange(SEQUENCE_LENGTH, dtype=jnp.int32)
    documents, rope_places = boundaries(lengths, positions)
    scale_one = lax.rsqrt(lax.optimization_barrier(jnp.mean(tokens * tokens, axis=1, keepdims=True)) + NORM_EPS)
    normed = low(tokens * scale_one * gain_one)
    query_rows = low(rotate(low_back(matmul_high(normed, query_full)), rope_places, 1.0))
    keys_reduced = low(rotate(low_back(matmul_high(normed, key_full)), rope_places, 1.0))
    values_reduced = low(low_back(matmul_high(normed, value_full)))
    query_groups = QUERY_HEADS // KEY_VALUE_HEADS
    head_queries = query_rows.reshape(SEQUENCE_LENGTH, KEY_VALUE_HEADS, query_groups, HEAD_SIZE)
    head_keys = keys_reduced.reshape(SEQUENCE_LENGTH, KEY_VALUE_HEADS, HEAD_SIZE)
    head_values = values_reduced.reshape(SEQUENCE_LENGTH, KEY_VALUE_HEADS, HEAD_SIZE)
    span = min(512, SEQUENCE_LENGTH)
    score_scale = 1.0 / math.sqrt(HEAD_SIZE)

    def attend_block(block_index):
        first_row = block_index * span
        query_part = lax.dynamic_slice_in_dim(head_queries, first_row, span, 0)
        query_places = first_row + jnp.arange(span, dtype=jnp.int32)
        query_documents = lax.dynamic_slice_in_dim(documents, first_row, span, 0)
        scores = low_back(jnp.einsum('qhgd,khd->hgqk', query_part, head_keys, precision=HIGHEST_PREC) * score_scale)
        allowed = visible(query_places, query_documents, positions, documents)
        probabilities = low(jax.nn.softmax(jnp.where(allowed, scores, MASK_VALUE_FILL), axis=-1))
        return jnp.einsum('hgqk,khd->qhgd', probabilities, head_values, precision=HIGHEST_PREC)
    mixed = lax.map(jax.checkpoint(attend_block), jnp.arange(SEQUENCE_LENGTH // span, dtype=jnp.int32))
    attended_rows = low(low_back(mixed.reshape(SEQUENCE_LENGTH, QUERY_HEADS * HEAD_SIZE)))
    residual = tokens + low_back(matmul_high(attended_rows, output_full))
    scale_two = lax.rsqrt(lax.optimization_barrier(jnp.mean(residual * residual, axis=1, keepdims=True)) + NORM_EPS)
    normed_two = low(residual * scale_two * gain_two)
    gate_linear = low_back(matmul_high(normed_two, gate_full))
    up_linear = low_back(matmul_high(normed_two, up_full))
    hidden_mid = low(jax.nn.silu(gate_linear) * up_linear)
    return residual + low_back(matmul_high(hidden_mid, down_full))

def reference(hidden_in, doc_lengths, attn_gain, query_weight, key_matrix, value_matrix, output_weight, mlp_gain, gate_weight, up_weight, down_weight, out_grad):
    params = (attn_gain.astype(jnp.float32), query_weight.astype(jnp.float32), key_matrix.astype(jnp.float32), value_matrix.astype(jnp.float32), output_weight.astype(jnp.float32), mlp_gain.astype(jnp.float32), gate_weight.astype(jnp.float32), up_weight.astype(jnp.float32), down_weight.astype(jnp.float32))

    def per_sequence(totals, sequence_item):
        tokens, lengths, upstream = sequence_item

        def forward_only(tokens_in, *weights_in):
            return block_forward(tokens_in, lengths, *weights_in)
        result, pullback = jax.vjp(forward_only, tokens.astype(jnp.float32), *params)
        gradients = pullback(upstream.astype(jnp.float32))
        totals = tuple((total_now + grad_now for total_now, grad_now in zip(totals, gradients[1:])))
        return (totals, (result, gradients[0]))
    zero_grads = tuple((jnp.zeros_like(weight_now) for weight_now in params))
    totals, (outputs, input_grads) = lax.scan(per_sequence, zero_grads, (hidden_in, doc_lengths, out_grad))
    return (outputs, input_grads, totals[0], totals[1], totals[2], totals[3], totals[4], totals[5], totals[6], totals[7], totals[8])
```

```python
import functools
import math

import jax
import jax.numpy as jnp
from jax import lax
from jax.experimental import pallas as pl
from jax.experimental.pallas import tpu as pltpu
from jax.sharding import PartitionSpec as P

MODEL_WIDTH = 2560
QUERY_HEADS = 32
KEY_VALUE_HEADS = 8
HEAD_SIZE = 80
WINDOW = 1024
GROUPS = QUERY_HEADS // KEY_VALUE_HEADS
HALF = HEAD_SIZE // 2
KV_WIDTH = KEY_VALUE_HEADS * HEAD_SIZE
STRIP = 640
HALF_KV = KV_WIDTH // 2
SCALE = 1.0 / math.sqrt(HEAD_SIZE)

NORM_EPS = 1e-05
ROPE_THETA = 1000000.0
MASK_VALUE_FILL = -1e30
VMEM = 60 * 1024 * 1024

NT = (((1,), (1,)), ((), ()))
TN = (((0,), (0,)), ((), ()))
NN = (((1,), (0,)), ((), ()))


def dot(left, right, dims):
    return lax.dot_general(left, right, dims, preferred_element_type=jnp.float32)


def params(**more):
    return pltpu.CompilerParams(vmem_limit_bytes=VMEM, **more)


def turn(x, cosine, sine):
    width = x.shape[1]
    lane = lax.broadcasted_iota(jnp.int32, x.shape, 1) % HEAD_SIZE
    partner = jnp.where(
        lane < HALF, pltpu.roll(x, width - HALF, 1), pltpu.roll(x, HALF, 1)
    )
    return x * cosine + partner * sine


def qkv_kernel(core_ref, x_ref, mine_ref, other_ref, cos_ref, sin_ref, q_ref, kv_ref):
    half, tile = pl.program_id(0), pl.program_id(1)
    tiles = pl.num_programs(1)

    def go(w_ref):
        acc = dot(x_ref[...], w_ref[...], NN)
        out = turn(acc, cos_ref[0], sin_ref[0]).astype(jnp.bfloat16)

        @pl.when(tile < tiles - 1)
        def _():
            q_ref[...] = out

        @pl.when(tile == tiles - 1)
        def _():
            kv_ref[0] = out

    @pl.when(half == 0)
    def _():
        go(mine_ref)

    @pl.when(half == 1)
    def _():
        go(other_ref)


def qkv_projection(core, x, mine, other, cosine, sine):
    tokens = x.shape[0]
    last = mine.shape[1] // STRIP - 1
    grid_spec = pltpu.PrefetchScalarGridSpec(
        num_scalar_prefetch=1,
        grid=(2, last + 1),
        in_specs=[
            pl.BlockSpec((tokens, MODEL_WIDTH), lambda h, t, c: (0, 0)),
            pl.BlockSpec((MODEL_WIDTH, STRIP), lambda h, t, c: (0, jnp.minimum(t + (last + 1) * h, last))),
            pl.BlockSpec((MODEL_WIDTH, STRIP), lambda h, t, c: (0, t * h)),
            pl.BlockSpec((1, tokens, STRIP), lambda h, t, c: (t // last, 0, 0)),
            pl.BlockSpec((1, tokens, STRIP), lambda h, t, c: (t // last, 0, 0)),
        ],
        out_specs=[
            pl.BlockSpec(
                (tokens, STRIP),
                lambda h, t, c: (0, (c[0] + h - 2 * c[0] * h) * last + jnp.minimum(t, last - 1)),
            ),
            pl.BlockSpec((1, tokens, STRIP), lambda h, t, c: (c[0] + h - 2 * c[0] * h, 0, 0)),
        ],
    )
    return pl.pallas_call(
        qkv_kernel,
        grid_spec=grid_spec,
        out_shape=[
            jax.ShapeDtypeStruct((tokens, QUERY_HEADS * HEAD_SIZE), jnp.bfloat16),
            jax.ShapeDtypeStruct((2, tokens, STRIP), jnp.bfloat16),
        ],
        compiler_params=params(),
    )(core, x, mine, other, cosine, sine)


def unturn_kernel(x_ref, cos_ref, sin_ref, o_ref):
    o_ref[0] = turn(x_ref[0].astype(jnp.float32), cos_ref[0], -sin_ref[0]).astype(jnp.bfloat16)


def unturn(x, cosine, sine):
    tokens = x.shape[1]
    return pl.pallas_call(
        unturn_kernel,
        grid=(2,),
        in_specs=[
            pl.BlockSpec((1, tokens, STRIP), lambda h: (h, 0, 0)),
            pl.BlockSpec((1, tokens, STRIP), lambda h: (1, 0, 0)),
            pl.BlockSpec((1, tokens, STRIP), lambda h: (1, 0, 0)),
        ],
        out_specs=pl.BlockSpec((1, tokens, STRIP), lambda h: (h, 0, 0)),
        out_shape=jax.ShapeDtypeStruct(x.shape, jnp.bfloat16),
        compiler_params=params(),
    )(x, cosine, sine)


def spread_heads(blocks, keys, values, length):
    for step, block in enumerate(blocks):
        rows = pl.ds(step * length, length)
        for head in range(KEY_VALUE_HEADS):
            half, at = head // 4, (head % 4) * HEAD_SIZE
            keys[head, rows, :] = block[0, half, 0, :, at : at + HEAD_SIZE]
            values[head, rows, :] = block[0, half, 0, :, HALF_KV + at : HALF_KV + at + HEAD_SIZE]


def attend_kernel(count, at_ref, q_ref, low_ref, *rest):
    blocks, (o_ref, lse_ref), (keys, values, bias) = (
        rest[:count],
        rest[count : count + 2],
        rest[count + 2 :],
    )
    pair = pl.program_id(1)
    length = q_ref.shape[1]
    window = bias.shape[1]

    @pl.when(pair == 0)
    def _():
        spread_heads(blocks, keys, values, length)
        key_place = at_ref[0] * length + lax.broadcasted_iota(jnp.int32, (length, window), 1)
        place = at_ref[1] * length + lax.broadcasted_iota(jnp.int32, (length, window), 0)
        seen = (key_place >= low_ref[0]) & (key_place <= place)
        bias[...] = jnp.where(seen, 0.0, MASK_VALUE_FILL)

    mixed, sums = [], []
    for side in range(2):
        key, value = keys[2 * pair + side], values[2 * pair + side]
        for group in range(GROUPS):
            at = (side * GROUPS + group) * HEAD_SIZE
            query = q_ref[0, :, at : at + HEAD_SIZE]
            scores = dot(query, key, NT) * SCALE + bias[...]
            peak = jnp.max(scores, axis=1, keepdims=True)
            weights = jnp.exp(scores - peak)
            total = jnp.sum(weights, axis=1, keepdims=True)
            mixed.append(dot(weights.astype(jnp.bfloat16), value, NN) / total)
            sums.append(peak + jnp.log(total))
    o_ref[0] = jnp.concatenate(mixed, axis=1).astype(jnp.bfloat16)
    spare = jnp.zeros((length, 128 - 2 * GROUPS), jnp.float32)
    lse_ref[0, 0] = jnp.transpose(jnp.concatenate(sums + [spare], axis=1))[: 2 * GROUPS]


def kv_specs(count, length):
    return [
        pl.BlockSpec(
            (1, 2, 1, length, STRIP),
            functools.partial(lambda step, b, p, at: (at[0] + step, 0, b, 0, 0), step),
        )
        for step in range(count)
    ]


def attend(at, queries, low, everyones, count):
    batches, length, width = queries.shape
    pairs = KEY_VALUE_HEADS // 2
    window = count * length
    grid_spec = pltpu.PrefetchScalarGridSpec(
        num_scalar_prefetch=1,
        grid=(batches, pairs),
        in_specs=[
            pl.BlockSpec((1, length, STRIP), lambda b, p, at: (b, 0, p)),
            pl.BlockSpec((1, length, 1), lambda b, p, at: (b, 0, 0)),
        ]
        + kv_specs(count, length),
        out_specs=[
            pl.BlockSpec((1, length, STRIP), lambda b, p, at: (b, 0, p)),
            pl.BlockSpec((1, 1, 2 * GROUPS, length), lambda b, p, at: (b, p, 0, 0)),
        ],
        scratch_shapes=[
            pltpu.VMEM((KEY_VALUE_HEADS, window, HEAD_SIZE), jnp.bfloat16),
            pltpu.VMEM((KEY_VALUE_HEADS, window, HEAD_SIZE), jnp.bfloat16),
            pltpu.VMEM((length, window), jnp.float32),
        ],
    )
    return pl.pallas_call(
        functools.partial(attend_kernel, count),
        grid_spec=grid_spec,
        out_shape=[
            jax.ShapeDtypeStruct((batches, length, width), jnp.bfloat16),
            jax.ShapeDtypeStruct((batches, pairs, 2 * GROUPS, length), jnp.float32),
        ],
        compiler_params=params(),
    )(at, queries, low, *([everyones] * count))


def attend_back_kernel(
    count, at_ref, q_ref, g_ref, a_ref, lse_ref, low_ref, cos_ref, sin_ref, *rest
):
    blocks, (dq_ref, dkv_ref), (keys, values, bias, key_sums, value_sums) = (
        rest[:count],
        rest[count : count + 2],
        rest[count + 2 :],
    )
    pair = pl.program_id(1)
    length = q_ref.shape[1]
    window = bias.shape[0]

    @pl.when(pair == 0)
    def _():
        spread_heads(blocks, keys, values, length)
        key_place = at_ref[0] * length + lax.broadcasted_iota(jnp.int32, (window, length), 0)
        place = at_ref[1] * length + lax.broadcasted_iota(jnp.int32, (window, length), 1)
        seen = (key_place >= low_ref[0]) & (key_place <= place)
        bias[...] = jnp.where(seen, 0.0, MASK_VALUE_FILL)

    products = g_ref[0].astype(jnp.float32) * a_ref[0].astype(jnp.float32)
    heads = [
        jnp.sum(products[:, h * HEAD_SIZE : (h + 1) * HEAD_SIZE], axis=1, keepdims=True)
        for h in range(2 * GROUPS)
    ]
    spare = jnp.zeros((length, 128 - 2 * GROUPS), jnp.float32)
    deltas = jnp.transpose(jnp.concatenate(heads + [spare], axis=1))
    turned = []
    for side in range(2):
        key, value = keys[2 * pair + side], values[2 * pair + side]
        key_sum = jnp.zeros((window, HEAD_SIZE), jnp.float32)
        value_sum = jnp.zeros((window, HEAD_SIZE), jnp.float32)
        for group in range(GROUPS):
            row = side * GROUPS + group
            at = row * HEAD_SIZE
            query = q_ref[0, :, at : at + HEAD_SIZE]
            gradient = g_ref[0, :, at : at + HEAD_SIZE]
            chances = jnp.exp(
                dot(key, query, NT) * SCALE + bias[...] - lse_ref[0, 0, row : row + 1, :]
            )
            value_sum = value_sum + dot(chances.astype(jnp.bfloat16), gradient, NN)
            slopes = dot(value, gradient, NT) - deltas[row : row + 1, :]
            slopes = (chances * slopes).astype(jnp.bfloat16)
            key_sum = key_sum + dot(slopes, query, NN)
            turned.append(dot(slopes, key, TN) * SCALE)
        key_sums[2 * pair + side] = (key_sum * SCALE).astype(jnp.bfloat16)
        value_sums[2 * pair + side] = value_sum.astype(jnp.bfloat16)
    dq_ref[0] = turn(jnp.concatenate(turned, axis=1), cos_ref[0], -sin_ref[0]).astype(jnp.bfloat16)

    @pl.when(pair == pl.num_programs(1) - 1)
    def _():
        for step in range(count):
            rows = pl.ds(step * length, length)
            for half in range(2):
                here = range(half * 4, half * 4 + 4)
                dkv_ref[step, half, 0] = jnp.concatenate(
                    [key_sums[h, rows, :] for h in here] + [value_sums[h, rows, :] for h in here],
                    axis=1,
                )


def attend_back(at, queries, gradient, attended, lse, low, cosine, sine, everyones, count):
    batches, length, width = queries.shape
    pairs = KEY_VALUE_HEADS // 2
    window = count * length
    strip = pl.BlockSpec((1, length, STRIP), lambda b, p, at: (b, 0, p))
    table = pl.BlockSpec((1, length, STRIP), lambda b, p, at: (0, b, 0))
    grid_spec = pltpu.PrefetchScalarGridSpec(
        num_scalar_prefetch=1,
        grid=(batches, pairs),
        in_specs=[
            strip,
            strip,
            strip,
            pl.BlockSpec((1, 1, 2 * GROUPS, length), lambda b, p, at: (b, p, 0, 0)),
            pl.BlockSpec((1, 1, length), lambda b, p, at: (b, 0, 0)),
            table,
            table,
        ]
        + kv_specs(count, length),
        out_specs=[
            strip,
            pl.BlockSpec((count, 2, 1, length, STRIP), lambda b, p, at: (0, 0, b, 0, 0)),
        ],
        scratch_shapes=[
            pltpu.VMEM((KEY_VALUE_HEADS, window, HEAD_SIZE), jnp.bfloat16),
            pltpu.VMEM((KEY_VALUE_HEADS, window, HEAD_SIZE), jnp.bfloat16),
            pltpu.VMEM((window, length), jnp.float32),
            pltpu.VMEM((KEY_VALUE_HEADS, window, HEAD_SIZE), jnp.bfloat16),
            pltpu.VMEM((KEY_VALUE_HEADS, window, HEAD_SIZE), jnp.bfloat16),
        ],
    )
    return pl.pallas_call(
        functools.partial(attend_back_kernel, count),
        grid_spec=grid_spec,
        out_shape=[
            jax.ShapeDtypeStruct((batches, length, width), jnp.bfloat16),
            jax.ShapeDtypeStruct((count, 2, batches, length, STRIP), jnp.bfloat16),
        ],
        compiler_params=params(),
    )(at, queries, gradient, attended, lse, low, cosine, sine, *([everyones] * count))


def boundaries(lengths, positions):
    cut_points = jnp.cumsum(lengths)[:-1]
    passed = positions[:, None] >= cut_points[None, :]
    return jnp.max(jnp.where(passed, cut_points[None, :], 0), axis=1)


def matmul(left, right):
    return dot(left, right, NN)


def matmul_back(gradient, weight):
    return dot(gradient, weight, NT)


def on_device(
    hidden_in,
    doc_lengths,
    attn_gain,
    query_weight,
    key_matrix,
    value_matrix,
    output_weight,
    mlp_gain,
    gate_weight,
    up_weight,
    down_weight,
    out_grad,
):
    owners, chain = lax.axis_size("fs"), lax.axis_size("ctx")
    owner, place = lax.axis_index("fs"), lax.axis_index("ctx")
    core = place % 2
    planes = chain // 2
    batches, length, width = hidden_in.shape
    tokens = batches * length
    rows = query_weight.shape[0]
    inner = down_weight.shape[0]
    count = min(WINDOW // length + 1, chain)
    first = jnp.maximum(place - (count - 1), 0)
    at = jnp.stack([first, place]).astype(jnp.int32)
    siblings = [(i, i ^ 1) for i in range(chain)]
    couples = [[2 * i, 2 * i + 1] for i in range(planes)]
    lines = [[2 * i + j for i in range(planes)] for j in range(2)]

    def fetch(shard):
        part = shard.shape[1] // 2
        mine = lax.dynamic_slice_in_dim(shard, core * part, part, 1)
        mine = lax.all_gather(mine, "fs", axis=0, tiled=True)
        return mine, lax.ppermute(mine, "ctx", siblings)

    def halves(shard):
        return shard.reshape(rows, 2, -1)

    joined = jnp.concatenate(
        [halves(query_weight), halves(key_matrix), halves(value_matrix)], axis=2
    ).reshape(rows, -1)
    in_mine, in_other = fetch(joined)
    out_mine, out_other = fetch(output_weight)
    gain_one = lax.all_gather(attn_gain, "fs", axis=0, tiled=True).astype(jnp.float32)
    gain_two = lax.all_gather(mlp_gain, "fs", axis=0, tiled=True).astype(jnp.float32)

    def columns(shard):
        part = inner // 2
        mine = shard.reshape(rows, owners, 2, part)
        mine = lax.dynamic_index_in_dim(mine, core, 2, keepdims=False)
        mine = lax.all_to_all(mine, "fs", split_axis=1, concat_axis=0, tiled=True)
        mine = mine.reshape(rows * owners, part)
        other = lax.ppermute(mine, "ctx", siblings)
        whole = jnp.zeros((rows * owners, inner), shard.dtype)
        whole = lax.dynamic_update_slice_in_dim(whole, mine, core * part, 1)
        return lax.dynamic_update_slice_in_dim(whole, other, (1 - core) * part, 1)

    gate_part, up_part = columns(gate_weight), columns(up_weight)
    grads_in = out_grad.reshape(tokens, width)
    grads_all = lax.all_gather(grads_in, "fs", axis=0, tiled=True)

    positions = place * length + jnp.arange(length, dtype=jnp.int32)
    starts = jax.vmap(lambda lengths: boundaries(lengths, positions))(doc_lengths)
    low = jnp.maximum(starts, positions[None, :] - (WINDOW - 1))
    frequency = ROPE_THETA ** (-2.0 * jnp.arange(HALF, dtype=jnp.float32) / HEAD_SIZE)
    turns = (positions[None, :] - starts).reshape(tokens).astype(jnp.float32)
    angles = turns[:, None] * frequency[None, :]
    cosine, sine = jnp.cos(angles), jnp.sin(angles)
    cosine = jnp.tile(jnp.concatenate([cosine, cosine], axis=1), (1, STRIP // HEAD_SIZE))
    sine = jnp.tile(jnp.concatenate([-sine, sine], axis=1), (1, STRIP // HEAD_SIZE))
    is_key = (jnp.arange(STRIP) < HALF_KV)[None, :]
    cosine = jnp.stack([cosine, jnp.where(is_key, cosine, 1.0)])
    sine = jnp.stack([sine, jnp.where(is_key, sine, 0.0)])

    x = hidden_in.reshape(tokens, width).astype(jnp.float32)
    scale_one = lax.rsqrt(jnp.mean(x * x, axis=1, keepdims=True) + NORM_EPS)
    normed = (x * scale_one * gain_one).astype(jnp.bfloat16)
    core_ref = core.reshape(1).astype(jnp.int32)
    queries, kv = qkv_projection(core_ref, normed, in_mine, in_other, cosine, sine)
    kv = kv.reshape(2, batches, length, STRIP)
    everyones = lax.all_gather(kv, "ctx", axis=0, tiled=False)
    queries = queries.reshape(batches, length, width)
    attended, lse = attend(at, queries, low[:, :, None], everyones, count)
    attended_rows = attended.reshape(tokens, width)

    def in_order(mine, other):
        return jnp.where(
            core == 0,
            jnp.concatenate([mine, other], axis=1),
            jnp.concatenate([other, mine], axis=1),
        )

    projected = in_order(matmul(attended_rows, out_mine), matmul(attended_rows, out_other))
    residual = x + projected
    scale_two = lax.rsqrt(jnp.mean(residual * residual, axis=1, keepdims=True) + NORM_EPS)
    normed_two = (residual * scale_two * gain_two).astype(jnp.bfloat16)

    normed_all = lax.all_gather(normed_two, "fs", axis=0, tiled=True)
    gate = matmul(normed_all, gate_part)
    up = matmul(normed_all, up_part)
    mid_grad = matmul_back(grads_all, down_weight)
    sigmoid = jax.nn.sigmoid(gate)
    silu = gate * sigmoid
    mid = (silu * up).astype(jnp.bfloat16)
    gate_slope = (mid_grad * up * sigmoid * (1.0 + gate * (1.0 - sigmoid))).astype(jnp.bfloat16)
    up_slope = (mid_grad * silu).astype(jnp.bfloat16)

    partial = matmul_back(gate_slope, gate_part) + matmul_back(up_slope, up_part)
    normed_two_grad = lax.psum_scatter(
        partial.astype(jnp.bfloat16), "fs", scatter_dimension=0, tiled=True
    ).astype(jnp.float32)
    lowered = lax.psum_scatter(
        matmul(mid, down_weight).astype(jnp.bfloat16), "fs", scatter_dimension=0, tiled=True
    )
    hidden_out = residual + lowered.astype(jnp.float32)

    spans = chain // owners

    def fold_columns(slopes):
        grads = lax.dot_general(
            normed_all.reshape(-1, owners, rows),
            slopes.reshape(-1, spans, inner // spans),
            TN,
            preferred_element_type=jnp.float32,
        ).astype(jnp.bfloat16)
        grads = jnp.transpose(grads, (0, 2, 1, 3))
        grads = grads.reshape(chain, rows, inner // spans)
        mine = lax.psum_scatter(grads, "ctx", scatter_dimension=0, tiled=True)[0]
        moves = [
            (f * chain + c, (c // spans) * chain + f * spans + c % spans)
            for f in range(owners)
            for c in range(chain)
        ]
        return lax.ppermute(mine, ("fs", "ctx"), moves).astype(jnp.float32)

    down_grad = lax.psum_scatter(
        dot(mid, grads_all, TN).astype(jnp.bfloat16), "ctx", scatter_dimension=1, tiled=True
    ).astype(jnp.float32)
    gate_grad = fold_columns(gate_slope)
    up_grad = fold_columns(up_slope)

    scaled_two = normed_two_grad * gain_two
    residual_grad = grads_in.astype(jnp.float32) + scale_two * (
        scaled_two
        - residual * scale_two * scale_two * jnp.mean(scaled_two * residual, axis=1, keepdims=True)
    )
    gain_two_part = jnp.sum(normed_two_grad * residual * scale_two, axis=0)
    attn_grad = residual_grad.astype(jnp.bfloat16)
    part = width // 2
    grad_mine = lax.dynamic_slice_in_dim(attn_grad, core * part, part, 1)
    grad_other = lax.dynamic_slice_in_dim(attn_grad, (1 - core) * part, part, 1)
    attended_grad = (matmul_back(grad_mine, out_mine) + matmul_back(grad_other, out_other)).astype(
        jnp.bfloat16
    )
    query_slopes, kv_parts = attend_back(
        at,
        queries,
        attended_grad.reshape(batches, length, width),
        attended,
        lse,
        low[:, None, :],
        cosine,
        sine,
        everyones,
        count,
    )
    kv_spread = lax.dynamic_update_slice_in_dim(
        jnp.zeros((chain,) + kv_parts.shape[1:], jnp.bfloat16), kv_parts, first, 0
    )
    kv_home = lax.psum_scatter(kv_spread, "ctx", scatter_dimension=0, tiled=True)[0]
    kv_slopes = unturn(kv_home.reshape(2, tokens, STRIP), cosine, sine)
    query_slopes = query_slopes.reshape(tokens, width)

    def by_owner(slopes):
        return slopes.reshape(tokens, planes, 2, -1)

    key_slopes = jnp.concatenate([kv_slopes[0, :, :HALF_KV], kv_slopes[1, :, :HALF_KV]], axis=1)
    value_slopes = jnp.concatenate([kv_slopes[0, :, HALF_KV:], kv_slopes[1, :, HALF_KV:]], axis=1)

    def fold_rows(left, slopes):
        own = slopes.shape[3]
        slopes = jnp.transpose(slopes, (2, 0, 1, 3)).reshape(2, tokens, planes * own)
        grads = jnp.stack([dot(left, slopes[j], TN).astype(jnp.bfloat16) for j in range(2)])
        grads = lax.psum_scatter(
            grads, "ctx", scatter_dimension=0, tiled=True, axis_index_groups=couples
        )[0]
        grads = lax.psum_scatter(grads, "fs", scatter_dimension=0, tiled=True)
        return lax.psum_scatter(
            grads, "ctx", scatter_dimension=1, tiled=True, axis_index_groups=lines
        ).astype(jnp.float32)

    output_grad = fold_rows(attended_rows, by_owner(attn_grad))
    in_slopes = jnp.concatenate(
        [by_owner(query_slopes), by_owner(key_slopes), by_owner(value_slopes)], axis=3
    )
    in_grad = fold_rows(normed, in_slopes)
    q_own, kv_own = width // chain, KV_WIDTH // chain
    query_grad = in_grad[:, :q_own]
    key_grad = in_grad[:, q_own : q_own + kv_own]
    value_grad = in_grad[:, q_own + kv_own :]

    def half_slopes(half):
        return jnp.concatenate(
            [
                lax.dynamic_slice_in_dim(query_slopes, half * (width // 2), width // 2, 1),
                lax.dynamic_index_in_dim(kv_slopes, half, 0, keepdims=False),
            ],
            axis=1,
        )

    normed_grad = matmul_back(half_slopes(core), in_mine) + matmul_back(
        half_slopes(1 - core), in_other
    )
    scaled_one = normed_grad * gain_one
    hidden_grad = residual_grad + scale_one * (
        scaled_one - x * scale_one * scale_one * jnp.mean(scaled_one * x, axis=1, keepdims=True)
    )
    gain_one_part = jnp.sum(normed_grad * x * scale_one, axis=0)
    gains = jnp.stack([gain_one_part, gain_two_part], axis=1)
    gains = lax.psum_scatter(gains, "fs", scatter_dimension=0, tiled=True)
    gains = lax.psum(gains, "ctx")
    return (
        hidden_out.reshape(batches, length, width),
        hidden_grad.reshape(batches, length, width),
        gains[:, 0],
        query_grad,
        key_grad,
        value_grad,
        output_grad,
        gains[:, 1],
        gate_grad,
        up_grad,
        down_grad,
    )


def solution(mesh):
    tokens_spec = P("fs", "ctx", None)
    rows_spec = P("fs", None)
    block_spec = P("fs", "ctx")
    return jax.shard_map(
        on_device,
        mesh=mesh,
        in_specs=(
            tokens_spec,
            rows_spec,
            P("fs"),
            rows_spec,
            rows_spec,
            rows_spec,
            rows_spec,
            P("fs"),
            rows_spec,
            rows_spec,
            rows_spec,
            tokens_spec,
        ),
        out_specs=(
            tokens_spec,
            tokens_spec,
            P("fs"),
            block_spec,
            block_spec,
            block_spec,
            block_spec,
            P("fs"),
            block_spec,
            block_spec,
            block_spec,
        ),
        check_vma=False,
    )
```

```python
import functools
import math

import jax
import jax.numpy as jnp
from jax import lax
from jax.experimental import pallas as pl
from jax.experimental.pallas import tpu as pltpu
from jax.sharding import PartitionSpec as P

MODEL_WIDTH = 2560
QUERY_HEADS = 32
KEY_VALUE_HEADS = 8
HEAD_SIZE = 80
WINDOW = 1024
GROUPS = QUERY_HEADS // KEY_VALUE_HEADS
HALF = HEAD_SIZE // 2
KV_WIDTH = KEY_VALUE_HEADS * HEAD_SIZE
STRIP = 640
HALF_KV = KV_WIDTH // 2
SCALE = 1.0 / math.sqrt(HEAD_SIZE)

NORM_EPS = 1e-05
ROPE_THETA = 1000000.0
MASK_VALUE_FILL = -1e30
VMEM = 60 * 1024 * 1024
FEED_VMEM = 62 * 1024 * 1024
MESH = pl.DeviceIdType.MESH

NT = (((1,), (1,)), ((), ()))
TN = (((0,), (0,)), ((), ()))
NN = (((1,), (0,)), ((), ()))


def dot(left, right, dims):
    return lax.dot_general(left, right, dims, preferred_element_type=jnp.float32)


def params(**more):
    return pltpu.CompilerParams(vmem_limit_bytes=VMEM, **more)


def turn(x, cosine, sine):
    width = x.shape[1]
    lane = lax.broadcasted_iota(jnp.int32, x.shape, 1) % HEAD_SIZE
    partner = jnp.where(
        lane < HALF, pltpu.roll(x, width - HALF, 1), pltpu.roll(x, HALF, 1)
    )
    return x * cosine + partner * sine


def qkv_kernel(core_ref, x_ref, mine_ref, other_ref, cos_ref, sin_ref, q_ref, kv_ref):
    half, tile = pl.program_id(0), pl.program_id(1)
    tiles = pl.num_programs(1)

    def go(w_ref):
        acc = dot(x_ref[...], w_ref[...], NN)
        out = turn(acc, cos_ref[0], sin_ref[0]).astype(jnp.bfloat16)

        @pl.when(tile < tiles - 1)
        def _():
            q_ref[...] = out

        @pl.when(tile == tiles - 1)
        def _():
            kv_ref[0] = out

    @pl.when(half == 0)
    def _():
        go(mine_ref)

    @pl.when(half == 1)
    def _():
        go(other_ref)


def qkv_projection(core, x, mine, other, cosine, sine):
    tokens = x.shape[0]
    last = mine.shape[1] // STRIP - 1
    grid_spec = pltpu.PrefetchScalarGridSpec(
        num_scalar_prefetch=1,
        grid=(2, last + 1),
        in_specs=[
            pl.BlockSpec((tokens, MODEL_WIDTH), lambda h, t, c: (0, 0)),
            pl.BlockSpec((MODEL_WIDTH, STRIP), lambda h, t, c: (0, jnp.minimum(t + (last + 1) * h, last))),
            pl.BlockSpec((MODEL_WIDTH, STRIP), lambda h, t, c: (0, t * h)),
            pl.BlockSpec((1, tokens, STRIP), lambda h, t, c: (t // last, 0, 0)),
            pl.BlockSpec((1, tokens, STRIP), lambda h, t, c: (t // last, 0, 0)),
        ],
        out_specs=[
            pl.BlockSpec(
                (tokens, STRIP),
                lambda h, t, c: (0, (c[0] + h - 2 * c[0] * h) * last + jnp.minimum(t, last - 1)),
            ),
            pl.BlockSpec((1, tokens, STRIP), lambda h, t, c: (c[0] + h - 2 * c[0] * h, 0, 0)),
        ],
    )
    return pl.pallas_call(
        qkv_kernel,
        grid_spec=grid_spec,
        out_shape=[
            jax.ShapeDtypeStruct((tokens, QUERY_HEADS * HEAD_SIZE), jnp.bfloat16),
            jax.ShapeDtypeStruct((2, tokens, STRIP), jnp.bfloat16),
        ],
        compiler_params=params(),
    )(core, x, mine, other, cosine, sine)


def unturn_kernel(x_ref, cos_ref, sin_ref, o_ref):
    o_ref[0] = turn(x_ref[0].astype(jnp.float32), cos_ref[0], -sin_ref[0]).astype(jnp.bfloat16)


def unturn(x, cosine, sine):
    tokens = x.shape[1]
    return pl.pallas_call(
        unturn_kernel,
        grid=(2,),
        in_specs=[
            pl.BlockSpec((1, tokens, STRIP), lambda h: (h, 0, 0)),
            pl.BlockSpec((1, tokens, STRIP), lambda h: (1, 0, 0)),
            pl.BlockSpec((1, tokens, STRIP), lambda h: (1, 0, 0)),
        ],
        out_specs=pl.BlockSpec((1, tokens, STRIP), lambda h: (h, 0, 0)),
        out_shape=jax.ShapeDtypeStruct(x.shape, jnp.bfloat16),
        compiler_params=params(),
    )(x, cosine, sine)


def spread_heads(blocks, keys, values, length):
    last = len(blocks) - 1
    for back, block in enumerate(blocks):
        rows = pl.ds((last - back) * length, length)
        for head in range(KEY_VALUE_HEADS):
            half, at = head // 4, (head % 4) * HEAD_SIZE
            keys[head, rows, :] = block[0, half, 0, :, at : at + HEAD_SIZE]
            values[head, rows, :] = block[0, half, 0, :, HALF_KV + at : HALF_KV + at + HEAD_SIZE]


def attend_kernel(count, at_ref, q_ref, low_ref, *rest):
    blocks, (o_ref, lse_ref), (keys, values, bias) = (
        rest[:count],
        rest[count : count + 2],
        rest[count + 2 :],
    )
    pair = pl.program_id(1)
    length = q_ref.shape[1]
    window = bias.shape[1]

    @pl.when(pair == 0)
    def _():
        spread_heads(blocks, keys, values, length)
        key_place = (at_ref[1] - count + 1) * length + lax.broadcasted_iota(jnp.int32, (length, window), 1)
        place = at_ref[1] * length + lax.broadcasted_iota(jnp.int32, (length, window), 0)
        seen = (key_place >= low_ref[0]) & (key_place <= place)
        bias[...] = jnp.where(seen, 0.0, MASK_VALUE_FILL)

    mixed, sums = [], []
    for side in range(2):
        key, value = keys[2 * pair + side], values[2 * pair + side]
        for group in range(GROUPS):
            at = (side * GROUPS + group) * HEAD_SIZE
            query = q_ref[0, :, at : at + HEAD_SIZE]
            scores = dot(query, key, NT) * SCALE + bias[...]
            peak = jnp.max(scores, axis=1, keepdims=True)
            weights = jnp.exp(scores - peak)
            total = jnp.sum(weights, axis=1, keepdims=True)
            mixed.append(dot(weights.astype(jnp.bfloat16), value, NN) / total)
            sums.append(peak + jnp.log(total))
    o_ref[0] = jnp.concatenate(mixed, axis=1).astype(jnp.bfloat16)
    spare = jnp.zeros((length, 128 - 2 * GROUPS), jnp.float32)
    lse_ref[0, 0] = jnp.transpose(jnp.concatenate(sums + [spare], axis=1))[: 2 * GROUPS]


def kv_specs(count, length):
    def index(back, b, p, at):
        if back % 2 == 0:
            return (back // 2, 0, b, 0, 0)
        return ((back + 1) // 2 - at[0], 0, b, 0, 0)

    return [
        pl.BlockSpec((1, 2, 1, length, STRIP), functools.partial(index, back))
        for back in range(count)
    ]


def kv_operands(lines, count):
    return [lines[back % 2] for back in range(count)]


def attend(at, queries, low, lines, count):
    batches, length, width = queries.shape
    pairs = KEY_VALUE_HEADS // 2
    window = count * length
    grid_spec = pltpu.PrefetchScalarGridSpec(
        num_scalar_prefetch=1,
        grid=(batches, pairs),
        in_specs=[
            pl.BlockSpec((1, length, STRIP), lambda b, p, at: (b, 0, p)),
            pl.BlockSpec((1, length, 1), lambda b, p, at: (b, 0, 0)),
        ]
        + kv_specs(count, length),
        out_specs=[
            pl.BlockSpec((1, length, STRIP), lambda b, p, at: (b, 0, p)),
            pl.BlockSpec((1, 1, 2 * GROUPS, length), lambda b, p, at: (b, p, 0, 0)),
        ],
        scratch_shapes=[
            pltpu.VMEM((KEY_VALUE_HEADS, window, HEAD_SIZE), jnp.bfloat16),
            pltpu.VMEM((KEY_VALUE_HEADS, window, HEAD_SIZE), jnp.bfloat16),
            pltpu.VMEM((length, window), jnp.float32),
        ],
    )
    return pl.pallas_call(
        functools.partial(attend_kernel, count),
        grid_spec=grid_spec,
        out_shape=[
            jax.ShapeDtypeStruct((batches, length, width), jnp.bfloat16),
            jax.ShapeDtypeStruct((batches, pairs, 2 * GROUPS, length), jnp.float32),
        ],
        compiler_params=params(),
    )(at, queries, low, *kv_operands(lines, count))


def attend_back_kernel(
    count, at_ref, q_ref, g_ref, a_ref, lse_ref, low_ref, cos_ref, sin_ref, *rest
):
    blocks, (dq_ref, dkv_ref), (keys, values, bias, key_sums, value_sums) = (
        rest[:count],
        rest[count : count + 2],
        rest[count + 2 :],
    )
    pair = pl.program_id(1)
    length = q_ref.shape[1]
    window = bias.shape[0]

    @pl.when(pair == 0)
    def _():
        spread_heads(blocks, keys, values, length)
        key_place = (at_ref[1] - count + 1) * length + lax.broadcasted_iota(jnp.int32, (window, length), 0)
        place = at_ref[1] * length + lax.broadcasted_iota(jnp.int32, (window, length), 1)
        seen = (key_place >= low_ref[0]) & (key_place <= place)
        bias[...] = jnp.where(seen, 0.0, MASK_VALUE_FILL)

    products = g_ref[0].astype(jnp.float32) * a_ref[0].astype(jnp.float32)
    heads = [
        jnp.sum(products[:, h * HEAD_SIZE : (h + 1) * HEAD_SIZE], axis=1, keepdims=True)
        for h in range(2 * GROUPS)
    ]
    spare = jnp.zeros((length, 128 - 2 * GROUPS), jnp.float32)
    deltas = jnp.transpose(jnp.concatenate(heads + [spare], axis=1))
    turned = []
    for side in range(2):
        key, value = keys[2 * pair + side], values[2 * pair + side]
        key_sum = jnp.zeros((window, HEAD_SIZE), jnp.float32)
        value_sum = jnp.zeros((window, HEAD_SIZE), jnp.float32)
        for group in range(GROUPS):
            row = side * GROUPS + group
            at = row * HEAD_SIZE
            query = q_ref[0, :, at : at + HEAD_SIZE]
            gradient = g_ref[0, :, at : at + HEAD_SIZE]
            chances = jnp.exp(
                dot(key, query, NT) * SCALE + bias[...] - lse_ref[0, 0, row : row + 1, :]
            )
            value_sum = value_sum + dot(chances.astype(jnp.bfloat16), gradient, NN)
            slopes = dot(value, gradient, NT) - deltas[row : row + 1, :]
            slopes = (chances * slopes).astype(jnp.bfloat16)
            key_sum = key_sum + dot(slopes, query, NN)
            turned.append(dot(slopes, key, TN) * SCALE)
        key_sums[2 * pair + side] = (key_sum * SCALE).astype(jnp.bfloat16)
        value_sums[2 * pair + side] = value_sum.astype(jnp.bfloat16)
    dq_ref[0] = turn(jnp.concatenate(turned, axis=1), cos_ref[0], -sin_ref[0]).astype(jnp.bfloat16)

    @pl.when(pair == pl.num_programs(1) - 1)
    def _():
        for step in range(count):
            rows = pl.ds(step * length, length)
            for half in range(2):
                here = range(half * 4, half * 4 + 4)
                dkv_ref[step, half, 0] = jnp.concatenate(
                    [key_sums[h, rows, :] for h in here] + [value_sums[h, rows, :] for h in here],
                    axis=1,
                )


def attend_back(at, queries, gradient, attended, lse, low, cosine, sine, lines, count):
    batches, length, width = queries.shape
    pairs = KEY_VALUE_HEADS // 2
    window = count * length
    strip = pl.BlockSpec((1, length, STRIP), lambda b, p, at: (b, 0, p))
    table = pl.BlockSpec((1, length, STRIP), lambda b, p, at: (0, b, 0))
    grid_spec = pltpu.PrefetchScalarGridSpec(
        num_scalar_prefetch=1,
        grid=(batches, pairs),
        in_specs=[
            strip,
            strip,
            strip,
            pl.BlockSpec((1, 1, 2 * GROUPS, length), lambda b, p, at: (b, p, 0, 0)),
            pl.BlockSpec((1, 1, length), lambda b, p, at: (b, 0, 0)),
            table,
            table,
        ]
        + kv_specs(count, length),
        out_specs=[
            strip,
            pl.BlockSpec((count, 2, 1, length, STRIP), lambda b, p, at: (0, 0, b, 0, 0)),
        ],
        scratch_shapes=[
            pltpu.VMEM((KEY_VALUE_HEADS, window, HEAD_SIZE), jnp.bfloat16),
            pltpu.VMEM((KEY_VALUE_HEADS, window, HEAD_SIZE), jnp.bfloat16),
            pltpu.VMEM((window, length), jnp.float32),
            pltpu.VMEM((KEY_VALUE_HEADS, window, HEAD_SIZE), jnp.bfloat16),
            pltpu.VMEM((KEY_VALUE_HEADS, window, HEAD_SIZE), jnp.bfloat16),
        ],
    )
    return pl.pallas_call(
        functools.partial(attend_back_kernel, count),
        grid_spec=grid_spec,
        out_shape=[
            jax.ShapeDtypeStruct((batches, length, width), jnp.bfloat16),
            jax.ShapeDtypeStruct((count, 2, batches, length, STRIP), jnp.bfloat16),
        ],
        compiler_params=params(),
    )(at, queries, gradient, attended, lse, low, cosine, sine, *kv_operands(lines, count))


def toggled(me, k, count):
    found, bit = me, 1
    while bit < count:
        found = found + ((k // bit) % 2) * bit * (1 - 2 * ((me // bit) % 2))
        bit *= 2
    return found


def feed_kernel(
    peers, chain, nt_ref, og_all, down_ref, *rest
):
    pieces, rest = rest[: 2 * peers], rest[2 * peers :]
    (gs_all, us_all, mid_all, dn_own, dn_in, out_part, gate_grad, up_grad, down_grad,
    nt_v, gs_v, us_v, mid_v, io, relay, out_v,
    load_sem, weight_sem, tile_sem, out_sem, own_sem, nt_send, nt_recv, dn_send, dn_recv) = rest
    tokens, width = nt_ref.shape
    inner = down_ref.shape[0]
    middle = tokens // 2
    square = peers == 4
    me = lax.axis_index("fs")
    core = lax.axis_index("ctx") % 2
    bf16 = jnp.bfloat16

    def remote(src, dst, send, recv, at, k):
        return pltpu.make_async_remote_copy(
            src_ref=src, dst_ref=dst, send_sem=send.at[at], recv_sem=recv.at[at],
            device_id={"fs": toggled(me, k, peers)}, device_id_type=MESH,
        )

    barrier = pltpu.get_barrier_semaphore()
    for k in range(1, peers):
        pl.semaphore_signal(barrier, inc=1, device_id={"fs": toggled(me, k, peers)}, device_id_type=MESH)
    pl.semaphore_wait(barrier, peers - 1)

    top, bottom = pl.ds(0, middle), pl.ds(middle, middle)
    reached = [1, 2] if square else list(range(1, peers))
    spread = {k: remote(nt_ref, nt_v.at[k], nt_send, nt_recv, k, k) for k in reached}
    for k in reached:
        spread[k].start()
    if square:
        spread[3] = remote(nt_v.at[1, top], nt_v.at[3, top], nt_send, nt_recv, 3, 2)
        spread[0] = remote(nt_v.at[2, bottom], nt_v.at[3, bottom], nt_send, nt_recv, 0, 1)
    own = pltpu.make_async_copy(nt_ref, nt_v.at[0], own_sem.at[0])
    own.start()

    def returns(k):
        if square and k == 3:
            return (
                remote(io.at[3, top], relay.at[0], dn_send, dn_recv, 3, 1),
                remote(io.at[3, bottom], relay.at[1], dn_send, dn_recv, 0, 2),
            )
        return (remote(io.at[k], dn_in.at[k - 1], dn_send, dn_recv, k, k),)

    tile = 256 if inner % 256 == 0 else 128
    tiles = inner // tile
    wide = 256
    strips = width // wide

    def both_passes(gate_v, up_v, down_v):
        weights = [pltpu.make_async_copy(down_ref, down_v, weight_sem.at[0])]
        share = pieces[0].shape[1]
        for i, piece in enumerate(pieces):
            k, side = i // 2, i % 2
            half = core + side - 2 * core * side
            at = pl.ds(toggled(me, k, peers) * 2 * share + half * share, share)
            weights.append(pltpu.make_async_copy(piece.at[0], gate_v.at[at], weight_sem.at[1 + 2 * i]))
            weights.append(pltpu.make_async_copy(piece.at[1], up_v.at[at], weight_sem.at[2 + 2 * i]))
        for copy in weights:
            copy.start()

        def grads_of(k):
            return pltpu.make_async_copy(
                og_all.at[toggled(me, k, peers)], io.at[k % 2], load_sem.at[k % 2]
            )

        grads_of(0).start()
        own.wait()
        for copy in weights:
            copy.wait()

        def stores(k, at):
            return [
                pltpu.make_async_copy(src.at[:, at], dst.at[:, at], tile_sem.at[i, at.start // tile])
                for i, (src, dst) in enumerate(
                    (
                        (gs_v, gs_all.at[k]),
                        (us_v, us_all.at[k]),
                        (mid_v, mid_all.at[toggled(me, k, peers)]),
                    )
                )
            ]

        for k in range(peers):
            if square and k == 1:
                spread[1].wait_recv()
                spread[3].start()
                spread[2].wait_recv()
                spread[0].start()
            elif square and k == 3:
                spread[3].wait_recv()
                spread[0].wait_recv()
            elif not square and k > 0:
                spread[k].wait_recv()
            grads_of(k).wait()
            if k + 1 < peers:
                grads_of(k + 1).start()

            def some(j, carry, k=k):
                at = pl.ds(pl.multiple_of(j * tile, tile), tile)
                gate = dot(nt_v[k], gate_v[:, at], NN)
                up = dot(nt_v[k], up_v[:, at], NN)
                grad = dot(io[k % 2], down_v[at, :], NT)
                sig = 1.0 / (1.0 + jnp.exp(-gate))
                silu = gate * sig
                if k > 0:
                    for copy in stores(k - 1, at):
                        copy.wait()
                mid_v[:, at] = (silu * up).astype(bf16)
                gs_v[:, at] = (grad * up * sig * (1.0 + gate * (1.0 - sig))).astype(bf16)
                us_v[:, at] = (grad * silu).astype(bf16)
                for copy in stores(k, at):
                    copy.start()
                return carry

            lax.fori_loop(0, tiles, some, 0)

        def settle(j, carry):
            at = pl.ds(pl.multiple_of(j * tile, tile), tile)
            for copy in stores(peers - 1, at):
                copy.wait()
            return carry

        lax.fori_loop(0, tiles, settle, 0)

        order = [peers - 1, 0] + list(range(peers - 2, 0, -1))
        for turn, k in enumerate(order):
            slab = toggled(me, k, peers)
            if turn > 0:
                loads = [
                    pltpu.make_async_copy(src, dst, tile_sem.at[i, 0])
                    for i, (src, dst) in enumerate(
                        ((gs_all.at[k], gs_v), (us_all.at[k], us_v), (mid_all.at[slab], mid_v))
                    )
                ]
                for copy in loads:
                    copy.start()
                for copy in loads:
                    copy.wait()
            if square and k == 2:
                returns(3)[0].wait_recv()
            if square and k == 1:
                returns(3)[1].wait_recv()

            def out_copy(j, k=k, slab=slab):
                at = pl.ds(pl.multiple_of(j * wide, wide), wide)
                return pltpu.make_async_copy(out_v.at[j % 2], out_part.at[slab, :, at], out_sem.at[j % 2])

            def more(j, carry, k=k, turn=turn, out_copy=out_copy):
                at = pl.ds(pl.multiple_of(j * wide, wide), wide)
                part = dot(gs_v[...], gate_v[at, :], NT) + dot(us_v[...], up_v[at, :], NT)
                if square and k == 2:
                    io[k, top, at] = (part[:middle] + relay[0, :, at].astype(jnp.float32)).astype(bf16)
                    io[k, bottom, at] = part[middle:].astype(bf16)
                elif square and k == 1:
                    io[k, top, at] = part[:middle].astype(bf16)
                    io[k, bottom, at] = (part[middle:] + relay[1, :, at].astype(jnp.float32)).astype(bf16)
                else:
                    io[k, :, at] = part.astype(bf16)
                back = dot(mid_v[...], down_v[:, at], NN).astype(bf16)

                @pl.when(j >= 2)
                def _():
                    out_copy(j - 2).wait()

                out_v[j % 2] = back
                out_copy(j).start()
                return carry

            lax.fori_loop(0, strips, more, 0)
            out_copy(strips - 2).wait()
            out_copy(strips - 1).wait()
            if k == 0:
                pltpu.make_async_copy(io.at[0], dn_own, own_sem.at[1]).start()
            else:
                for copy in returns(k):
                    copy.start()
        pltpu.make_async_copy(io.at[0], dn_own, own_sem.at[1]).wait()

    pl.run_scoped(
        both_passes,
        pltpu.VMEM((width, inner), bf16),
        pltpu.VMEM((width, inner), bf16),
        pltpu.VMEM((inner, width), bf16),
    )

    total = peers * tokens
    block = 512

    def three_body(gs, us, gg, ug):
        at = pl.ds(pl.multiple_of(pl.program_id(0) * block, block), block)
        turned = jnp.transpose(nt_v[:, :, at].reshape(total, block))
        gg[...] = dot(turned, gs[...].reshape(total, inner), NN).astype(bf16)
        ug[...] = dot(turned, us[...].reshape(total, inner), NN).astype(bf16)

    fixed = pl.BlockSpec((peers, tokens, inner), lambda j: (0, 0, 0), pipeline_mode=pl.Buffered(1))
    pltpu.emit_pipeline(
        three_body,
        grid=(width // block,),
        in_specs=[fixed, fixed],
        out_specs=[pl.BlockSpec((block, inner), lambda j: (j, 0))] * 2,
    )(gs_all, us_all, gate_grad, up_grad)

    owned = width // chain
    per = 1280 // owned

    def four_body(og, mid, dg):
        turned = jnp.transpose(mid[...].reshape(total, tile))
        acc = dot(turned, og[...].reshape(total, 1280), NN).astype(bf16)
        for c in range(per):
            dg[c] = acc[:, c * owned : (c + 1) * owned]

    pltpu.emit_pipeline(
        four_body,
        grid=(width // 1280, inner // tile),
        in_specs=[
            pl.BlockSpec((peers, tokens, 1280), lambda i, j: (0, 0, i)),
            pl.BlockSpec((peers, tokens, tile), lambda i, j: (0, 0, j)),
        ],
        out_specs=[pl.BlockSpec((per, tile, owned), lambda i, j: (i, j, 0))],
    )(og_all, mid_all, down_grad)

    for copy in spread.values():
        copy.wait_send()
    for k in range(1, peers):
        for copy in returns(k):
            copy.wait_send()
            if not (square and k == 3):
                copy.wait_recv()


def feed(peers, chain, nt, og_all, down, pieces):
    tokens, width = nt.shape
    inner = down.shape[0]
    bf = jnp.bfloat16
    S = jax.ShapeDtypeStruct
    any_ = pl.BlockSpec(memory_space=pl.ANY)
    DMA = pltpu.SemaphoreType.DMA
    inner_shape = S((peers, tokens, inner), bf)
    halves = 2 if peers == 4 else peers - 1
    return pl.pallas_call(
        functools.partial(feed_kernel, peers, chain),
        in_specs=[any_] * (3 + len(pieces)),
        out_specs=[any_] * 9,
        out_shape=[inner_shape, inner_shape, inner_shape,
                   S((tokens, width), bf), S((halves, tokens, width), bf), S((peers, tokens, width), bf),
                   S((width, inner), bf), S((width, inner), bf), S((chain, inner, width // chain), bf)],
        scratch_shapes=[
            pltpu.VMEM((peers, tokens, width), bf),
            pltpu.VMEM((tokens, inner), bf), pltpu.VMEM((tokens, inner), bf), pltpu.VMEM((tokens, inner), bf),
            pltpu.VMEM((peers, tokens, width), bf),
            pltpu.VMEM((2, tokens // 2, width), bf),
            pltpu.VMEM((2, tokens, 256), bf),
            DMA((2,)), DMA((1 + 2 * len(pieces),)), DMA((3, 16)), DMA((2,)), DMA((2,)),
            DMA((peers,)), DMA((peers,)), DMA((peers,)), DMA((peers,)),
        ],
        compiler_params=pltpu.CompilerParams(vmem_limit_bytes=FEED_VMEM, collective_id=1, has_side_effects=True),
    )(nt, og_all, down, *pieces)


def boundaries(lengths, positions):
    cut_points = jnp.cumsum(lengths)[:-1]
    passed = positions[:, None] >= cut_points[None, :]
    return jnp.max(jnp.where(passed, cut_points[None, :], 0), axis=1)


def matmul(left, right):
    return dot(left, right, NN)


def matmul_back(gradient, weight):
    return dot(gradient, weight, NT)


def on_device(
    hidden_in,
    doc_lengths,
    attn_gain,
    query_weight,
    key_matrix,
    value_matrix,
    output_weight,
    mlp_gain,
    gate_weight,
    up_weight,
    down_weight,
    out_grad,
):
    owners, chain = lax.axis_size("fs"), lax.axis_size("ctx")
    owner, place = lax.axis_index("fs"), lax.axis_index("ctx")
    core = place % 2
    planes = chain // 2
    batches, length, width = hidden_in.shape
    tokens = batches * length
    rows = query_weight.shape[0]
    inner = down_weight.shape[0]
    count = min(WINDOW // length + 1, chain)
    at = jnp.stack([core, place]).astype(jnp.int32)
    siblings = [(i, i ^ 1) for i in range(chain)]
    onward = [(i, i + 2) for i in range(chain - 2)]
    homeward = [(i + 2, i) for i in range(chain - 2)]
    lines_of_chips = [[2 * i + j for i in range(planes)] for j in range(2)]

    def fetch(shard):
        part = shard.shape[1] // 2
        mine = lax.dynamic_slice_in_dim(shard, core * part, part, 1)
        mine = lax.all_gather(mine, "fs", axis=0, tiled=True)
        return mine, lax.ppermute(mine, "ctx", siblings)

    def halves(shard):
        return shard.reshape(rows, 2, -1)

    joined = jnp.concatenate(
        [halves(query_weight), halves(key_matrix), halves(value_matrix)], axis=2
    ).reshape(rows, -1)
    in_mine, in_other = fetch(joined)
    out_mine, out_other = fetch(output_weight)
    gain_one = lax.all_gather(attn_gain, "fs", axis=0, tiled=True).astype(jnp.float32)
    gain_two = lax.all_gather(mlp_gain, "fs", axis=0, tiled=True).astype(jnp.float32)

    def across(x, k):
        return lax.ppermute(x, "fs", [(i, i ^ k) for i in range(owners)])

    share = rows // 2
    both = jnp.stack([gate_weight, up_weight])
    both = lax.dynamic_slice_in_dim(both, core * share, share, 1)
    pieces = []
    for k in range(owners):
        piece = lax.dynamic_slice_in_dim(both, (owner ^ k) * inner, inner, 2)
        piece = across(piece, k) if k else piece
        pieces += [piece, lax.ppermute(piece, "ctx", siblings)]
    grads_in = out_grad.reshape(tokens, width)
    grads_all = lax.all_gather(grads_in, "fs", axis=0, tiled=False)

    positions = place * length + jnp.arange(length, dtype=jnp.int32)
    starts = jax.vmap(lambda lengths: boundaries(lengths, positions))(doc_lengths)
    low = jnp.maximum(starts, positions[None, :] - (WINDOW - 1))
    frequency = ROPE_THETA ** (-2.0 * jnp.arange(HALF, dtype=jnp.float32) / HEAD_SIZE)
    turns = (positions[None, :] - starts).reshape(tokens).astype(jnp.float32)
    angles = turns[:, None] * frequency[None, :]
    cosine, sine = jnp.cos(angles), jnp.sin(angles)
    cosine = jnp.tile(jnp.concatenate([cosine, cosine], axis=1), (1, STRIP // HEAD_SIZE))
    sine = jnp.tile(jnp.concatenate([-sine, sine], axis=1), (1, STRIP // HEAD_SIZE))
    is_key = (jnp.arange(STRIP) < HALF_KV)[None, :]
    cosine = jnp.stack([cosine, jnp.where(is_key, cosine, 1.0)])
    sine = jnp.stack([sine, jnp.where(is_key, sine, 0.0)])

    x = hidden_in.reshape(tokens, width).astype(jnp.float32)
    scale_one = lax.rsqrt(jnp.mean(x * x, axis=1, keepdims=True) + NORM_EPS)
    normed = (x * scale_one * gain_one).astype(jnp.bfloat16)
    core_ref = core.reshape(1).astype(jnp.int32)
    queries, kv = qkv_projection(core_ref, normed, in_mine, in_other, cosine, sine)
    kv = kv.reshape(2, batches, length, STRIP)
    line = [kv]
    for _ in range((count - 1) // 2):
        line.append(lax.ppermute(line[-1], "ctx", onward))
    line = jnp.stack(line)
    lines = (line, lax.ppermute(line, "ctx", siblings))
    queries = queries.reshape(batches, length, width)
    attended, lse = attend(at, queries, low[:, :, None], lines, count)
    attended_rows = attended.reshape(tokens, width)

    def in_order(mine, other):
        return jnp.where(
            core == 0,
            jnp.concatenate([mine, other], axis=1),
            jnp.concatenate([other, mine], axis=1),
        )

    projected = in_order(matmul(attended_rows, out_mine), matmul(attended_rows, out_other))
    residual = x + projected
    scale_two = lax.rsqrt(jnp.mean(residual * residual, axis=1, keepdims=True) + NORM_EPS)
    normed_two = (residual * scale_two * gain_two).astype(jnp.bfloat16)

    fed = feed(owners, chain, normed_two, grads_all, down_weight, pieces)
    own_part, in_parts, out_parts, gate_part, up_part, down_part = fed[3:]
    normed_two_grad = own_part.astype(jnp.float32) + jnp.sum(in_parts.astype(jnp.float32), axis=0)

    def fold_tokens(parts):
        total = lax.dynamic_index_in_dim(parts, owner, 0, keepdims=False).astype(jnp.float32)
        for k in range(1, owners):
            part = lax.dynamic_index_in_dim(parts, owner ^ k, 0, keepdims=False)
            total = total + across(part, k).astype(jnp.float32)
        return total

    hidden_out = residual + fold_tokens(out_parts)

    spans = chain // owners
    down_grad = lax.psum_scatter(down_part, "ctx", scatter_dimension=0, tiled=True)[0]
    down_grad = down_grad.astype(jnp.float32)
    gate_mine = lax.psum_scatter(gate_part, "ctx", scatter_dimension=0, tiled=True)
    up_mine = lax.psum_scatter(up_part, "ctx", scatter_dimension=0, tiled=True)
    slot = place % spans
    strip = inner // spans
    gate_grad = jnp.zeros((spans,) + (gate_mine.shape[0], strip), jnp.float32)
    up_grad = gate_grad
    for k in range(spans):
        moves = [
            (f * chain + c, (c // spans) * chain + f * spans + (c % spans + k) % spans)
            for f in range(owners)
            for c in range(chain)
        ]
        cut = ((slot + k) % spans) * strip
        piece = jnp.stack([lax.dynamic_slice_in_dim(m, cut, strip, 1) for m in (gate_mine, up_mine)])
        piece = lax.ppermute(piece, ("fs", "ctx"), moves).astype(jnp.float32)
        to = (slot - k) % spans
        gate_grad = lax.dynamic_update_slice_in_dim(gate_grad, piece[:1], to, 0)
        up_grad = lax.dynamic_update_slice_in_dim(up_grad, piece[1:], to, 0)
    gate_grad = gate_grad.reshape(rows, strip)
    up_grad = up_grad.reshape(rows, strip)

    scaled_two = normed_two_grad * gain_two
    residual_grad = grads_in.astype(jnp.float32) + scale_two * (
        scaled_two
        - residual * scale_two * scale_two * jnp.mean(scaled_two * residual, axis=1, keepdims=True)
    )
    gain_two_part = jnp.sum(normed_two_grad * residual * scale_two, axis=0)
    attn_grad = residual_grad.astype(jnp.bfloat16)
    part = width // 2
    grad_mine = lax.dynamic_slice_in_dim(attn_grad, core * part, part, 1)
    grad_other = lax.dynamic_slice_in_dim(attn_grad, (1 - core) * part, part, 1)
    attended_grad = (matmul_back(grad_mine, out_mine) + matmul_back(grad_other, out_other)).astype(
        jnp.bfloat16
    )
    query_slopes, kv_parts = attend_back(
        at,
        queries,
        attended_grad.reshape(batches, length, width),
        attended,
        lse,
        low[:, None, :],
        cosine,
        sine,
        lines,
        count,
    )
    parts = [kv_parts[count - 1 - back] for back in range(count)]
    odd = lax.ppermute(jnp.stack(parts[1::2]), "ctx", siblings).astype(jnp.float32)
    sums = []
    for step in range((count + 1) // 2):
        mine = parts[2 * step].astype(jnp.float32)
        nothing = jnp.zeros_like(mine)
        near = odd[step] if step < odd.shape[0] else nothing
        far = odd[step - 1] if step > 0 else nothing
        sums.append(mine + jnp.where(core == 0, near, far))
    moving = sums[-1]
    for step in range(len(sums) - 2, -1, -1):
        moving = lax.ppermute(moving.astype(jnp.bfloat16), "ctx", homeward).astype(jnp.float32)
        moving = moving + sums[step]
    kv_home = moving.astype(jnp.bfloat16)
    kv_slopes = unturn(kv_home.reshape(2, tokens, STRIP), cosine, sine)
    query_slopes = query_slopes.reshape(tokens, width)

    def by_owner(slopes):
        return slopes.reshape(tokens, planes, 2, -1)

    key_slopes = jnp.concatenate([kv_slopes[0, :, :HALF_KV], kv_slopes[1, :, :HALF_KV]], axis=1)
    value_slopes = jnp.concatenate([kv_slopes[0, :, HALF_KV:], kv_slopes[1, :, HALF_KV:]], axis=1)

    def fold_rows(left, slopes):
        own = slopes.shape[3]
        slopes = jnp.transpose(slopes, (2, 0, 1, 3)).reshape(2, tokens, planes * own)
        near = lax.dynamic_index_in_dim(slopes, core, 0, keepdims=False)
        far = lax.dynamic_index_in_dim(slopes, 1 - core, 0, keepdims=False)
        given = lax.ppermute(dot(left, far, TN).astype(jnp.bfloat16), "ctx", siblings)
        grads = (dot(left, near, TN) + given.astype(jnp.float32)).astype(jnp.bfloat16)
        grads = grads.reshape(owners, rows, planes * own)
        grads = fold_tokens(grads).astype(jnp.bfloat16)
        return lax.psum_scatter(
            grads, "ctx", scatter_dimension=1, tiled=True, axis_index_groups=lines_of_chips
        ).astype(jnp.float32)

    output_grad = fold_rows(attended_rows, by_owner(attn_grad))
    in_slopes = jnp.concatenate(
        [by_owner(query_slopes), by_owner(key_slopes), by_owner(value_slopes)], axis=3
    )
    in_grad = fold_rows(normed, in_slopes)
    q_own, kv_own = width // chain, KV_WIDTH // chain
    query_grad = in_grad[:, :q_own]
    key_grad = in_grad[:, q_own : q_own + kv_own]
    value_grad = in_grad[:, q_own + kv_own :]

    def half_slopes(half):
        return jnp.concatenate(
            [
                lax.dynamic_slice_in_dim(query_slopes, half * (width // 2), width // 2, 1),
                lax.dynamic_index_in_dim(kv_slopes, half, 0, keepdims=False),
            ],
            axis=1,
        )

    normed_grad = matmul_back(half_slopes(core), in_mine) + matmul_back(
        half_slopes(1 - core), in_other
    )
    scaled_one = normed_grad * gain_one
    hidden_grad = residual_grad + scale_one * (
        scaled_one - x * scale_one * scale_one * jnp.mean(scaled_one * x, axis=1, keepdims=True)
    )
    gain_one_part = jnp.sum(normed_grad * x * scale_one, axis=0)
    gains = jnp.stack([gain_one_part, gain_two_part], axis=1)
    gains = lax.psum_scatter(gains, "fs", scatter_dimension=0, tiled=True)
    gains = lax.psum(gains, "ctx")
    return (
        hidden_out.reshape(batches, length, width),
        hidden_grad.reshape(batches, length, width),
        gains[:, 0],
        query_grad,
        key_grad,
        value_grad,
        output_grad,
        gains[:, 1],
        gate_grad,
        up_grad,
        down_grad,
    )


def solution(mesh):
    tokens_spec = P("fs", "ctx", None)
    rows_spec = P("fs", None)
    block_spec = P("fs", "ctx")
    return jax.shard_map(
        on_device,
        mesh=mesh,
        in_specs=(
            tokens_spec,
            rows_spec,
            P("fs"),
            rows_spec,
            rows_spec,
            rows_spec,
            rows_spec,
            P("fs"),
            rows_spec,
            rows_spec,
            rows_spec,
            tokens_spec,
        ),
        out_specs=(
            tokens_spec,
            tokens_spec,
            P("fs"),
            block_spec,
            block_spec,
            block_spec,
            block_spec,
            P("fs"),
            block_spec,
            block_spec,
            block_spec,
        ),
        check_vma=False,
    )
```

```python
import functools
import math

import jax
import jax.numpy as jnp
from jax import lax
from jax.experimental import pallas as pl
from jax.experimental.pallas import tpu as pltpu
from jax.sharding import PartitionSpec as P

MODEL_WIDTH = 2560
QUERY_HEADS = 32
KEY_VALUE_HEADS = 8
HEAD_SIZE = 80
WINDOW = 1024
GROUPS = QUERY_HEADS // KEY_VALUE_HEADS
HALF = HEAD_SIZE // 2
KV_WIDTH = KEY_VALUE_HEADS * HEAD_SIZE
STRIP = 640
HALF_KV = KV_WIDTH // 2
SCALE = 1.0 / math.sqrt(HEAD_SIZE)

NORM_EPS = 1e-05
ROPE_THETA = 1000000.0
MASK_VALUE_FILL = -1e30
VMEM = 60 * 1024 * 1024
FEED_VMEM = 62 * 1024 * 1024
MESH = pl.DeviceIdType.MESH

NT = (((1,), (1,)), ((), ()))
TN = (((0,), (0,)), ((), ()))
NN = (((1,), (0,)), ((), ()))


def dot(left, right, dims):
    return lax.dot_general(left, right, dims, preferred_element_type=jnp.float32)


def params(**more):
    return pltpu.CompilerParams(vmem_limit_bytes=VMEM, **more)


def cost(flops, moved, exps=0):
    return pl.CostEstimate(flops=int(flops), bytes_accessed=int(moved), transcendentals=int(exps))


def turn(x, cosine, sine):
    width = x.shape[1]
    lane = lax.broadcasted_iota(jnp.int32, x.shape, 1) % HEAD_SIZE
    partner = jnp.where(
        lane < HALF, pltpu.roll(x, width - HALF, 1), pltpu.roll(x, HALF, 1)
    )
    return x * cosine + partner * sine


def unturn_kernel(x_ref, cos_ref, sin_ref, o_ref):
    x = x_ref[0].astype(jnp.float32)
    o_ref[...] = turn(x, cos_ref[...], -sin_ref[...]).astype(jnp.bfloat16)


def unturn(x, cosine, sine):
    tokens = x.shape[1]
    table = pl.BlockSpec((tokens, STRIP), lambda h: (0, 0))
    return pl.pallas_call(
        unturn_kernel,
        grid=(1,),
        in_specs=[pl.BlockSpec((1, tokens, STRIP), lambda h: (0, 0, 0)), table, table],
        out_specs=table,
        out_shape=jax.ShapeDtypeStruct((tokens, STRIP), jnp.bfloat16),
        compiler_params=params(),
        cost_estimate=cost(10 * x.size, 8 * x.size),
    )(x, cosine, sine)


def spread_heads(blocks, keys, values, length):
    last = len(blocks) - 1
    for back, block in enumerate(blocks):
        rows = pl.ds((last - back) * length, length)
        for head in range(KEY_VALUE_HEADS):
            at = head * HEAD_SIZE
            keys[head, rows, :] = block[0, 0, 0, :, at : at + HEAD_SIZE]
            values[head, rows, :] = block[0, 1, 0, :, at : at + HEAD_SIZE]


def kv_specs(count, length):
    def index(back, b, p, at):
        if back % 2 == 0:
            return (back // 2, 0, b, 0, 0)
        return ((back + 1) // 2 - at[0], 0, b, 0, 0)

    return [
        pl.BlockSpec((1, 2, 1, length, STRIP), functools.partial(index, back))
        for back in range(count)
    ]


def kv_operands(lines, count):
    return [lines[back % 2] for back in range(count)]


def attend_back_kernel(
    count, at_ref, q_ref, g_ref, a_ref, lse_ref, low_ref, cos_ref, sin_ref, *rest
):
    blocks, (dq_ref, dkv_ref), (keys, values, bias, key_sums, value_sums) = (
        rest[:count],
        rest[count : count + 2],
        rest[count + 2 :],
    )
    pair = pl.program_id(1)
    length = q_ref.shape[1]
    window = bias.shape[0]

    @pl.when(pair == 0)
    def _():
        spread_heads(blocks, keys, values, length)
        key_place = (at_ref[1] - count + 1) * length + lax.broadcasted_iota(jnp.int32, (window, length), 0)
        place = at_ref[1] * length + lax.broadcasted_iota(jnp.int32, (window, length), 1)
        seen = (key_place >= low_ref[0]) & (key_place <= place)
        bias[...] = jnp.where(seen, 0.0, MASK_VALUE_FILL)

    products = g_ref[0].astype(jnp.float32) * a_ref[0].astype(jnp.float32)
    heads = [
        jnp.sum(products[:, h * HEAD_SIZE : (h + 1) * HEAD_SIZE], axis=1, keepdims=True)
        for h in range(2 * GROUPS)
    ]
    spare = jnp.zeros((length, 128 - 2 * GROUPS), jnp.float32)
    deltas = jnp.transpose(jnp.concatenate(heads + [spare], axis=1))
    turned = []
    for side in range(2):
        key, value = keys[2 * pair + side], values[2 * pair + side]
        key_sum = jnp.zeros((window, HEAD_SIZE), jnp.float32)
        value_sum = jnp.zeros((window, HEAD_SIZE), jnp.float32)
        for group in range(GROUPS):
            row = side * GROUPS + group
            at = row * HEAD_SIZE
            query = q_ref[0, :, at : at + HEAD_SIZE]
            gradient = g_ref[0, :, at : at + HEAD_SIZE]
            chances = jnp.exp(
                dot(key, query, NT) * SCALE + bias[...] - lse_ref[0, 0, row : row + 1, :]
            )
            value_sum = value_sum + dot(chances.astype(jnp.bfloat16), gradient, NN)
            slopes = dot(value, gradient, NT) - deltas[row : row + 1, :]
            slopes = (chances * slopes).astype(jnp.bfloat16)
            key_sum = key_sum + dot(slopes, query, NN)
            turned.append(dot(slopes, key, TN) * SCALE)
        key_sums[2 * pair + side] = (key_sum * SCALE).astype(jnp.bfloat16)
        value_sums[2 * pair + side] = value_sum.astype(jnp.bfloat16)
    dq_ref[0] = turn(jnp.concatenate(turned, axis=1), cos_ref[...], -sin_ref[...]).astype(jnp.bfloat16)

    @pl.when(pair == pl.num_programs(1) - 1)
    def _():
        for step in range(count):
            rows = pl.ds(step * length, length)
            for kind, sums in ((0, key_sums), (1, value_sums)):
                dkv_ref[step, kind, 0] = jnp.concatenate(
                    [sums[h, rows, :] for h in range(KEY_VALUE_HEADS)], axis=1
                )


def attend_back(at, queries, gradient, attended, lse, low, cosine, sine, lines, count):
    batches, length, width = queries.shape
    pairs = KEY_VALUE_HEADS // 2
    window = count * length
    strip = pl.BlockSpec((1, length, STRIP), lambda b, p, at: (b, 0, p))
    table = pl.BlockSpec((length, STRIP), lambda b, p, at: (b, 0))
    grid_spec = pltpu.PrefetchScalarGridSpec(
        num_scalar_prefetch=1,
        grid=(batches, pairs),
        in_specs=[
            strip,
            strip,
            strip,
            pl.BlockSpec((1, 1, 2 * GROUPS, length), lambda b, p, at: (b, p, 0, 0)),
            pl.BlockSpec((1, 1, length), lambda b, p, at: (b, 0, 0)),
            table,
            table,
        ]
        + kv_specs(count, length),
        out_specs=[
            strip,
            pl.BlockSpec((count, 2, 1, length, STRIP), lambda b, p, at: (0, 0, b, 0, 0)),
        ],
        scratch_shapes=[
            pltpu.VMEM((KEY_VALUE_HEADS, window, HEAD_SIZE), jnp.bfloat16),
            pltpu.VMEM((KEY_VALUE_HEADS, window, HEAD_SIZE), jnp.bfloat16),
            pltpu.VMEM((window, length), jnp.float32),
            pltpu.VMEM((KEY_VALUE_HEADS, window, HEAD_SIZE), jnp.bfloat16),
            pltpu.VMEM((KEY_VALUE_HEADS, window, HEAD_SIZE), jnp.bfloat16),
        ],
    )
    return pl.pallas_call(
        functools.partial(attend_back_kernel, count),
        grid_spec=grid_spec,
        out_shape=[
            jax.ShapeDtypeStruct((batches, length, width), jnp.bfloat16),
            jax.ShapeDtypeStruct((count, 2, batches, length, STRIP), jnp.bfloat16),
        ],
        compiler_params=params(),
        cost_estimate=cost(
            5 * 2 * 2 * 128 * QUERY_HEADS * batches * length * window * 4,
            16 * queries.size,
            QUERY_HEADS * batches * length * window,
        ),
    )(at, queries, gradient, attended, lse, low, cosine, sine, *kv_operands(lines, count))


def toggled(me, k, count):
    found, bit = me, 1
    while bit < count:
        found = found + ((k // bit) % 2) * bit * (1 - 2 * ((me // bit) % 2))
        bit *= 2
    return found


def feed_kernel(
    peers, nt_ref, og_all, down_ref, gate_ref, up_ref, *rest
):
    (gs_all, us_all, mid_all, dn_own, dn_in, out_part, gate_grad, up_grad,
    nt_v, gs_v, us_v, mid_v, io, relay, out_v,
    load_sem, weight_sem, tile_sem, out_sem, own_sem, nt_send, nt_recv, dn_send, dn_recv) = rest
    tokens, width = nt_ref.shape
    inner = down_ref.shape[0]
    middle = tokens // 2
    square = peers == 4
    me = lax.axis_index("fs")
    bf16 = jnp.bfloat16

    def remote(src, dst, send, recv, at, k):
        return pltpu.make_async_remote_copy(
            src_ref=src, dst_ref=dst, send_sem=send.at[at], recv_sem=recv.at[at],
            device_id={"fs": toggled(me, k, peers)}, device_id_type=MESH,
        )

    barrier = pltpu.get_barrier_semaphore()
    for k in range(1, peers):
        pl.semaphore_signal(barrier, inc=1, device_id={"fs": toggled(me, k, peers)}, device_id_type=MESH)
    pl.semaphore_wait(barrier, peers - 1)

    top, bottom = pl.ds(0, middle), pl.ds(middle, middle)
    reached = [1, 2] if square else list(range(1, peers))
    spread = {k: remote(nt_ref, nt_v.at[k], nt_send, nt_recv, k, k) for k in reached}
    for k in reached:
        spread[k].start()
    if square:
        spread[3] = remote(nt_v.at[1, top], nt_v.at[3, top], nt_send, nt_recv, 3, 2)
        spread[0] = remote(nt_v.at[2, bottom], nt_v.at[3, bottom], nt_send, nt_recv, 0, 1)
    own = pltpu.make_async_copy(nt_ref, nt_v.at[0], own_sem.at[0])
    own.start()

    def returns(k):
        if square and k == 3:
            return (
                remote(io.at[3, top], relay.at[0], dn_send, dn_recv, 3, 1),
                remote(io.at[3, bottom], relay.at[1], dn_send, dn_recv, 0, 2),
            )
        return (remote(io.at[k], dn_in.at[k - 1], dn_send, dn_recv, k, k),)

    tile = 256 if inner % 256 == 0 else 128
    tiles = inner // tile
    wide = 256
    strips = width // wide

    def both_passes(gate_v, up_v, down_v):
        weights = [
            pltpu.make_async_copy(src, dst, weight_sem.at[i])
            for i, (src, dst) in enumerate(((gate_ref, gate_v), (up_ref, up_v), (down_ref, down_v)))
        ]
        for copy in weights:
            copy.start()

        def grads_of(k):
            return pltpu.make_async_copy(
                og_all.at[toggled(me, k, peers)], io.at[k % 2], load_sem.at[k % 2]
            )

        grads_of(0).start()
        own.wait()
        for copy in weights:
            copy.wait()

        def stores(k, at):
            return [
                pltpu.make_async_copy(src.at[:, at], dst.at[:, at], tile_sem.at[i, at.start // tile])
                for i, (src, dst) in enumerate(
                    (
                        (gs_v, gs_all.at[k]),
                        (us_v, us_all.at[k]),
                        (mid_v, mid_all.at[toggled(me, k, peers)]),
                    )
                )
            ]

        for k in range(peers):
            if square and k == 1:
                spread[1].wait_recv()
                spread[3].start()
                spread[2].wait_recv()
                spread[0].start()
            elif square and k == 3:
                spread[3].wait_recv()
                spread[0].wait_recv()
            elif not square and k > 0:
                spread[k].wait_recv()
            grads_of(k).wait()
            if k + 1 < peers:
                grads_of(k + 1).start()

            def some(j, carry, k=k):
                at = pl.ds(pl.multiple_of(j * tile, tile), tile)
                gate = dot(nt_v[k], gate_v[:, at], NN)
                up = dot(nt_v[k], up_v[:, at], NN)
                grad = dot(io[k % 2], down_v[at, :], NT)
                sig = 1.0 / (1.0 + jnp.exp(-gate))
                silu = gate * sig
                if k > 0:
                    for copy in stores(k - 1, at):
                        copy.wait()
                mid_v[:, at] = (silu * up).astype(bf16)
                gs_v[:, at] = (grad * up * sig * (1.0 + gate * (1.0 - sig))).astype(bf16)
                us_v[:, at] = (grad * silu).astype(bf16)
                for copy in stores(k, at):
                    copy.start()
                return carry

            lax.fori_loop(0, tiles, some, 0)

        def settle(j, carry):
            at = pl.ds(pl.multiple_of(j * tile, tile), tile)
            for copy in stores(peers - 1, at):
                copy.wait()
            return carry

        lax.fori_loop(0, tiles, settle, 0)

        order = [peers - 1, 0] + list(range(peers - 2, 0, -1))
        for turn, k in enumerate(order):
            slab = toggled(me, k, peers)
            if turn > 0:
                loads = [
                    pltpu.make_async_copy(src, dst, tile_sem.at[i, 0])
                    for i, (src, dst) in enumerate(
                        ((gs_all.at[k], gs_v), (us_all.at[k], us_v), (mid_all.at[slab], mid_v))
                    )
                ]
                for copy in loads:
                    copy.start()
                for copy in loads:
                    copy.wait()
            if square and k == 2:
                returns(3)[0].wait_recv()
            if square and k == 1:
                returns(3)[1].wait_recv()

            def out_copy(j, k=k, slab=slab):
                at = pl.ds(pl.multiple_of(j * wide, wide), wide)
                return pltpu.make_async_copy(out_v.at[j % 2], out_part.at[slab, :, at], out_sem.at[j % 2])

            def more(j, carry, k=k, turn=turn, out_copy=out_copy):
                at = pl.ds(pl.multiple_of(j * wide, wide), wide)
                part = dot(gs_v[...], gate_v[at, :], NT) + dot(us_v[...], up_v[at, :], NT)
                if square and k == 2:
                    io[k, top, at] = (part[:middle] + relay[0, :, at].astype(jnp.float32)).astype(bf16)
                    io[k, bottom, at] = part[middle:].astype(bf16)
                elif square and k == 1:
                    io[k, top, at] = part[:middle].astype(bf16)
                    io[k, bottom, at] = (part[middle:] + relay[1, :, at].astype(jnp.float32)).astype(bf16)
                else:
                    io[k, :, at] = part.astype(bf16)
                back = dot(mid_v[...], down_v[:, at], NN).astype(bf16)

                @pl.when(j >= 2)
                def _():
                    out_copy(j - 2).wait()

                out_v[j % 2] = back
                out_copy(j).start()
                return carry

            lax.fori_loop(0, strips, more, 0)
            out_copy(strips - 2).wait()
            out_copy(strips - 1).wait()
            if k == 0:
                pltpu.make_async_copy(io.at[0], dn_own, own_sem.at[1]).start()
            else:
                for copy in returns(k):
                    copy.start()
        pltpu.make_async_copy(io.at[0], dn_own, own_sem.at[1]).wait()

    pl.run_scoped(
        both_passes,
        pltpu.VMEM((width, inner), bf16),
        pltpu.VMEM((width, inner), bf16),
        pltpu.VMEM((inner, width), bf16),
    )

    total = peers * tokens
    block = 512

    def three_body(gs, us, gg, ug):
        at = pl.ds(pl.multiple_of(pl.program_id(0) * block, block), block)
        turned = jnp.transpose(nt_v[:, :, at].reshape(total, block))
        gg[...] = dot(turned, gs[...].reshape(total, inner), NN).astype(bf16)
        ug[...] = dot(turned, us[...].reshape(total, inner), NN).astype(bf16)

    fixed = pl.BlockSpec((peers, tokens, inner), lambda j: (0, 0, 0), pipeline_mode=pl.Buffered(1))
    pltpu.emit_pipeline(
        three_body,
        grid=(width // block,),
        in_specs=[fixed, fixed],
        out_specs=[pl.BlockSpec((block, inner), lambda j: (j, 0))] * 2,
    )(gs_all, us_all, gate_grad, up_grad)

    for copy in spread.values():
        copy.wait_send()
    for k in range(1, peers):
        for copy in returns(k):
            copy.wait_send()
            if not (square and k == 3):
                copy.wait_recv()


def feed(peers, nt, og_all, down, gate, up):
    tokens, width = nt.shape
    inner = down.shape[0]
    bf = jnp.bfloat16
    S = jax.ShapeDtypeStruct
    any_ = pl.BlockSpec(memory_space=pl.ANY)
    DMA = pltpu.SemaphoreType.DMA
    inner_shape = S((peers, tokens, inner), bf)
    halves = 2 if peers == 4 else peers - 1
    return pl.pallas_call(
        functools.partial(feed_kernel, peers),
        in_specs=[any_] * 5,
        out_specs=[any_] * 8,
        out_shape=[inner_shape, inner_shape, inner_shape,
                   S((tokens, width), bf), S((halves, tokens, width), bf), S((peers, tokens, width), bf),
                   S((width, inner), bf), S((width, inner), bf)],
        scratch_shapes=[
            pltpu.VMEM((peers, tokens, width), bf),
            pltpu.VMEM((tokens, inner), bf), pltpu.VMEM((tokens, inner), bf), pltpu.VMEM((tokens, inner), bf),
            pltpu.VMEM((peers, tokens, width), bf),
            pltpu.VMEM((2, tokens // 2, width), bf),
            pltpu.VMEM((2, tokens, 256), bf),
            DMA((2,)), DMA((3,)), DMA((3, 16)), DMA((2,)), DMA((2,)),
            DMA((peers,)), DMA((peers,)), DMA((peers,)), DMA((peers,)),
        ],
        compiler_params=pltpu.CompilerParams(vmem_limit_bytes=FEED_VMEM, collective_id=1, has_side_effects=True),
        cost_estimate=cost(16 * peers * tokens * width * inner, 40 * width * inner, peers * tokens * inner),
    )(nt, og_all, down, gate, up)


def down_fold_kernel(og_ref, mid_ref, out_ref):
    peers, tokens, tile = mid_ref.shape
    owned = out_ref.shape[2]
    turned = jnp.transpose(mid_ref[...].reshape(peers * tokens, tile))
    wide = og_ref.shape[2]
    acc = dot(turned, og_ref[...].reshape(peers * tokens, wide), NN).astype(jnp.bfloat16)
    for c in range(out_ref.shape[0]):
        out_ref[c] = acc[:, c * owned : (c + 1) * owned]


def down_fold(og_all, mid_all, chain):
    peers, tokens, width = og_all.shape
    inner = mid_all.shape[2]
    tile = 256 if inner % 256 == 0 else 128
    owned = width // chain
    wide = 1280
    return pl.pallas_call(
        down_fold_kernel,
        grid=(width // wide, inner // tile),
        in_specs=[
            pl.BlockSpec((peers, tokens, wide), lambda i, j: (0, 0, i)),
            pl.BlockSpec((peers, tokens, tile), lambda i, j: (0, 0, j)),
        ],
        out_specs=pl.BlockSpec((wide // owned, tile, owned), lambda i, j: (i, j, 0)),
        out_shape=jax.ShapeDtypeStruct((chain, inner, owned), jnp.bfloat16),
        compiler_params=params(),
        cost_estimate=cost(2 * peers * tokens * width * inner, 2 * (og_all.size + 3 * mid_all.size)),
    )(og_all, mid_all)


def outer_kernel(left_ref, right_ref, *rest):
    given, out_ref = rest if len(rest) == 2 else (None, *rest)
    owners, _, _, rows = out_ref.shape
    turned = jnp.transpose(right_ref[0])
    for owner in range(owners):
        part = dot(turned, left_ref[:, owner * rows : (owner + 1) * rows], NN)
        if given is not None:
            part = part + given[owner, 0].astype(jnp.float32)
        out_ref[owner, 0] = part.astype(jnp.bfloat16)


def outer(left, right, owners, given=None):
    tokens, width = left.shape
    planes, _, own = right.shape
    rows = width // owners
    block = pl.BlockSpec((owners, 1, own, rows), lambda p: (0, p, 0, 0))
    operands = [left, right] + ([] if given is None else [given])
    return pl.pallas_call(
        outer_kernel,
        grid=(planes,),
        in_specs=[
            pl.BlockSpec((tokens, width), lambda p: (0, 0)),
            pl.BlockSpec((1, tokens, own), lambda p: (p, 0, 0)),
        ]
        + [block] * (len(operands) - 2),
        out_specs=block,
        out_shape=jax.ShapeDtypeStruct((owners, planes, own, rows), jnp.bfloat16),
        compiler_params=params(),
        cost_estimate=cost(2 * tokens * width * planes * own, 2 * left.size + 4 * width * planes * own),
    )(*operands)


def front_kernel(peers, chain, count, batches, *refs):
    (hid, gains, q_w, k_w, v_w, o_w, gate_w, up_w, og, cos_ref, sin_ref, low_ref) = refs[:12]
    (w_in, o_full, gate_part, up_part, og_all, normed_o, q_o, line_o, sib_o, att_o, lse_o, gain_o) = refs[12:24]
    (w_v, nt_v, nt_b, q_v, att_v, line_v, sib_v, gains_v) = refs[24:32]
    (own_sem, out_sem, gain_s, gain_r, qkv_s, qkv_r, twin_s, twin_r, back_s, back_r,
     og_s, og_r, hop_s, hop_r, kin_s, kin_r) = refs[32:]
    tokens, width = nt_v.shape
    rows = q_w.shape[0]
    inner = gate_part.shape[1]
    length = tokens // batches
    slots = line_v.shape[0]
    window = count * length
    square = peers == 4
    bf16, f32 = jnp.bfloat16, jnp.float32
    me, place = lax.axis_index("fs"), lax.axis_index("ctx")
    core, plane = place % 2, place // 2
    parity = plane % 2
    twin = place + 1 - 2 * core
    partner = place + 2 - 4 * parity
    deep = place >= 2
    ahead = place + 2 < chain

    def send(src, dst, send_sem, recv_sem, target):
        return pltpu.make_async_remote_copy(
            src_ref=src, dst_ref=dst, send_sem=send_sem, recv_sem=recv_sem,
            device_id=target, device_id_type=MESH,
        )

    def owner(k):
        return toggled(me, k, peers)

    def along(k):
        return {"fs": owner(k)}

    for i in range(1, slots):

        @pl.when(plane < i)
        def _(i=i):
            line_v[i] = jnp.zeros(line_v.shape[1:], bf16)
            sib_v[i] = jnp.zeros(line_v.shape[1:], bf16)

    barrier = pltpu.get_barrier_semaphore()
    for k in range(1, peers):
        pl.semaphore_signal(barrier, inc=1, device_id=along(k), device_id_type=MESH)
    pl.semaphore_signal(barrier, inc=1, device_id={"ctx": twin}, device_id_type=MESH)

    @pl.when(deep)
    def _():
        pl.semaphore_signal(barrier, inc=1, device_id={"ctx": place - 2}, device_id_type=MESH)

    @pl.when(ahead)
    def _():
        pl.semaphore_signal(barrier, inc=1, device_id={"ctx": place + 2}, device_id_type=MESH)

    planes = chain // 2
    behind = (plane + planes - 1) // planes
    before = (2 * planes - 2 - plane) // planes
    pl.semaphore_wait(barrier, peers + behind + before)

    share = rows // 2
    half = share // 2
    mats = ((q_w, pl.ds(0, width)), (k_w, pl.ds(width, KV_WIDTH)), (v_w, pl.ds(width + KV_WIDTH, KV_WIDTH)))

    def block(k, at, size):
        return pl.ds(pl.multiple_of(owner(k) * rows + core * share + at, 16), size)

    def first_hop(k, m):
        src, cols = mats[m]
        mine = pl.ds(pl.multiple_of(core * share, 16), share)
        return send(src.at[mine, :], w_v.at[block(0, 0, share), cols], qkv_s.at[k, m], qkv_r.at[k, m], along(k))

    def relay(part, m):
        source, target = (1, 2) if part == 3 else (2, 1)
        where = w_v.at[block(source, 0 if part == 3 else half, half), mats[m][1]]
        return send(where, where, qkv_s.at[part, m], qkv_r.at[part, m], along(target))

    def to_twin(part, m):
        if square and part in (0, 3):
            rows_at = block(3, 0 if part == 3 else half, half)
        else:
            rows_at = block(part, 0, share)
        where = w_v.at[rows_at, mats[m][1]]
        return send(where, where, twin_s.at[part, m], twin_r.at[part, m], {"ctx": twin})

    reached = [1, 2] if square else list(range(1, peers))
    for k in reached:
        for m in range(3):
            first_hop(k, m).start()
    own_rows = pl.ds(pl.multiple_of(me * rows, 16), rows)
    own_loads = [
        pltpu.make_async_copy(src, w_v.at[own_rows, cols], own_sem.at[i])
        for i, (src, cols) in enumerate(mats)
    ]
    for copy in own_loads:
        copy.start()
    gain_moves = [send(gains, gains_v.at[me], gain_s.at[k], gain_r.at[k], along(k)) for k in range(1, peers)]
    for copy in gain_moves:
        copy.start()
    gains_v[me] = gains[...]
    for copy in gain_moves:
        copy.wait_recv()
    whole_gain = jnp.concatenate([gains_v[f] for f in range(peers)], axis=1)
    gain_o[...] = whole_gain

    chunk = 64

    def norm(i, carry):
        at = pl.ds(pl.multiple_of(i * chunk, chunk), chunk)
        x = hid[at, :].astype(f32)
        scale = lax.rsqrt(jnp.mean(x * x, axis=1, keepdims=True) + NORM_EPS)
        normed = (x * scale * whole_gain[0:1]).astype(bf16)
        nt_v[at, :] = normed
        for f in range(peers):
            nt_b[f, at, :] = normed[:, f * rows : (f + 1) * rows]
        return carry

    lax.fori_loop(0, tokens // chunk, norm, 0)
    normed_out = pltpu.make_async_copy(nt_v, normed_o, out_sem.at[0])
    normed_out.start()

    quarter = rows // 4
    sources = (o_w, gate_w, up_w)
    fulls = (o_full, gate_part, up_part)

    def region(m, k, c, p):
        return fulls[m].at[pl.ds(pl.multiple_of(owner(k) * rows + (c + 2 * p) * quarter, 16), quarter), :]

    def back_first(m, k):
        at = pl.ds(pl.multiple_of((core + 2 * parity) * quarter, 16), quarter)
        if m == 0:
            src = o_w.at[at, :]
        else:
            src = sources[m].at[at, pl.ds(pl.multiple_of(owner(k) * inner, 128), inner)]
        return send(src, region(m, 0, core, parity), back_s.at[0, m, k], back_r.at[0, m, k], along(k))

    def back_plane(m, k):
        where = region(m, k, core, parity)
        return send(where, where, back_s.at[1, m, k], back_r.at[1, m, k], {"ctx": partner})

    def back_twin(m, k, p, stage):
        where = region(m, k, core, p)
        return send(where, where, back_s.at[stage, m, k], back_r.at[stage, m, k], {"ctx": twin})

    others = range(1, peers)

    def spread_first(which):
        for m in which:
            for k in others:
                back_first(m, k).start()

    def spread_second(which):
        for m in which:
            for k in others:
                back_first(m, k).wait_recv()
                back_plane(m, k).start()
                back_twin(m, k, parity, 2).start()

    def spread_third(which):
        for m in which:
            for k in others:
                back_plane(m, k).wait_recv()
                back_twin(m, k, 1 - parity, 3).start()

    def og_hop(k):
        return send(og, og_all.at[me], og_s.at[k], og_r.at[k], along(k))

    middle = tokens // 2

    def og_relay(part):
        source, target = (1, 2) if part == 3 else (2, 1)
        where = og_all.at[owner(source), pl.ds(0 if part == 3 else middle, middle), :]
        return send(where, where, og_s.at[part], og_r.at[part], along(target))

    wide = STRIP
    tiles = w_v.shape[1] // wide

    def project(acc, bounce):
        def through(src, dst, sem):
            shape = src.shape
            there = bounce.at[pl.ds(0, shape[0]), pl.ds(0, shape[1])]
            copy = pltpu.make_async_copy(src, there, sem.at[3])
            copy.start()
            copy.wait()
            copy = pltpu.make_async_copy(there, dst, sem.at[4])
            copy.start()
            copy.wait()

        through(og, og_all.at[me], own_sem)
        through(o_w, o_full.at[own_rows, :], own_sem)
        mine = pl.ds(pl.multiple_of(me * inner, 128), inner)
        through(gate_w.at[:, mine], gate_part.at[own_rows, :], own_sem)
        through(up_w.at[:, mine], up_part.at[own_rows, :], own_sem)
        for copy in own_loads:
            copy.wait()

        def add(k):
            rows_at = pl.ds(pl.multiple_of(owner(k) * rows, 16), rows)

            def one(j, carry):
                at = pl.ds(pl.multiple_of(j * wide, wide), wide)
                part = dot(nt_b[owner(k)], w_v[rows_at, at], NN)
                acc[:, at] = part if k == 0 else acc[:, at] + part
                return carry

            lax.fori_loop(0, tiles, one, 0)

        add(0)
        if square:
            for k, part in ((1, 3), (2, 0)):
                for m in range(3):
                    first_hop(k, m).wait_recv()
                for m in range(3):
                    relay(part, m).start()
                    to_twin(k, m).start()
                if k == 2:
                    spread_first([0])
                for m in range(3):
                    to_twin(k, m).wait_recv()
                add(k)
            for part in (3, 0):
                for m in range(3):
                    relay(part, m).wait_recv()
                    to_twin(part, m).start()
            spread_first([1, 2])
            for k in (1, 2):
                og_hop(k).start()
            for part in (3, 0):
                for m in range(3):
                    to_twin(part, m).wait_recv()
            add(3)
        else:
            for k in others:
                for m in range(3):
                    first_hop(k, m).wait_recv()
                    to_twin(k, m).start()
                for m in range(3):
                    to_twin(k, m).wait_recv()
                add(k)
            spread_first([0, 1, 2])
            for k in others:
                og_hop(k).start()

        line_v[0, 0] = turn(acc[:, width : width + KV_WIDTH], cos_ref[...], sin_ref[...]).astype(bf16)
        line_v[0, 1] = acc[:, width + KV_WIDTH :].astype(bf16)

        @pl.when(ahead)
        def _():
            hop(0).start()

        kin(0).start()

        def finish(j, carry):
            at = pl.ds(pl.multiple_of(j * wide, wide), wide)
            q_v[:, at] = turn(acc[:, at], cos_ref[...], sin_ref[...]).astype(bf16)
            return carry

        lax.fori_loop(0, width // wide, finish, 0)

    def hop(i):
        return send(line_v.at[i], line_v.at[i + 1], hop_s.at[i], hop_r.at[i], {"ctx": place + 2})

    def kin(i):
        return send(line_v.at[i], sib_v.at[i], kin_s.at[i], kin_r.at[i], {"ctx": twin})

    pl.run_scoped(project, pltpu.VMEM((tokens, w_v.shape[1]), f32), pltpu.VMEM((rows, width), bf16))

    w_out = pltpu.make_async_copy(w_v, w_in, out_sem.at[1])
    w_out.start()
    q_out = pltpu.make_async_copy(q_v, q_o, out_sem.at[2])
    q_out.start()
    spread_second([0])
    for i in range(1, slots):

        @pl.when(plane >= i)
        def _(i=i):
            hop(i - 1).wait_recv()
            kin(i).start()

        if i + 1 < slots:

            @pl.when((plane >= i) & ahead)
            def _(i=i):
                hop(i).start()

    kin(0).wait_recv()
    for i in range(1, slots):

        @pl.when(plane >= i)
        def _(i=i):
            kin(i).wait_recv()

    line_out = pltpu.make_async_copy(line_v, line_o, out_sem.at[3])
    line_out.start()
    sib_out = pltpu.make_async_copy(sib_v, sib_o, out_sem.at[4])
    sib_out.start()

    def attention(keys, values, bias):
        for b in range(batches):
            here = pl.ds(b * length, length)
            for back in range(count):
                at_rows = pl.ds((count - 1 - back) * length, length)
                for kind, target in ((0, keys), (1, values)):
                    if back % 2 == 0:
                        found = line_v[back // 2, kind, here, :]
                    else:
                        found = sib_v[(back + 1) // 2 - core, kind, here, :]
                    for head in range(KEY_VALUE_HEADS):
                        target[head, at_rows, :] = found[:, head * HEAD_SIZE : (head + 1) * HEAD_SIZE]
            key_place = (place - count + 1) * length + lax.broadcasted_iota(jnp.int32, (length, window), 1)
            query_place = place * length + lax.broadcasted_iota(jnp.int32, (length, window), 0)
            seen = (key_place >= low_ref[b]) & (key_place <= query_place)
            bias[...] = jnp.where(seen, 0.0, MASK_VALUE_FILL)

            def pair_of_heads(pair, carry, b=b, here=here):
                cols = pl.ds(pl.multiple_of(pair * STRIP, STRIP), STRIP)
                strip = q_v[here, cols]
                mixed, sums = [], []
                for side in range(2):
                    key, value = keys[2 * pair + side], values[2 * pair + side]
                    for group in range(GROUPS):
                        at = (side * GROUPS + group) * HEAD_SIZE
                        scores = dot(strip[:, at : at + HEAD_SIZE], key, NT) * SCALE + bias[...]
                        peak = jnp.max(scores, axis=1, keepdims=True)
                        weights = jnp.exp(scores - peak)
                        total = jnp.sum(weights, axis=1, keepdims=True)
                        mixed.append(dot(weights.astype(bf16), value, NN) / total)
                        sums.append(peak + jnp.log(total))
                att_v[here, cols] = jnp.concatenate(mixed, axis=1).astype(bf16)
                spare = jnp.zeros((length, 128 - 2 * GROUPS), f32)
                turned = jnp.transpose(jnp.concatenate(sums + [spare], axis=1))
                lse_o[b, pair] = turned[: 2 * GROUPS]
                return carry

            lax.fori_loop(0, KEY_VALUE_HEADS // 2, pair_of_heads, 0)
            if b == 0:
                spread_third([0])
                spread_second([1, 2])
                if square:
                    for k, part in ((1, 3), (2, 0)):
                        og_hop(k).wait_recv()
                        og_relay(part).start()

    pl.run_scoped(
        attention,
        pltpu.VMEM((KEY_VALUE_HEADS, window, HEAD_SIZE), bf16),
        pltpu.VMEM((KEY_VALUE_HEADS, window, HEAD_SIZE), bf16),
        pltpu.VMEM((length, window), f32),
    )
    att_out = pltpu.make_async_copy(att_v, att_o, out_sem.at[5])
    att_out.start()
    spread_third([1, 2])

    for copy in (normed_out, w_out, q_out, line_out, sib_out, att_out):
        copy.wait()
    for copy in gain_moves:
        copy.wait_send()
    for m in range(3):
        for k in reached:
            first_hop(k, m).wait_send()
            to_twin(k, m).wait_send()
        if square:
            for part in (3, 0):
                relay(part, m).wait_send()
                to_twin(part, m).wait_send()
    for k in reached:
        og_hop(k).wait_send()
        if not square:
            og_hop(k).wait_recv()
    if square:
        for part in (3, 0):
            og_relay(part).wait()
    for m in range(3):
        for k in others:
            back_first(m, k).wait_send()
            back_plane(m, k).wait_send()
            back_twin(m, k, parity, 2).wait()
            back_twin(m, k, 1 - parity, 3).wait()
    kin(0).wait_send()

    @pl.when(ahead)
    def _():
        hop(0).wait_send()

    for i in range(1, slots):

        @pl.when(plane >= i)
        def _(i=i):
            kin(i).wait_send()

        if i + 1 < slots:

            @pl.when((plane >= i) & ahead)
            def _(i=i):
                hop(i).wait_send()


def front(peers, chain, count, hidden, gains, weights, og, cosine, sine, low):
    batches, length, _ = low.shape
    tokens, width = hidden.shape
    rows = weights[0].shape[0]
    inner = weights[4].shape[1] // peers
    slots = (count - 1) // 2 + 1
    bf = jnp.bfloat16
    S = jax.ShapeDtypeStruct
    DMA = pltpu.SemaphoreType.DMA
    far = pl.BlockSpec(memory_space=pl.ANY)
    near = pl.BlockSpec(memory_space=pltpu.VMEM)
    whole = S((tokens, width), bf)
    line = (slots, 2, tokens, KV_WIDTH)
    return pl.pallas_call(
        functools.partial(front_kernel, peers, chain, count, batches),
        in_specs=[near, near] + [far] * 7 + [near] * 3,
        out_specs=[far] * 10 + [near, near],
        out_shape=[
            S((width, width + 2 * KV_WIDTH), bf),
            S((width, width), bf),
            S((width, inner), bf),
            S((width, inner), bf),
            S((peers, tokens, width), bf),
            whole,
            whole,
            S(line, bf),
            S(line, bf),
            whole,
            S((batches, KEY_VALUE_HEADS // 2, 2 * GROUPS, length), jnp.float32),
            S((8, width), jnp.float32),
        ],
        scratch_shapes=[
            pltpu.VMEM((width, width + 2 * KV_WIDTH), bf),
            pltpu.VMEM((tokens, width), bf),
            pltpu.VMEM((peers, tokens, rows), bf),
            pltpu.VMEM((tokens, width), bf),
            pltpu.VMEM((tokens, width), bf),
            pltpu.VMEM(line, bf),
            pltpu.VMEM(line, bf),
            pltpu.VMEM((peers, 8, rows), jnp.float32),
            DMA((5,)), DMA((6,)), DMA((peers,)), DMA((peers,)),
            DMA((peers, 3)), DMA((peers, 3)), DMA((peers, 3)), DMA((peers, 3)),
            DMA((4, 3, peers)), DMA((4, 3, peers)), DMA((peers,)), DMA((peers,)),
            DMA((slots,)), DMA((slots,)), DMA((slots,)), DMA((slots,)),
        ],
        compiler_params=pltpu.CompilerParams(
            vmem_limit_bytes=FEED_VMEM, collective_id=2, has_side_effects=True
        ),
        cost_estimate=cost(2 * tokens * width * 3840 * 10, 200 * tokens * width, QUERY_HEADS * tokens * count * length),
    )(hidden, gains, *weights, og, cosine, sine, low)


def boundaries(lengths, positions):
    cut_points = jnp.cumsum(lengths)[:-1]
    passed = positions[:, None] >= cut_points[None, :]
    return jnp.max(jnp.where(passed, cut_points[None, :], 0), axis=1)


def matmul(left, right):
    return dot(left, right, NN)


def matmul_back(gradient, weight):
    return dot(gradient, weight, NT)


def on_device(
    hidden_in,
    doc_lengths,
    attn_gain,
    query_weight,
    key_matrix,
    value_matrix,
    output_weight,
    mlp_gain,
    gate_weight,
    up_weight,
    down_weight,
    out_grad,
):
    owners, chain = lax.axis_size("fs"), lax.axis_size("ctx")
    owner, place = lax.axis_index("fs"), lax.axis_index("ctx")
    core = place % 2
    planes = chain // 2
    batches, length, width = hidden_in.shape
    tokens = batches * length
    rows = query_weight.shape[0]
    inner = down_weight.shape[0]
    count = min(WINDOW // length + 1, chain)
    at = jnp.stack([core, place]).astype(jnp.int32)
    siblings = [(i, i ^ 1) for i in range(chain)]
    onward = [(i, i + 2) for i in range(chain - 2)]
    homeward = [(i + 2, i) for i in range(chain - 2)]
    lines_of_chips = [[2 * i + j for i in range(planes)] for j in range(2)]

    def across(x, k):
        return lax.ppermute(x, "fs", [(i, i ^ k) for i in range(owners)])

    grads_in = out_grad.reshape(tokens, width)

    positions = place * length + jnp.arange(length, dtype=jnp.int32)
    starts = jax.vmap(lambda lengths: boundaries(lengths, positions))(doc_lengths)
    low = jnp.maximum(starts, positions[None, :] - (WINDOW - 1))
    frequency = ROPE_THETA ** (-2.0 * jnp.arange(HALF, dtype=jnp.float32) / HEAD_SIZE)
    turns = (positions[None, :] - starts).reshape(tokens).astype(jnp.float32)
    angles = turns[:, None] * frequency[None, :]
    cosine, sine = jnp.cos(angles), jnp.sin(angles)
    cosine = jnp.tile(jnp.concatenate([cosine, cosine], axis=1), (1, STRIP // HEAD_SIZE))
    sine = jnp.tile(jnp.concatenate([-sine, sine], axis=1), (1, STRIP // HEAD_SIZE))

    gains = jnp.concatenate([jnp.stack([attn_gain, mlp_gain]).astype(jnp.float32), jnp.zeros((6, rows))])
    (
        in_full, out_full, gate_full, up_full, grads_all, normed, queries, line, kin, attended_rows, lse, gain_rows
    ) = front(
        owners,
        chain,
        count,
        hidden_in.reshape(tokens, width),
        gains,
        (query_weight, key_matrix, value_matrix, output_weight, gate_weight, up_weight),
        grads_in,
        cosine,
        sine,
        low[:, :, None],
    )
    gain_one, gain_two = gain_rows[0], gain_rows[1]
    lines = [x.reshape(x.shape[:2] + (batches, length, KV_WIDTH)) for x in (line, kin)]
    queries = queries.reshape(batches, length, width)
    attended = attended_rows.reshape(batches, length, width)

    x = hidden_in.reshape(tokens, width).astype(jnp.float32)
    scale_one = lax.rsqrt(jnp.mean(x * x, axis=1, keepdims=True) + NORM_EPS)
    projected = matmul(attended_rows, out_full)
    residual = x + projected
    scale_two = lax.rsqrt(jnp.mean(residual * residual, axis=1, keepdims=True) + NORM_EPS)
    normed_two = (residual * scale_two * gain_two).astype(jnp.bfloat16)

    fed = feed(owners, normed_two, grads_all, down_weight, gate_full, up_full)
    own_part, in_parts, out_parts, gate_part, up_part = fed[3:]
    normed_two_grad = own_part.astype(jnp.float32) + jnp.sum(in_parts.astype(jnp.float32), axis=0)

    def fold_tokens(parts):
        total = lax.dynamic_index_in_dim(parts, owner, 0, keepdims=False).astype(jnp.float32)
        for k in range(1, owners):
            part = lax.dynamic_index_in_dim(parts, owner ^ k, 0, keepdims=False)
            total = total + across(part, k).astype(jnp.float32)
        return total

    spans = chain // owners
    down_part = down_fold(grads_all, fed[2], chain)
    down_grad = lax.psum_scatter(down_part, "ctx", scatter_dimension=0, tiled=True)[0]
    down_grad = down_grad.astype(jnp.float32)
    gate_mine = lax.psum_scatter(gate_part, "ctx", scatter_dimension=0, tiled=True)
    up_mine = lax.psum_scatter(up_part, "ctx", scatter_dimension=0, tiled=True)
    slot = place % spans
    strip = inner // spans
    gate_grad = jnp.zeros((spans,) + (gate_mine.shape[0], strip), jnp.float32)
    up_grad = gate_grad
    for k in range(spans):
        moves = [
            (f * chain + c, (c // spans) * chain + f * spans + (c % spans + k) % spans)
            for f in range(owners)
            for c in range(chain)
        ]
        cut = ((slot + k) % spans) * strip
        piece = jnp.stack([lax.dynamic_slice_in_dim(m, cut, strip, 1) for m in (gate_mine, up_mine)])
        piece = lax.ppermute(piece, ("fs", "ctx"), moves).astype(jnp.float32)
        to = (slot - k) % spans
        gate_grad = lax.dynamic_update_slice_in_dim(gate_grad, piece[:1], to, 0)
        up_grad = lax.dynamic_update_slice_in_dim(up_grad, piece[1:], to, 0)
    gate_grad = gate_grad.reshape(rows, strip)
    up_grad = up_grad.reshape(rows, strip)

    scaled_two = normed_two_grad * gain_two
    residual_grad = grads_in.astype(jnp.float32) + scale_two * (
        scaled_two
        - residual * scale_two * scale_two * jnp.mean(scaled_two * residual, axis=1, keepdims=True)
    )
    gain_two_part = jnp.sum(normed_two_grad * residual * scale_two, axis=0)
    attn_grad = residual_grad.astype(jnp.bfloat16)
    attended_grad = matmul_back(attn_grad, out_full).astype(jnp.bfloat16)
    query_slopes, kv_parts = attend_back(
        at,
        queries,
        attended_grad.reshape(batches, length, width),
        attended,
        lse,
        low[:, None, :],
        cosine,
        sine,
        lines,
        count,
    )
    parts = [kv_parts[count - 1 - back] for back in range(count)]
    odd = lax.ppermute(jnp.stack(parts[1::2]), "ctx", siblings).astype(jnp.float32)
    sums = []
    for step in range((count + 1) // 2):
        mine = parts[2 * step].astype(jnp.float32)
        nothing = jnp.zeros_like(mine)
        near = odd[step] if step < odd.shape[0] else nothing
        far = odd[step - 1] if step > 0 else nothing
        sums.append(mine + jnp.where(core == 0, near, far))
    moving = sums[-1]
    for step in range(len(sums) - 2, -1, -1):
        moving = lax.ppermute(moving.astype(jnp.bfloat16), "ctx", homeward).astype(jnp.float32)
        moving = moving + sums[step]
    kv_home = moving.astype(jnp.bfloat16)
    kv_home = kv_home.reshape(2, tokens, KV_WIDTH)
    key_slopes, value_slopes = unturn(kv_home, cosine, sine), kv_home[1]
    query_slopes = query_slopes.reshape(tokens, width)
    residual_late = lax.optimization_barrier((residual, query_slopes))[0]
    hidden_out = residual_late + fold_tokens(out_parts)

    def by_owner(slopes):
        return jnp.transpose(slopes.reshape(tokens, planes, 2, -1), (2, 1, 0, 3))

    def fold_rows(left, slopes):
        near = lax.dynamic_index_in_dim(slopes, core, 0, keepdims=False)
        far = lax.dynamic_index_in_dim(slopes, 1 - core, 0, keepdims=False)
        given = lax.ppermute(outer(left, far, owners), "ctx", siblings)
        grads = fold_tokens(outer(left, near, owners, given)).astype(jnp.bfloat16)
        plane = place // 2
        total = lax.dynamic_index_in_dim(grads, plane, 0, keepdims=False).astype(jnp.float32)
        for k in range(1, planes):
            part = lax.dynamic_index_in_dim(grads, plane ^ k, 0, keepdims=False)
            moves = [(c, (c // 2 ^ k) * 2 + c % 2) for c in range(chain)]
            total = total + lax.ppermute(part, "ctx", moves).astype(jnp.float32)
        return total.T

    output_grad = fold_rows(attended_rows, by_owner(attn_grad))
    query_grad = fold_rows(normed, by_owner(query_slopes))
    kv_grad = fold_rows(
        normed, jnp.concatenate([by_owner(key_slopes), by_owner(value_slopes)], axis=3)
    )
    kv_own = KV_WIDTH // chain
    key_grad, value_grad = kv_grad[:, :kv_own], kv_grad[:, kv_own:]

    normed_grad = matmul_back(
        jnp.concatenate([query_slopes, key_slopes, value_slopes], axis=1), in_full
    )
    scaled_one = normed_grad * gain_one
    hidden_grad = residual_grad + scale_one * (
        scaled_one - x * scale_one * scale_one * jnp.mean(scaled_one * x, axis=1, keepdims=True)
    )
    gain_one_part = jnp.sum(normed_grad * x * scale_one, axis=0)
    gain_grads = jnp.stack([gain_one_part, gain_two_part]).reshape(2, owners, rows)
    gain_grads = fold_tokens(jnp.transpose(gain_grads, (1, 0, 2)))
    step = 1
    while step < chain:
        gain_grads = gain_grads + lax.ppermute(gain_grads, "ctx", [(c, c ^ step) for c in range(chain)])
        step *= 2
    return (
        hidden_out.reshape(batches, length, width),
        hidden_grad.reshape(batches, length, width),
        gain_grads[0],
        query_grad,
        key_grad,
        value_grad,
        output_grad,
        gain_grads[1],
        gate_grad,
        up_grad,
        down_grad,
    )


def solution(mesh):
    tokens_spec = P("fs", "ctx", None)
    rows_spec = P("fs", None)
    block_spec = P("fs", "ctx")
    return jax.shard_map(
        on_device,
        mesh=mesh,
        in_specs=(
            tokens_spec,
            rows_spec,
            P("fs"),
            rows_spec,
            rows_spec,
            rows_spec,
            rows_spec,
            P("fs"),
            rows_spec,
            rows_spec,
            rows_spec,
            tokens_spec,
        ),
        out_specs=(
            tokens_spec,
            tokens_spec,
            P("fs"),
            block_spec,
            block_spec,
            block_spec,
            block_spec,
            P("fs"),
            block_spec,
            block_spec,
            block_spec,
        ),
        check_vma=False,
    )
```

```python
import functools
import math

import jax
import jax.numpy as jnp
from jax import lax
from jax.experimental import pallas as pl
from jax.experimental.pallas import tpu as pltpu
from jax.sharding import PartitionSpec as P

MODEL_WIDTH = 2560
QUERY_HEADS = 32
KEY_VALUE_HEADS = 8
HEAD_SIZE = 80
WINDOW = 1024
GROUPS = QUERY_HEADS // KEY_VALUE_HEADS
HALF = HEAD_SIZE // 2
KV_WIDTH = KEY_VALUE_HEADS * HEAD_SIZE
STRIP = 640
HALF_KV = KV_WIDTH // 2
SCALE = 1.0 / math.sqrt(HEAD_SIZE)

NORM_EPS = 1e-05
ROPE_THETA = 1000000.0
MASK_VALUE_FILL = -1e30
VMEM = 60 * 1024 * 1024
FEED_VMEM = 62 * 1024 * 1024
MESH = pl.DeviceIdType.MESH

NT = (((1,), (1,)), ((), ()))
TN = (((0,), (0,)), ((), ()))
NN = (((1,), (0,)), ((), ()))


def dot(left, right, dims):
    return lax.dot_general(left, right, dims, preferred_element_type=jnp.float32)


def params(**more):
    return pltpu.CompilerParams(vmem_limit_bytes=VMEM, **more)


def cost(flops, moved, exps=0):
    return pl.CostEstimate(flops=int(flops), bytes_accessed=int(moved), transcendentals=int(exps))


def turn(x, cosine, sine):
    width = x.shape[1]
    lane = lax.broadcasted_iota(jnp.int32, x.shape, 1) % HEAD_SIZE
    partner = jnp.where(
        lane < HALF, pltpu.roll(x, width - HALF, 1), pltpu.roll(x, HALF, 1)
    )
    return x * cosine + partner * sine


def toggled(me, k, count):
    found, bit = me, 1
    while bit < count:
        found = found + ((k // bit) % 2) * bit * (1 - 2 * ((me // bit) % 2))
        bit *= 2
    return found


def feed_kernel(
    peers, nt_ref, og_all, down_ref, gate_ref, up_ref,
    nt_all, gs_all, us_all, mid_all,
    nt_v, gs_v, us_v, mid_v, og_v, gate_v, up_v, down_v,
    load_sem, weight_sem, tile_sem, own_sem, keep_sem, nt_send, nt_recv,
):
    tokens = nt_ref.shape[0]
    inner = down_ref.shape[0]
    middle = tokens // 2
    square = peers == 4
    me = lax.axis_index("fs")
    bf16 = jnp.bfloat16

    def remote(src, dst, at, k):
        return pltpu.make_async_remote_copy(
            src_ref=src, dst_ref=dst, send_sem=nt_send.at[at], recv_sem=nt_recv.at[at],
            device_id={"fs": toggled(me, k, peers)}, device_id_type=MESH,
        )

    barrier = pltpu.get_barrier_semaphore()
    for k in range(1, peers):
        pl.semaphore_signal(barrier, inc=1, device_id={"fs": toggled(me, k, peers)}, device_id_type=MESH)
    pl.semaphore_wait(barrier, peers - 1)

    top, bottom = pl.ds(0, middle), pl.ds(middle, middle)
    reached = [1, 2] if square else list(range(1, peers))
    spread = {k: remote(nt_ref, nt_v.at[k], k, k) for k in reached}
    for k in reached:
        spread[k].start()
    if square:
        spread[3] = remote(nt_v.at[1, top], nt_v.at[3, top], 3, 2)
        spread[0] = remote(nt_v.at[2, bottom], nt_v.at[3, bottom], 0, 1)
    own = pltpu.make_async_copy(nt_ref, nt_v.at[0], own_sem.at[0])
    own.start()
    weights = [
        pltpu.make_async_copy(src, dst, weight_sem.at[i])
        for i, (src, dst) in enumerate(((gate_ref, gate_v), (up_ref, up_v), (down_ref, down_v)))
    ]
    for copy in weights:
        copy.start()

    def grads_of(k):
        return pltpu.make_async_copy(
            og_all.at[toggled(me, k, peers)], og_v.at[k % 2], load_sem.at[k % 2]
        )

    def keep(k):
        return pltpu.make_async_copy(nt_v.at[k], nt_all.at[k], keep_sem.at[k])

    grads_of(0).start()
    own.wait()
    for copy in weights:
        copy.wait()
    tile = 256 if inner % 256 == 0 else 128
    tiles = inner // tile

    def stores(k, at):
        return [
            pltpu.make_async_copy(src.at[:, at], dst.at[:, at], tile_sem.at[i, at.start // tile])
            for i, (src, dst) in enumerate(
                (
                    (gs_v, gs_all.at[k]),
                    (us_v, us_all.at[k]),
                    (mid_v, mid_all.at[toggled(me, k, peers)]),
                )
            )
        ]

    for k in range(peers):
        if square and k == 1:
            spread[1].wait_recv()
            spread[3].start()
            spread[2].wait_recv()
            spread[0].start()
        elif square and k == 3:
            spread[3].wait_recv()
            spread[0].wait_recv()
        elif not square and k > 0:
            spread[k].wait_recv()
        keep(k).start()
        grads_of(k).wait()
        if k + 1 < peers:
            grads_of(k + 1).start()

        def some(j, carry, k=k):
            at = pl.ds(pl.multiple_of(j * tile, tile), tile)
            gate = dot(nt_v[k], gate_v[:, at], NN)
            up = dot(nt_v[k], up_v[:, at], NN)
            grad = dot(og_v[k % 2], down_v[at, :], NT)
            sig = 1.0 / (1.0 + jnp.exp(-gate))
            silu = gate * sig
            if k > 0:
                for copy in stores(k - 1, at):
                    copy.wait()
            mid_v[:, at] = (silu * up).astype(bf16)
            gs_v[:, at] = (grad * up * sig * (1.0 + gate * (1.0 - sig))).astype(bf16)
            us_v[:, at] = (grad * silu).astype(bf16)
            for copy in stores(k, at):
                copy.start()
            return carry

        lax.fori_loop(0, tiles, some, 0)

    def settle(j, carry):
        at = pl.ds(pl.multiple_of(j * tile, tile), tile)
        for copy in stores(peers - 1, at):
            copy.wait()
        return carry

    lax.fori_loop(0, tiles, settle, 0)
    for k in range(peers):
        keep(k).wait()
    for copy in spread.values():
        copy.wait_send()


def feed(peers, nt, og_all, down, gate, up):
    tokens, width = nt.shape
    inner = down.shape[0]
    bf = jnp.bfloat16
    S = jax.ShapeDtypeStruct
    any_ = pl.BlockSpec(memory_space=pl.ANY)
    DMA = pltpu.SemaphoreType.DMA
    inner_shape = S((peers, tokens, inner), bf)
    return pl.pallas_call(
        functools.partial(feed_kernel, peers),
        in_specs=[any_] * 5,
        out_specs=[any_] * 4,
        out_shape=[S((peers, tokens, width), bf), inner_shape, inner_shape, inner_shape],
        scratch_shapes=[
            pltpu.VMEM((peers, tokens, width), bf),
            pltpu.VMEM((tokens, inner), bf), pltpu.VMEM((tokens, inner), bf), pltpu.VMEM((tokens, inner), bf),
            pltpu.VMEM((2, tokens, width), bf),
            pltpu.VMEM((width, inner), bf), pltpu.VMEM((width, inner), bf), pltpu.VMEM((inner, width), bf),
            DMA((2,)), DMA((3,)), DMA((3, 16)), DMA((1,)), DMA((peers,)),
            DMA((peers,)), DMA((peers,)),
        ],
        compiler_params=pltpu.CompilerParams(vmem_limit_bytes=FEED_VMEM, collective_id=1, has_side_effects=True),
        cost_estimate=cost(6 * peers * tokens * width * inner, 20 * width * inner, peers * tokens * inner),
    )(nt, og_all, down, gate, up)


def feed_back_kernel(
    peers, gs_all, us_all, mid_all, down_ref, gate_ref, up_ref,
    dn_own, dn_in, out_part,
    gs_v, us_v, io, relay, out_v, gate_v, up_v, down_v,
    load_sem, weight_sem, out_sem, own_sem, dn_send, dn_recv,
):
    tokens, inner = gs_v.shape[1:]
    width = gate_ref.shape[0]
    middle = tokens // 2
    square = peers == 4
    me = lax.axis_index("fs")
    bf16 = jnp.bfloat16

    def remote(src, dst, at, k):
        return pltpu.make_async_remote_copy(
            src_ref=src, dst_ref=dst, send_sem=dn_send.at[at], recv_sem=dn_recv.at[at],
            device_id={"fs": toggled(me, k, peers)}, device_id_type=MESH,
        )

    barrier = pltpu.get_barrier_semaphore()
    for k in range(1, peers):
        pl.semaphore_signal(barrier, inc=1, device_id={"fs": toggled(me, k, peers)}, device_id_type=MESH)
    pl.semaphore_wait(barrier, peers - 1)
    top, bottom = pl.ds(0, middle), pl.ds(middle, middle)

    def returns(k):
        if square and k == 3:
            return (remote(io.at[3, top], relay.at[0], 3, 1), remote(io.at[3, bottom], relay.at[1], 0, 2))
        return (remote(io.at[k], dn_in.at[k - 1], k, k),)

    order = [peers - 1, 0] + list(range(peers - 2, 0, -1))
    weights = [
        pltpu.make_async_copy(src, dst, weight_sem.at[i])
        for i, (src, dst) in enumerate(((gate_ref, gate_v), (up_ref, up_v), (down_ref, down_v)))
    ]
    for copy in weights:
        copy.start()

    def slopes_of(turn):
        k, slot = order[turn], turn % 2
        return [
            pltpu.make_async_copy(src.at[k], dst.at[slot], load_sem.at[i, slot])
            for i, (src, dst) in enumerate(((gs_all, gs_v), (us_all, us_v)))
        ]

    def units_of(turn):
        slab, slot = toggled(me, order[turn], peers), turn % 2
        return pltpu.make_async_copy(mid_all.at[slab], gs_v.at[slot], load_sem.at[0, slot])

    for copy in slopes_of(0):
        copy.start()
    wide = 256
    strips = width // wide
    weights[0].wait()
    weights[1].wait()
    for turn, k in enumerate(order):
        slot = turn % 2
        for copy in slopes_of(turn):
            copy.wait()
        if turn + 1 < peers:
            for copy in slopes_of(turn + 1):
                copy.start()
        if square and k == 2:
            returns(3)[0].wait_recv()
        if square and k == 1:
            returns(3)[1].wait_recv()

        def more(j, carry, k=k, slot=slot):
            at = pl.ds(pl.multiple_of(j * wide, wide), wide)
            part = dot(gs_v[slot], gate_v[at, :], NT) + dot(us_v[slot], up_v[at, :], NT)
            if square and k == 2:
                io[k, top, at] = (part[:middle] + relay[0, :, at].astype(jnp.float32)).astype(bf16)
                io[k, bottom, at] = part[middle:].astype(bf16)
            elif square and k == 1:
                io[k, top, at] = part[:middle].astype(bf16)
                io[k, bottom, at] = (part[middle:] + relay[1, :, at].astype(jnp.float32)).astype(bf16)
            else:
                io[k, :, at] = part.astype(bf16)
            return carry

        lax.fori_loop(0, strips, more, 0)
        if k == 0:
            pltpu.make_async_copy(io.at[0], dn_own, own_sem.at[0]).start()
        else:
            for copy in returns(k):
                copy.start()

    weights[2].wait()
    units_of(0).start()
    for turn, k in enumerate(order):
        slot, slab = turn % 2, toggled(me, k, peers)
        units_of(turn).wait()
        if turn + 1 < peers:
            units_of(turn + 1).start()

        def out_copy(j, slab=slab):
            at = pl.ds(pl.multiple_of(j * wide, wide), wide)
            return pltpu.make_async_copy(out_v.at[j % 2], out_part.at[slab, :, at], out_sem.at[j % 2])

        def last(j, carry, slot=slot, out_copy=out_copy):
            at = pl.ds(pl.multiple_of(j * wide, wide), wide)
            found = dot(gs_v[slot], down_v[:, at], NN).astype(bf16)

            @pl.when(j >= 2)
            def _():
                out_copy(j - 2).wait()

            out_v[j % 2] = found
            out_copy(j).start()
            return carry

        lax.fori_loop(0, strips, last, 0)
        out_copy(strips - 2).wait()
        out_copy(strips - 1).wait()

    pltpu.make_async_copy(io.at[0], dn_own, own_sem.at[0]).wait()
    for k in range(1, peers):
        for copy in returns(k):
            copy.wait_send()
            if not (square and k == 3):
                copy.wait_recv()


def feed_back(peers, gs, us, mid, down, gate, up):
    tokens, inner = gs.shape[1:]
    width = gate.shape[0]
    bf = jnp.bfloat16
    S = jax.ShapeDtypeStruct
    any_ = pl.BlockSpec(memory_space=pl.ANY)
    DMA = pltpu.SemaphoreType.DMA
    halves = 2 if peers == 4 else peers - 1
    return pl.pallas_call(
        functools.partial(feed_back_kernel, peers),
        in_specs=[any_] * 6,
        out_specs=[any_] * 3,
        out_shape=[S((tokens, width), bf), S((halves, tokens, width), bf), S((peers, tokens, width), bf)],
        scratch_shapes=[
            pltpu.VMEM((2, tokens, inner), bf), pltpu.VMEM((2, tokens, inner), bf),
            pltpu.VMEM((peers, tokens, width), bf),
            pltpu.VMEM((2, tokens // 2, width), bf),
            pltpu.VMEM((2, tokens, 256), bf),
            pltpu.VMEM((width, inner), bf), pltpu.VMEM((width, inner), bf), pltpu.VMEM((inner, width), bf),
            DMA((2, 2)), DMA((3,)), DMA((2,)), DMA((1,)), DMA((peers,)), DMA((peers,)),
        ],
        compiler_params=pltpu.CompilerParams(vmem_limit_bytes=FEED_VMEM, collective_id=4, has_side_effects=True),
        cost_estimate=cost(6 * peers * tokens * width * inner, 20 * width * inner),
    )(gs, us, mid, down, gate, up)


def gate_fold_kernel(nt_ref, gs_ref, us_ref, gate_ref, up_ref):
    peers, tokens, block = nt_ref.shape
    inner = gs_ref.shape[2]
    total = peers * tokens
    turned = jnp.transpose(nt_ref[...].reshape(total, block))
    gate_ref[...] = dot(turned, gs_ref[...].reshape(total, inner), NN).astype(jnp.bfloat16)
    up_ref[...] = dot(turned, us_ref[...].reshape(total, inner), NN).astype(jnp.bfloat16)


def gate_fold(nt_all, gs, us):
    peers, tokens, width = nt_all.shape
    inner = gs.shape[2]
    block = 512
    fixed = pl.BlockSpec((peers, tokens, inner), lambda j: (0, 0, 0), pipeline_mode=pl.Buffered(1))
    return pl.pallas_call(
        gate_fold_kernel,
        grid=(width // block,),
        in_specs=[pl.BlockSpec((peers, tokens, block), lambda j: (0, 0, j)), fixed, fixed],
        out_specs=[pl.BlockSpec((block, inner), lambda j: (j, 0))] * 2,
        out_shape=[jax.ShapeDtypeStruct((width, inner), jnp.bfloat16)] * 2,
        compiler_params=params(),
        cost_estimate=cost(4 * peers * tokens * width * inner, 2 * (nt_all.size + 3 * gs.size)),
    )(nt_all, gs, us)


def down_fold_kernel(og_ref, mid_ref, out_ref):
    peers, tokens, tile = mid_ref.shape
    owned = out_ref.shape[2]
    turned = jnp.transpose(mid_ref[...].reshape(peers * tokens, tile))
    wide = og_ref.shape[2]
    acc = dot(turned, og_ref[...].reshape(peers * tokens, wide), NN).astype(jnp.bfloat16)
    for c in range(out_ref.shape[0]):
        out_ref[c] = acc[:, c * owned : (c + 1) * owned]


def down_fold(og_all, mid_all, chain):
    peers, tokens, width = og_all.shape
    inner = mid_all.shape[2]
    tile = 256 if inner % 256 == 0 else 128
    owned = width // chain
    wide = 1280
    return pl.pallas_call(
        down_fold_kernel,
        grid=(width // wide, inner // tile),
        in_specs=[
            pl.BlockSpec((peers, tokens, wide), lambda i, j: (0, 0, i)),
            pl.BlockSpec((peers, tokens, tile), lambda i, j: (0, 0, j)),
        ],
        out_specs=pl.BlockSpec((wide // owned, tile, owned), lambda i, j: (i, j, 0)),
        out_shape=jax.ShapeDtypeStruct((chain, inner, owned), jnp.bfloat16),
        compiler_params=params(),
        cost_estimate=cost(2 * peers * tokens * width * inner, 2 * (og_all.size + 3 * mid_all.size)),
    )(og_all, mid_all)


def front_kernel(peers, chain, count, batches, *refs):
    (hid, gains, q_w, k_w, v_w, o_w, gate_w, up_w, og, cos_ref, sin_ref, low_ref) = refs[:12]
    (w_in, o_full, gate_part, up_part, og_all, normed_o, q_o, line_o, sib_o, att_o, lse_o, gain_o) = refs[12:24]
    (w_v, nt_v, nt_b, q_v, att_v, line_v, sib_v, gains_v) = refs[24:32]
    (own_sem, out_sem, gain_s, gain_r, qkv_s, qkv_r, twin_s, twin_r, back_s, back_r,
     og_s, og_r, hop_s, hop_r, kin_s, kin_r) = refs[32:]
    tokens, width = nt_v.shape
    rows = q_w.shape[0]
    inner = gate_part.shape[1]
    length = tokens // batches
    slots = line_v.shape[0]
    window = count * length
    square = peers == 4
    bf16, f32 = jnp.bfloat16, jnp.float32
    me, place = lax.axis_index("fs"), lax.axis_index("ctx")
    core, plane = place % 2, place // 2
    parity = plane % 2
    twin = place + 1 - 2 * core
    partner = place + 2 - 4 * parity
    deep = place >= 2
    ahead = place + 2 < chain

    def send(src, dst, send_sem, recv_sem, target):
        return pltpu.make_async_remote_copy(
            src_ref=src, dst_ref=dst, send_sem=send_sem, recv_sem=recv_sem,
            device_id=target, device_id_type=MESH,
        )

    def owner(k):
        return toggled(me, k, peers)

    def along(k):
        return {"fs": owner(k)}

    for i in range(1, slots):

        @pl.when(plane < i)
        def _(i=i):
            line_v[i] = jnp.zeros(line_v.shape[1:], bf16)
            sib_v[i] = jnp.zeros(line_v.shape[1:], bf16)

    barrier = pltpu.get_barrier_semaphore()
    for k in range(1, peers):
        pl.semaphore_signal(barrier, inc=1, device_id=along(k), device_id_type=MESH)
    pl.semaphore_signal(barrier, inc=1, device_id={"ctx": twin}, device_id_type=MESH)

    @pl.when(deep)
    def _():
        pl.semaphore_signal(barrier, inc=1, device_id={"ctx": place - 2}, device_id_type=MESH)

    @pl.when(ahead)
    def _():
        pl.semaphore_signal(barrier, inc=1, device_id={"ctx": place + 2}, device_id_type=MESH)

    planes = chain // 2
    behind = (plane + planes - 1) // planes
    before = (2 * planes - 2 - plane) // planes
    pl.semaphore_wait(barrier, peers + behind + before)

    share = rows // 2
    half = share // 2
    mats = ((q_w, pl.ds(0, width)), (k_w, pl.ds(width, KV_WIDTH)), (v_w, pl.ds(width + KV_WIDTH, KV_WIDTH)))

    def block(k, at, size):
        return pl.ds(pl.multiple_of(owner(k) * rows + core * share + at, 16), size)

    def first_hop(k, m):
        src, cols = mats[m]
        mine = pl.ds(pl.multiple_of(core * share, 16), share)
        return send(src.at[mine, :], w_v.at[block(0, 0, share), cols], qkv_s.at[k, m], qkv_r.at[k, m], along(k))

    def relay(part, m):
        source, target = (1, 2) if part == 3 else (2, 1)
        where = w_v.at[block(source, 0 if part == 3 else half, half), mats[m][1]]
        return send(where, where, qkv_s.at[part, m], qkv_r.at[part, m], along(target))

    def to_twin(part, m):
        if square and part in (0, 3):
            rows_at = block(3, 0 if part == 3 else half, half)
        else:
            rows_at = block(part, 0, share)
        where = w_v.at[rows_at, mats[m][1]]
        return send(where, where, twin_s.at[part, m], twin_r.at[part, m], {"ctx": twin})

    reached = [1, 2] if square else list(range(1, peers))
    for k in reached:
        for m in range(3):
            first_hop(k, m).start()
    own_rows = pl.ds(pl.multiple_of(me * rows, 16), rows)
    own_loads = [
        pltpu.make_async_copy(src, w_v.at[own_rows, cols], own_sem.at[i])
        for i, (src, cols) in enumerate(mats)
    ]
    for copy in own_loads:
        copy.start()
    gain_moves = [send(gains, gains_v.at[me], gain_s.at[k], gain_r.at[k], along(k)) for k in range(1, peers)]
    for copy in gain_moves:
        copy.start()
    gains_v[me] = gains[...]
    for copy in gain_moves:
        copy.wait_recv()
    whole_gain = jnp.concatenate([gains_v[f] for f in range(peers)], axis=1)
    gain_o[...] = whole_gain

    chunk = 64

    def norm(i, carry):
        at = pl.ds(pl.multiple_of(i * chunk, chunk), chunk)
        x = hid[at, :].astype(f32)
        scale = lax.rsqrt(jnp.mean(x * x, axis=1, keepdims=True) + NORM_EPS)
        normed = (x * scale * whole_gain[0:1]).astype(bf16)
        nt_v[at, :] = normed
        for f in range(peers):
            nt_b[f, at, :] = normed[:, f * rows : (f + 1) * rows]
        return carry

    lax.fori_loop(0, tokens // chunk, norm, 0)
    normed_out = pltpu.make_async_copy(nt_v, normed_o, out_sem.at[0])
    normed_out.start()

    quarter = rows // 4
    sources = (o_w, gate_w, up_w)
    fulls = (o_full, gate_part, up_part)

    def region(m, k, c, p):
        return fulls[m].at[pl.ds(pl.multiple_of(owner(k) * rows + (c + 2 * p) * quarter, 16), quarter), :]

    def back_first(m, k):
        at = pl.ds(pl.multiple_of((core + 2 * parity) * quarter, 16), quarter)
        if m == 0:
            src = o_w.at[at, :]
        else:
            src = sources[m].at[at, pl.ds(pl.multiple_of(owner(k) * inner, 128), inner)]
        return send(src, region(m, 0, core, parity), back_s.at[0, m, k], back_r.at[0, m, k], along(k))

    def back_plane(m, k):
        where = region(m, k, core, parity)
        return send(where, where, back_s.at[1, m, k], back_r.at[1, m, k], {"ctx": partner})

    def back_twin(m, k, p, stage):
        where = region(m, k, core, p)
        return send(where, where, back_s.at[stage, m, k], back_r.at[stage, m, k], {"ctx": twin})

    others = range(1, peers)

    def spread_first(which):
        for m in which:
            for k in others:
                back_first(m, k).start()

    def spread_second(which):
        for m in which:
            for k in others:
                back_first(m, k).wait_recv()
                back_plane(m, k).start()
                back_twin(m, k, parity, 2).start()

    def spread_third(which):
        for m in which:
            for k in others:
                back_plane(m, k).wait_recv()
                back_twin(m, k, 1 - parity, 3).start()

    def og_hop(k):
        return send(og, og_all.at[me], og_s.at[k], og_r.at[k], along(k))

    middle = tokens // 2

    def og_relay(part):
        source, target = (1, 2) if part == 3 else (2, 1)
        where = og_all.at[owner(source), pl.ds(0 if part == 3 else middle, middle), :]
        return send(where, where, og_s.at[part], og_r.at[part], along(target))

    wide = STRIP
    tiles = w_v.shape[1] // wide

    def project(acc, bounce):
        def through(src, dst, sem):
            shape = src.shape
            there = bounce.at[pl.ds(0, shape[0]), pl.ds(0, shape[1])]
            copy = pltpu.make_async_copy(src, there, sem.at[3])
            copy.start()
            copy.wait()
            copy = pltpu.make_async_copy(there, dst, sem.at[4])
            copy.start()
            copy.wait()

        through(og, og_all.at[me], own_sem)
        through(o_w, o_full.at[own_rows, :], own_sem)
        mine = pl.ds(pl.multiple_of(me * inner, 128), inner)
        through(gate_w.at[:, mine], gate_part.at[own_rows, :], own_sem)
        through(up_w.at[:, mine], up_part.at[own_rows, :], own_sem)
        for copy in own_loads:
            copy.wait()

        def add(k):
            rows_at = pl.ds(pl.multiple_of(owner(k) * rows, 16), rows)

            def one(j, carry):
                at = pl.ds(pl.multiple_of(j * wide, wide), wide)
                part = dot(nt_b[owner(k)], w_v[rows_at, at], NN)
                acc[:, at] = part if k == 0 else acc[:, at] + part
                return carry

            lax.fori_loop(0, tiles, one, 0)

        add(0)
        if square:
            for k, part in ((1, 3), (2, 0)):
                for m in range(3):
                    first_hop(k, m).wait_recv()
                for m in range(3):
                    relay(part, m).start()
                    to_twin(k, m).start()
                if k == 2:
                    spread_first([0])
                for m in range(3):
                    to_twin(k, m).wait_recv()
                add(k)
            for part in (3, 0):
                for m in range(3):
                    relay(part, m).wait_recv()
                    to_twin(part, m).start()
            spread_first([1, 2])
            for k in (1, 2):
                og_hop(k).start()
            for part in (3, 0):
                for m in range(3):
                    to_twin(part, m).wait_recv()
            add(3)
        else:
            for k in others:
                for m in range(3):
                    first_hop(k, m).wait_recv()
                    to_twin(k, m).start()
                for m in range(3):
                    to_twin(k, m).wait_recv()
                add(k)
            spread_first([0, 1, 2])
            for k in others:
                og_hop(k).start()

        line_v[0, 0] = turn(acc[:, width : width + KV_WIDTH], cos_ref[...], sin_ref[...]).astype(bf16)
        line_v[0, 1] = acc[:, width + KV_WIDTH :].astype(bf16)

        @pl.when(ahead)
        def _():
            hop(0).start()

        kin(0).start()

        def finish(j, carry):
            at = pl.ds(pl.multiple_of(j * wide, wide), wide)
            q_v[:, at] = turn(acc[:, at], cos_ref[...], sin_ref[...]).astype(bf16)
            return carry

        lax.fori_loop(0, width // wide, finish, 0)

    def hop(i):
        return send(line_v.at[i], line_v.at[i + 1], hop_s.at[i], hop_r.at[i], {"ctx": place + 2})

    def kin(i):
        return send(line_v.at[i], sib_v.at[i], kin_s.at[i], kin_r.at[i], {"ctx": twin})

    pl.run_scoped(project, pltpu.VMEM((tokens, w_v.shape[1]), f32), pltpu.VMEM((rows, width), bf16))

    w_out = pltpu.make_async_copy(w_v, w_in, out_sem.at[1])
    w_out.start()
    q_out = pltpu.make_async_copy(q_v, q_o, out_sem.at[2])
    q_out.start()
    spread_second([0])
    for i in range(1, slots):

        @pl.when(plane >= i)
        def _(i=i):
            hop(i - 1).wait_recv()
            kin(i).start()

        if i + 1 < slots:

            @pl.when((plane >= i) & ahead)
            def _(i=i):
                hop(i).start()

    kin(0).wait_recv()
    for i in range(1, slots):

        @pl.when(plane >= i)
        def _(i=i):
            kin(i).wait_recv()

    line_out = pltpu.make_async_copy(line_v, line_o, out_sem.at[3])
    line_out.start()
    sib_out = pltpu.make_async_copy(sib_v, sib_o, out_sem.at[4])
    sib_out.start()

    def attention(keys, values, bias):
        for b in range(batches):
            here = pl.ds(b * length, length)
            for back in range(count):
                at_rows = pl.ds((count - 1 - back) * length, length)
                for kind, target in ((0, keys), (1, values)):
                    if back % 2 == 0:
                        found = line_v[back // 2, kind, here, :]
                    else:
                        found = sib_v[(back + 1) // 2 - core, kind, here, :]
                    for head in range(KEY_VALUE_HEADS):
                        target[head, at_rows, :] = found[:, head * HEAD_SIZE : (head + 1) * HEAD_SIZE]
            key_place = (place - count + 1) * length + lax.broadcasted_iota(jnp.int32, (length, window), 1)
            query_place = place * length + lax.broadcasted_iota(jnp.int32, (length, window), 0)
            seen = (key_place >= low_ref[b]) & (key_place <= query_place)
            bias[...] = jnp.where(seen, 0.0, MASK_VALUE_FILL)

            def pair_of_heads(pair, carry, b=b, here=here):
                cols = pl.ds(pl.multiple_of(pair * STRIP, STRIP), STRIP)
                strip = q_v[here, cols]
                mixed, sums = [], []
                for side in range(2):
                    key, value = keys[2 * pair + side], values[2 * pair + side]
                    for group in range(GROUPS):
                        at = (side * GROUPS + group) * HEAD_SIZE
                        scores = dot(strip[:, at : at + HEAD_SIZE], key, NT) * SCALE + bias[...]
                        peak = jnp.max(scores, axis=1, keepdims=True)
                        weights = jnp.exp(scores - peak)
                        total = jnp.sum(weights, axis=1, keepdims=True)
                        mixed.append(dot(weights.astype(bf16), value, NN) / total)
                        sums.append(peak + jnp.log(total))
                att_v[here, cols] = jnp.concatenate(mixed, axis=1).astype(bf16)
                spare = jnp.zeros((length, 128 - 2 * GROUPS), f32)
                turned = jnp.transpose(jnp.concatenate(sums + [spare], axis=1))
                lse_o[b, pair] = turned[: 2 * GROUPS]
                return carry

            lax.fori_loop(0, KEY_VALUE_HEADS // 2, pair_of_heads, 0)
            if b == 0:
                spread_third([0])
                spread_second([1, 2])
                if square:
                    for k, part in ((1, 3), (2, 0)):
                        og_hop(k).wait_recv()
                        og_relay(part).start()

    pl.run_scoped(
        attention,
        pltpu.VMEM((KEY_VALUE_HEADS, window, HEAD_SIZE), bf16),
        pltpu.VMEM((KEY_VALUE_HEADS, window, HEAD_SIZE), bf16),
        pltpu.VMEM((length, window), f32),
    )
    att_out = pltpu.make_async_copy(att_v, att_o, out_sem.at[5])
    att_out.start()
    spread_third([1, 2])

    for copy in (normed_out, w_out, q_out, line_out, sib_out, att_out):
        copy.wait()
    for copy in gain_moves:
        copy.wait_send()
    for m in range(3):
        for k in reached:
            first_hop(k, m).wait_send()
            to_twin(k, m).wait_send()
        if square:
            for part in (3, 0):
                relay(part, m).wait_send()
                to_twin(part, m).wait_send()
    for k in reached:
        og_hop(k).wait_send()
        if not square:
            og_hop(k).wait_recv()
    if square:
        for part in (3, 0):
            og_relay(part).wait()
    for m in range(3):
        for k in others:
            back_first(m, k).wait_send()
            back_plane(m, k).wait_send()
            back_twin(m, k, parity, 2).wait()
            back_twin(m, k, 1 - parity, 3).wait()
    kin(0).wait_send()

    @pl.when(ahead)
    def _():
        hop(0).wait_send()

    for i in range(1, slots):

        @pl.when(plane >= i)
        def _(i=i):
            kin(i).wait_send()

        if i + 1 < slots:

            @pl.when((plane >= i) & ahead)
            def _(i=i):
                hop(i).wait_send()


def front(peers, chain, count, hidden, gains, weights, og, cosine, sine, low):
    batches, length, _ = low.shape
    tokens, width = hidden.shape
    rows = weights[0].shape[0]
    inner = weights[4].shape[1] // peers
    slots = (count - 1) // 2 + 1
    bf = jnp.bfloat16
    S = jax.ShapeDtypeStruct
    DMA = pltpu.SemaphoreType.DMA
    far = pl.BlockSpec(memory_space=pl.ANY)
    near = pl.BlockSpec(memory_space=pltpu.VMEM)
    whole = S((tokens, width), bf)
    line = (slots, 2, tokens, KV_WIDTH)
    return pl.pallas_call(
        functools.partial(front_kernel, peers, chain, count, batches),
        in_specs=[near, near] + [far] * 7 + [near] * 3,
        out_specs=[far] * 10 + [near, near],
        out_shape=[
            S((width, width + 2 * KV_WIDTH), bf),
            S((width, width), bf),
            S((width, inner), bf),
            S((width, inner), bf),
            S((peers, tokens, width), bf),
            whole,
            whole,
            S(line, bf),
            S(line, bf),
            whole,
            S((batches, KEY_VALUE_HEADS // 2, 2 * GROUPS, length), jnp.float32),
            S((8, width), jnp.float32),
        ],
        scratch_shapes=[
            pltpu.VMEM((width, width + 2 * KV_WIDTH), bf),
            pltpu.VMEM((tokens, width), bf),
            pltpu.VMEM((peers, tokens, rows), bf),
            pltpu.VMEM((tokens, width), bf),
            pltpu.VMEM((tokens, width), bf),
            pltpu.VMEM(line, bf),
            pltpu.VMEM(line, bf),
            pltpu.VMEM((peers, 8, rows), jnp.float32),
            DMA((5,)), DMA((6,)), DMA((peers,)), DMA((peers,)),
            DMA((peers, 3)), DMA((peers, 3)), DMA((peers, 3)), DMA((peers, 3)),
            DMA((4, 3, peers)), DMA((4, 3, peers)), DMA((peers,)), DMA((peers,)),
            DMA((slots,)), DMA((slots,)), DMA((slots,)), DMA((slots,)),
        ],
        compiler_params=pltpu.CompilerParams(
            vmem_limit_bytes=FEED_VMEM, collective_id=2, has_side_effects=True
        ),
        cost_estimate=cost(2 * tokens * width * 3840 * 10, 200 * tokens * width, QUERY_HEADS * tokens * count * length),
    )(hidden, gains, *weights, og, cosine, sine, low)


def back_kernel(peers, chain, count, batches, *refs):
    (normed, attended, d_attn, d_att, q_v, lse, low, cos_ref, sin_ref, scale, gain_two, line, sib, hid, w_in) = refs[:15]
    (slope_out, grad_o, grad_q, grad_kv, gain_out, far_o, far_q, far_kv, fs_o, fs_q, fs_kv, parts, odd_in, hop_in) = refs[15:29]
    (nb_o, z_o, z_q, z_kv, slopes_t, load_v, part_v, d_v, block_v, gain_v, gain_fs, gain_all) = refs[29:41]
    (far_s, far_r, fs_s, fs_r, zs_s, zs_r, load_sem, fsl_sem, part_sem, odd_s, odd_r, hop_s, hop_r, sum_sem, block_sem, gf_s, gf_r, ga_s, ga_r) = refs[41:]
    tokens, width = normed.shape
    rows = width // peers
    planes = chain // 2
    length = tokens // batches
    window = count * length
    reach = (count - 1) // 2
    bf16, f32 = jnp.bfloat16, jnp.float32
    me, place = lax.axis_index("fs"), lax.axis_index("ctx")
    core, plane = place % 2, place // 2
    twin = place + 1 - 2 * core
    deep, ahead = place >= 2, place + 2 < chain

    def send(src, dst, send_sem, recv_sem, target):
        return pltpu.make_async_remote_copy(
            src_ref=src, dst_ref=dst, send_sem=send_sem, recv_sem=recv_sem,
            device_id=target, device_id_type=MESH,
        )

    barrier = pltpu.get_barrier_semaphore()
    for k in range(1, peers):
        pl.semaphore_signal(barrier, inc=1, device_id={"fs": toggled(me, k, peers)}, device_id_type=MESH)
    for k in range(1, chain):
        pl.semaphore_signal(barrier, inc=1, device_id={"ctx": toggled(place, k, chain)}, device_id_type=MESH)
    pl.semaphore_wait(barrier, peers + chain - 2)

    kinds = {
        "o": (0, attended, far_o, fs_o, nb_o, z_o, grad_o),
        "kv": (2, normed, far_kv, fs_kv, nb_o, z_kv, grad_kv),
    }

    def own_of(x):
        return kinds[x][2].shape[1]

    def turn_slopes(x):
        own = own_of(x)
        for p in range(planes):
            if x == "kv":
                half = own // 2
                sides = []
                for c in range(2):
                    at = (2 * p + c) * half
                    sides.append(
                        jnp.concatenate(
                            [
                                d_v[:, width + at : width + at + half],
                                d_v[:, width + KV_WIDTH + at : width + KV_WIDTH + at + half],
                            ],
                            axis=1,
                        )
                    )
            else:
                sides = [d_v[:, (2 * p + c) * own : (2 * p + c + 1) * own] for c in range(2)]
            first, second = (jnp.transpose(side.astype(f32)) for side in sides)
            slopes_t[0, p, :own] = jnp.where(core == 0, first, second).astype(bf16)
            slopes_t[1, p, :own] = jnp.where(core == 0, second, first).astype(bf16)

    def far_copy(x, t):
        i, _, far, _, nb, _, _ = kinds[x]
        return send(nb.at[t, pl.ds(0, own_of(x))], far.at[t], far_s.at[i, t], far_r.at[i, t], {"ctx": twin})

    def far_phase(x):
        _, left, _, _, nb, _, _ = kinds[x]
        own = own_of(x)
        for f in range(peers):

            def one(p, carry, f=f):
                t = f * planes + p
                part = dot(slopes_t[1, p, :own], left[:, f * rows : (f + 1) * rows], NN)
                nb[t, :own] = part.astype(bf16)
                far_copy(x, t).start()
                return carry

            lax.fori_loop(0, planes, one, 0)

    def fs_copy(x, f, p):
        i, _, _, fs, nb, _, _ = kinds[x]
        src = nb.at[f * planes + p, pl.ds(0, own_of(x))]
        return send(src, fs.at[me, p], fs_s.at[i, f, p], fs_r.at[i, me, p], {"fs": f})

    def fs_arrival(x, s, p):
        i, _, _, fs, nb, _, _ = kinds[x]
        src = nb.at[p, pl.ds(0, own_of(x))]
        return send(src, fs.at[s, p], fs_s.at[i, s, p], fs_r.at[i, s, p], {"fs": s})

    def near_phase(x):
        _, left, far, _, nb, _, _ = kinds[x]
        own = own_of(x)
        total = peers * planes

        def load(t):
            slot = t % 2
            return pltpu.make_async_copy(far.at[t], load_v.at[slot, pl.ds(0, own)], load_sem.at[slot])

        far_copy(x, 0).wait_recv()
        load(0).start()
        for f in range(peers):

            def one(p, carry, f=f):
                t = f * planes + p

                @pl.when(t + 1 < total)
                def _():
                    far_copy(x, t + 1).wait_recv()
                    load(t + 1).start()

                part = dot(slopes_t[0, p, :own], left[:, f * rows : (f + 1) * rows], NN)
                load(t).wait()
                far_copy(x, t).wait_send()
                nb[t, :own] = (part + load_v[t % 2, :own].astype(f32)).astype(bf16)

                @pl.when(f != me)
                def _():
                    fs_copy(x, f, p).start()

                return carry

            lax.fori_loop(0, planes, one, 0)

    def z_copy(x, p):
        i, _, _, _, nb, z, _ = kinds[x]
        src = nb.at[me * planes + p, pl.ds(0, own_of(x))]
        return send(src, z.at[plane], zs_s.at[i, p], zs_r.at[i, plane], {"ctx": 2 * p + core})

    def z_arrival(x, p):
        i, _, _, _, nb, z, _ = kinds[x]
        src = nb.at[me * planes + p, pl.ds(0, own_of(x))]
        return send(src, z.at[p], zs_s.at[i, p], zs_r.at[i, p], {"ctx": 2 * p + core})

    def z_phase(x, fs_load):
        _, _, _, fs, nb, _, tot = kinds[x]
        own = own_of(x)

        def one(p, carry):
            for s in range(peers):
                there = pltpu.make_async_copy(fs.at[s, p], fs_load.at[s, pl.ds(0, own)], fsl_sem.at[s])

                @pl.when(s != me)
                def _(s=s, there=there):
                    fs_arrival(x, s, p).wait_recv()
                    there.start()

            fs_load[me, :own] = nb[me * planes + p, :own]
            for s in range(peers):
                there = pltpu.make_async_copy(fs.at[s, p], fs_load.at[s, pl.ds(0, own)], fsl_sem.at[s])

                @pl.when(s != me)
                def _(there=there):
                    there.wait()

            total = fs_load[0, :own].astype(f32)
            for s in range(1, peers):
                total = total + fs_load[s, :own].astype(f32)

            @pl.when(p == plane)
            def _():
                tot[...] = total

            @pl.when(p != plane)
            def _():
                nb[me * planes + p, :own] = total.astype(bf16)
                z_copy(x, p).start()

            return carry

        lax.fori_loop(0, planes, one, 0)

    def finish(x):
        _, _, _, _, _, z, tot = kinds[x]
        total = tot[...]
        for p in range(planes):

            @pl.when(p != plane)
            def _(p=p):
                z_arrival(x, p).wait_recv()

            @pl.when(p == plane)
            def _(p=p):
                z[p] = jnp.zeros(z.shape[1:], bf16)

            total = total + z[p].astype(f32)
        tot[...] = total

    def settle(x):
        for p in range(planes):
            for f in range(peers):

                @pl.when(f != me)
                def _(f=f, p=p):
                    fs_copy(x, f, p).wait_send()

            @pl.when(p != plane)
            def _(p=p):
                z_copy(x, p).wait_send()

    def part_store(b):
        return pltpu.make_async_copy(part_v, parts.at[:, :, pl.ds(b * length, length)], part_sem.at[0])

    def attention(keys, values, bias, key_sums, value_sums):
        def one_batch(b):
            here = pl.ds(b * length, length)

            def fetch(back):
                if back % 2 == 0:
                    src = line.at[back // 2, :, here]
                else:
                    src = sib.at[(back + 1) // 2 - core, :, here]
                return pltpu.make_async_copy(src, block_v.at[back % 2], block_sem.at[back % 2])

            fetch(0).start()
            for back in range(count):
                if back + 1 < count:
                    fetch(back + 1).start()
                fetch(back).wait()
                at_rows = pl.ds((count - 1 - back) * length, length)
                for kind, target in ((0, keys), (1, values)):
                    found = block_v[back % 2, kind]
                    for head in range(KEY_VALUE_HEADS):
                        target[head, at_rows, :] = found[:, head * HEAD_SIZE : (head + 1) * HEAD_SIZE]
            key_place = (place - count + 1) * length + lax.broadcasted_iota(jnp.int32, (window, length), 0)
            query_place = place * length + lax.broadcasted_iota(jnp.int32, (window, length), 1)
            seen = (key_place >= low[b]) & (key_place <= query_place)
            bias[...] = jnp.where(seen, 0.0, MASK_VALUE_FILL)

            def pair_of_heads(pair, carry):
                cols = pl.ds(pl.multiple_of(pair * STRIP, STRIP), STRIP)
                strip, slope = q_v[here, cols], d_att[here, cols]
                products = slope.astype(f32) * attended[here, cols].astype(f32)
                heads = [
                    jnp.sum(products[:, h * HEAD_SIZE : (h + 1) * HEAD_SIZE], axis=1, keepdims=True)
                    for h in range(2 * GROUPS)
                ]
                spare = jnp.zeros((length, 128 - 2 * GROUPS), f32)
                deltas = jnp.transpose(jnp.concatenate(heads + [spare], axis=1))
                sums = lse[b, pair]
                turned = []
                for side in range(2):
                    key, value = keys[2 * pair + side], values[2 * pair + side]
                    key_sum = jnp.zeros((window, HEAD_SIZE), f32)
                    value_sum = jnp.zeros((window, HEAD_SIZE), f32)
                    for group in range(GROUPS):
                        row = side * GROUPS + group
                        query = strip[:, row * HEAD_SIZE : (row + 1) * HEAD_SIZE]
                        gradient = slope[:, row * HEAD_SIZE : (row + 1) * HEAD_SIZE]
                        chances = jnp.exp(dot(key, query, NT) * SCALE + bias[...] - sums[row : row + 1, :])
                        value_sum = value_sum + dot(chances.astype(bf16), gradient, NN)
                        steep = dot(value, gradient, NT) - deltas[row : row + 1, :]
                        steep = (chances * steep).astype(bf16)
                        key_sum = key_sum + dot(steep, query, NN)
                        turned.append(dot(steep, key, TN) * SCALE)
                    key_sums[2 * pair + side] = (key_sum * SCALE).astype(bf16)
                    value_sums[2 * pair + side] = value_sum.astype(bf16)
                whole = jnp.concatenate(turned, axis=1)
                d_v[here, cols] = turn(whole, cos_ref[here, :], -sin_ref[here, :]).astype(bf16)
                return carry

            lax.fori_loop(0, KEY_VALUE_HEADS // 2, pair_of_heads, 0)
            if b > 0:
                part_store(b - 1).wait()
            for back in range(count):
                at_rows = pl.ds((count - 1 - back) * length, length)
                for kind, found in ((0, key_sums), (1, value_sums)):
                    part_v[back, kind] = jnp.concatenate(
                        [found[h, at_rows, :] for h in range(KEY_VALUE_HEADS)], axis=1
                    )
            part_store(b).start()

        for b in range(batches):
            one_batch(b)
            if b == 0:
                near_phase("o")
        part_store(batches - 1).wait()

    def odd_copy(i):
        return send(parts.at[2 * i + 1], odd_in.at[i], odd_s.at[i], odd_r.at[i], {"ctx": twin})

    def hop_copy(step, sum_v):
        return send(sum_v.at[3 + step % 2], hop_in.at[step], hop_s.at[step], hop_r.at[step], {"ctx": place - 2})

    def gathered(step, sum_v):
        def fill(slot, src, sem):
            return pltpu.make_async_copy(src, sum_v.at[slot], sum_sem.at[sem])

        fill(0, parts.at[2 * step], 0).start()
        fill(0, parts.at[2 * step], 0).wait()
        if step < reach:

            @pl.when(core == 0)
            def _():
                fill(1, odd_in.at[step], 1).start()
                fill(1, odd_in.at[step], 1).wait()

        else:

            @pl.when(core == 0)
            def _():
                sum_v[1] = jnp.zeros(sum_v.shape[1:], bf16)

        if step > 0:

            @pl.when(core == 1)
            def _():
                fill(1, odd_in.at[step - 1], 1).start()
                fill(1, odd_in.at[step - 1], 1).wait()

        else:

            @pl.when(core == 1)
            def _():
                sum_v[1] = jnp.zeros(sum_v.shape[1:], bf16)

    def hop_out(step, sum_v):
        gathered(step, sum_v)
        if step < reach:

            @pl.when(ahead)
            def _():
                hop_copy(step + 1, sum_v).wait_recv()
                came = pltpu.make_async_copy(hop_in.at[step + 1], sum_v.at[2], sum_sem.at[2])
                came.start()
                came.wait()

            @pl.when(place + 2 >= chain)
            def _():
                sum_v[2] = jnp.zeros(sum_v.shape[1:], bf16)

        small = tokens // 4

        def one(i, carry):
            at = pl.ds(pl.multiple_of((i % 4) * small, small), small)
            kind = i // 4
            total = sum_v[0, kind, at, :].astype(f32) + sum_v[1, kind, at, :].astype(f32)
            if step < reach:
                total = total + sum_v[2, kind, at, :].astype(f32)
            if step > 0:
                sum_v[3 + step % 2, kind, at, :] = total.astype(bf16)
            else:

                @pl.when(kind == 0)
                def _():
                    turned = turn(total, cos_ref[at, :], -sin_ref[at, :])
                    d_v[at, width : width + KV_WIDTH] = turned.astype(bf16)

                @pl.when(kind == 1)
                def _():
                    d_v[at, width + KV_WIDTH :] = total.astype(bf16)

            return carry

        if step > 0 and step + 2 <= reach:

            @pl.when(deep)
            def _():
                hop_copy(step + 2, sum_v).wait_send()

        lax.fori_loop(0, 8, one, 0)
        if step > 0:

            @pl.when(deep)
            def _():
                hop_copy(step, sum_v).start()

    first_load = pltpu.make_async_copy(d_attn, d_v.at[:, pl.ds(0, width)], load_sem.at[0])
    first_load.start()
    first_load.wait()
    turn_slopes("o")
    far_phase("o")
    pl.run_scoped(
        attention,
        pltpu.VMEM((KEY_VALUE_HEADS, window, HEAD_SIZE), bf16),
        pltpu.VMEM((KEY_VALUE_HEADS, window, HEAD_SIZE), bf16),
        pltpu.VMEM((window, length), f32),
        pltpu.VMEM((KEY_VALUE_HEADS, window, HEAD_SIZE), bf16),
        pltpu.VMEM((KEY_VALUE_HEADS, window, HEAD_SIZE), bf16),
    )
    def remainder(nb_q, sum_v, fs_load):
        kinds["q"] = (1, normed, far_q, fs_q, nb_q, z_q, grad_q)
        for i in range(reach):
            odd_copy(i).start()
        turn_slopes("q")
        far_phase("q")
        for i in range(reach):
            odd_copy(i).wait_recv()
        hop_out(reach, sum_v)
        near_phase("q")
        for step in range(reach - 1, 0, -1):
            hop_out(step, sum_v)
        z_phase("o", fs_load)
        settle("o")
        hop_out(0, sum_v)
        turn_slopes("kv")
        far_phase("kv")

        def slope_body(w_block, h_block, out):
            found = dot(d_v[...], w_block[...], NT)
            out[...] = found
            at = pl.ds(pl.multiple_of(pl.program_id(0) * 256, 256), 256)
            gain_v[0:1, at] = jnp.sum(found * h_block[...].astype(f32) * scale[...], axis=0, keepdims=True)

        pltpu.emit_pipeline(
            slope_body,
            grid=(width // 256,),
            in_specs=[
                pl.BlockSpec((256, w_in.shape[1]), lambda j: (j, 0)),
                pl.BlockSpec((tokens, 256), lambda j: (0, j)),
            ],
            out_specs=[pl.BlockSpec((tokens, 256), lambda j: (0, j))],
        )(w_in, hid, slope_out)
        gain_v[1:2, :] = gain_two[...]
        near_phase("kv")

        for f in range(peers):
            gain_fs[f, 0:2] = gain_v[0:2, f * rows : (f + 1) * rows]

        def gain_hop(f):
            return send(gain_fs.at[f], gain_all.at[chain + me], gf_s.at[f], gf_r.at[me], {"fs": f})

        def gain_arrival(s):
            return send(gain_fs.at[s], gain_all.at[chain + s], gf_s.at[s], gf_r.at[s], {"fs": s})

        for f in range(peers):

            @pl.when(f != me)
            def _(f=f):
                gain_hop(f).start()

        mine = gain_fs[me]
        for s in range(peers):

            @pl.when(s != me)
            def _(s=s):
                gain_arrival(s).wait_recv()

            @pl.when(s == me)
            def _(s=s):
                gain_all[chain + s] = jnp.zeros(gain_all.shape[1:], f32)

            mine = mine + gain_all[chain + s]
        gain_all[place] = mine

        def gain_spread(k):
            return send(gain_all.at[place], gain_all.at[place], ga_s.at[k], ga_r.at[k], {"ctx": toggled(place, k, chain)})

        for k in range(1, chain):
            gain_spread(k).start()
        z_phase("q", fs_load)
        for k in range(1, chain):
            gain_spread(k).wait_recv()
        total = gain_all[0]
        for c in range(1, chain):
            total = total + gain_all[c]
        gain_out[...] = total
        z_phase("kv", fs_load)
        finish("o")
        finish("q")
        finish("kv")

        settle("q")
        settle("kv")
        for i in range(reach):
            odd_copy(i).wait_send()
        for step in range(min(reach, 2), 0, -1):

            @pl.when(deep)
            def _(step=step):
                hop_copy(step, sum_v).wait_send()

        for f in range(peers):

            @pl.when(f != me)
            def _(f=f):
                gain_hop(f).wait_send()

        for k in range(1, chain):
            gain_spread(k).wait_send()

    pl.run_scoped(
        remainder,
        pltpu.VMEM(nb_o.shape, bf16),
        pltpu.VMEM((5, 2, tokens, KV_WIDTH), bf16),
        pltpu.VMEM((peers,) + z_o.shape[1:], bf16),
    )


def back(peers, chain, count, normed, attended, d_attn, d_att, queries, lse, low, cosine, sine, scale, gain_two, line, sib, hidden, w_in):
    tokens, width = normed.shape
    batches = low.shape[0]
    length = tokens // batches
    window = count * length
    planes, rows = chain // 2, width // peers
    own, own_kv = width // chain, 2 * KV_WIDTH // chain
    reach = (count - 1) // 2
    bf, f32 = jnp.bfloat16, jnp.float32
    S = jax.ShapeDtypeStruct
    DMA = pltpu.SemaphoreType.DMA
    far = pl.BlockSpec(memory_space=pl.ANY)
    near = pl.BlockSpec(memory_space=pltpu.VMEM)
    tiles = peers * planes
    return pl.pallas_call(
        functools.partial(back_kernel, peers, chain, count, batches),
        in_specs=[near, near, far] + [near] * 8 + [far] * 4,
        out_specs=[far] + [near] * 4 + [far] * 9,
        out_shape=[
            S((tokens, width), f32),
            S((own, rows), f32),
            S((own, rows), f32),
            S((own_kv, rows), f32),
            S((8, rows), f32),
            S((tiles, own, rows), bf),
            S((tiles, own, rows), bf),
            S((tiles, own_kv, rows), bf),
            S((peers, planes, own, rows), bf),
            S((peers, planes, own, rows), bf),
            S((peers, planes, own_kv, rows), bf),
            S((count, 2, tokens, KV_WIDTH), bf),
            S((reach, 2, tokens, KV_WIDTH), bf),
            S((reach + 1, 2, tokens, KV_WIDTH), bf),
        ],
        scratch_shapes=[
            pltpu.VMEM((tiles, own, rows), bf),
            pltpu.VMEM((planes, own, rows), bf),
            pltpu.VMEM((planes, own, rows), bf),
            pltpu.VMEM((planes, own_kv, rows), bf),
            pltpu.VMEM((2, planes, own, tokens), bf),
            pltpu.VMEM((2, own, rows), bf),
            pltpu.VMEM((count, 2, length, KV_WIDTH), bf),
            pltpu.VMEM((tokens, width + 2 * KV_WIDTH), bf),
            pltpu.VMEM((2, 2, length, KV_WIDTH), bf),
            pltpu.VMEM((8, width), f32),
            pltpu.VMEM((peers, 8, rows), f32),
            pltpu.VMEM((chain + peers, 8, rows), f32),
            DMA((3, tiles)), DMA((3, tiles)), DMA((3, peers, planes)), DMA((3, peers, planes)),
            DMA((3, planes)), DMA((3, planes)), DMA((2,)), DMA((peers,)), DMA((1,)),
            DMA((reach,)), DMA((reach,)), DMA((reach + 1,)), DMA((reach + 1,)), DMA((3,)), DMA((2,)),
            DMA((peers,)), DMA((peers,)), DMA((chain,)), DMA((chain,)),
        ],
        compiler_params=pltpu.CompilerParams(
            vmem_limit_bytes=FEED_VMEM, collective_id=3, has_side_effects=True
        ),
        cost_estimate=cost(2 * tokens * width * 3840 * 20, 200 * tokens * width, QUERY_HEADS * tokens * window),
    )(normed, attended, d_attn, d_att, queries, lse, low, cosine, sine, scale, gain_two, line, sib, hidden, w_in)


def boundaries(lengths, positions):
    cut_points = jnp.cumsum(lengths)[:-1]
    passed = positions[:, None] >= cut_points[None, :]
    return jnp.max(jnp.where(passed, cut_points[None, :], 0), axis=1)


def matmul(left, right):
    return dot(left, right, NN)


def matmul_back(gradient, weight):
    return dot(gradient, weight, NT)


def on_device(
    hidden_in,
    doc_lengths,
    attn_gain,
    query_weight,
    key_matrix,
    value_matrix,
    output_weight,
    mlp_gain,
    gate_weight,
    up_weight,
    down_weight,
    out_grad,
):
    owners, chain = lax.axis_size("fs"), lax.axis_size("ctx")
    owner, place = lax.axis_index("fs"), lax.axis_index("ctx")
    core = place % 2
    planes = chain // 2
    batches, length, width = hidden_in.shape
    tokens = batches * length
    rows = query_weight.shape[0]
    inner = down_weight.shape[0]
    count = min(WINDOW // length + 1, chain)

    def across(x, k):
        return lax.ppermute(x, "fs", [(i, i ^ k) for i in range(owners)])

    grads_in = out_grad.reshape(tokens, width)

    positions = place * length + jnp.arange(length, dtype=jnp.int32)
    starts = jax.vmap(lambda lengths: boundaries(lengths, positions))(doc_lengths)
    low = jnp.maximum(starts, positions[None, :] - (WINDOW - 1))
    frequency = ROPE_THETA ** (-2.0 * jnp.arange(HALF, dtype=jnp.float32) / HEAD_SIZE)
    turns = (positions[None, :] - starts).reshape(tokens).astype(jnp.float32)
    angles = turns[:, None] * frequency[None, :]
    cosine, sine = jnp.cos(angles), jnp.sin(angles)
    cosine = jnp.tile(jnp.concatenate([cosine, cosine], axis=1), (1, STRIP // HEAD_SIZE))
    sine = jnp.tile(jnp.concatenate([-sine, sine], axis=1), (1, STRIP // HEAD_SIZE))

    gains = jnp.concatenate([jnp.stack([attn_gain, mlp_gain]).astype(jnp.float32), jnp.zeros((6, rows))])
    (
        in_full, out_full, gate_full, up_full, grads_all, normed, queries, line, kin, attended_rows, lse, gain_rows
    ) = front(
        owners,
        chain,
        count,
        hidden_in.reshape(tokens, width),
        gains,
        (query_weight, key_matrix, value_matrix, output_weight, gate_weight, up_weight),
        grads_in,
        cosine,
        sine,
        low[:, :, None],
    )
    gain_one, gain_two = gain_rows[0], gain_rows[1]

    x = hidden_in.reshape(tokens, width).astype(jnp.float32)
    scale_one = lax.rsqrt(jnp.mean(x * x, axis=1, keepdims=True) + NORM_EPS)
    projected = matmul(attended_rows, out_full)
    residual = x + projected
    scale_two = lax.rsqrt(jnp.mean(residual * residual, axis=1, keepdims=True) + NORM_EPS)
    normed_two = (residual * scale_two * gain_two).astype(jnp.bfloat16)

    normed_all, gate_slopes, up_slopes, mid = feed(
        owners, normed_two, grads_all, down_weight, gate_full, up_full
    )
    gate_part, up_part = gate_fold(normed_all, gate_slopes, up_slopes)
    mid, gate_part, up_part = lax.optimization_barrier((mid, gate_part, up_part))
    down_part = down_fold(grads_all, mid, chain)
    gate_slopes, up_slopes, mid, gate_part, up_part, down_part = lax.optimization_barrier(
        (gate_slopes, up_slopes, mid, gate_part, up_part, down_part)
    )
    own_part, in_parts, out_parts = feed_back(
        owners, gate_slopes, up_slopes, mid, down_weight, gate_full, up_full
    )
    normed_two_grad = own_part.astype(jnp.float32) + jnp.sum(in_parts.astype(jnp.float32), axis=0)

    def fold_tokens(parts):
        total = lax.dynamic_index_in_dim(parts, owner, 0, keepdims=False).astype(jnp.float32)
        for k in range(1, owners):
            part = lax.dynamic_index_in_dim(parts, owner ^ k, 0, keepdims=False)
            total = total + across(part, k).astype(jnp.float32)
        return total

    spans = chain // owners
    down_grad = lax.psum_scatter(down_part, "ctx", scatter_dimension=0, tiled=True)[0]
    down_grad = down_grad.astype(jnp.float32)
    gate_mine = lax.psum_scatter(gate_part, "ctx", scatter_dimension=0, tiled=True)
    up_mine = lax.psum_scatter(up_part, "ctx", scatter_dimension=0, tiled=True)
    slot = place % spans
    strip = inner // spans
    gate_grad = jnp.zeros((spans,) + (gate_mine.shape[0], strip), jnp.float32)
    up_grad = gate_grad
    for k in range(spans):
        moves = [
            (f * chain + c, (c // spans) * chain + f * spans + (c % spans + k) % spans)
            for f in range(owners)
            for c in range(chain)
        ]
        cut = ((slot + k) % spans) * strip
        piece = jnp.stack([lax.dynamic_slice_in_dim(m, cut, strip, 1) for m in (gate_mine, up_mine)])
        piece = lax.ppermute(piece, ("fs", "ctx"), moves).astype(jnp.float32)
        to = (slot - k) % spans
        gate_grad = lax.dynamic_update_slice_in_dim(gate_grad, piece[:1], to, 0)
        up_grad = lax.dynamic_update_slice_in_dim(up_grad, piece[1:], to, 0)
    gate_grad = gate_grad.reshape(rows, strip)
    up_grad = up_grad.reshape(rows, strip)

    scaled_two = normed_two_grad * gain_two
    residual_grad = grads_in.astype(jnp.float32) + scale_two * (
        scaled_two
        - residual * scale_two * scale_two * jnp.mean(scaled_two * residual, axis=1, keepdims=True)
    )
    gain_two_part = jnp.sum(normed_two_grad * residual * scale_two, axis=0)
    attn_grad = residual_grad.astype(jnp.bfloat16)
    attended_grad = matmul_back(attn_grad, out_full).astype(jnp.bfloat16)
    ended = back(
        owners,
        chain,
        count,
        normed,
        attended_rows,
        attn_grad,
        attended_grad,
        queries,
        lse,
        low[:, None, :],
        cosine,
        sine,
        scale_one,
        gain_two_part[None, :],
        line,
        kin,
        hidden_in.reshape(tokens, width),
        in_full,
    )
    normed_grad, output_turned, query_turned, kv_turned, gain_grads = ended[:5]
    residual_late = lax.optimization_barrier((residual, normed_grad))[0]
    hidden_out = residual_late + fold_tokens(out_parts)
    output_grad, query_grad = output_turned.T, query_turned.T
    kv_own = KV_WIDTH // chain
    key_grad, value_grad = kv_turned[:kv_own].T, kv_turned[kv_own:].T
    scaled_one = normed_grad * gain_one
    hidden_grad = residual_grad + scale_one * (
        scaled_one - x * scale_one * scale_one * jnp.mean(scaled_one * x, axis=1, keepdims=True)
    )
    return (
        hidden_out.reshape(batches, length, width),
        hidden_grad.reshape(batches, length, width),
        gain_grads[0],
        query_grad,
        key_grad,
        value_grad,
        output_grad,
        gain_grads[1],
        gate_grad,
        up_grad,
        down_grad,
    )


def solution(mesh):
    tokens_spec = P("fs", "ctx", None)
    rows_spec = P("fs", None)
    block_spec = P("fs", "ctx")
    return jax.shard_map(
        on_device,
        mesh=mesh,
        in_specs=(
            tokens_spec,
            rows_spec,
            P("fs"),
            rows_spec,
            rows_spec,
            rows_spec,
            rows_spec,
            P("fs"),
            rows_spec,
            rows_spec,
            rows_spec,
            tokens_spec,
        ),
        out_specs=(
            tokens_spec,
            tokens_spec,
            P("fs"),
            block_spec,
            block_spec,
            block_spec,
            block_spec,
            P("fs"),
            block_spec,
            block_spec,
            block_spec,
        ),
        check_vma=False,
    )
```

```python
import functools
import math

import jax
import jax.numpy as jnp
from jax import lax
from jax.experimental import pallas as pl
from jax.experimental.pallas import tpu as pltpu
from jax.sharding import PartitionSpec as P

MODEL_WIDTH = 2560
QUERY_HEADS = 32
KEY_VALUE_HEADS = 8
HEAD_SIZE = 80
WINDOW = 1024
GROUPS = QUERY_HEADS // KEY_VALUE_HEADS
HALF = HEAD_SIZE // 2
KV_WIDTH = KEY_VALUE_HEADS * HEAD_SIZE
STRIP = 640
HALF_KV = KV_WIDTH // 2
SCALE = 1.0 / math.sqrt(HEAD_SIZE)

NORM_EPS = 1e-05
ROPE_THETA = 1000000.0
MASK_VALUE_FILL = -1e30
VMEM = 60 * 1024 * 1024
FEED_VMEM = 62 * 1024 * 1024
MESH = pl.DeviceIdType.MESH

NT = (((1,), (1,)), ((), ()))
TN = (((0,), (0,)), ((), ()))
NN = (((1,), (0,)), ((), ()))


def dot(left, right, dims):
    return lax.dot_general(left, right, dims, preferred_element_type=jnp.float32)


def params(**more):
    return pltpu.CompilerParams(vmem_limit_bytes=VMEM, **more)


def cost(flops, moved, exps=0):
    return pl.CostEstimate(flops=int(flops), bytes_accessed=int(moved), transcendentals=int(exps))


def turn(x, cosine, sine):
    width = x.shape[1]
    lane = lax.broadcasted_iota(jnp.int32, x.shape, 1) % HEAD_SIZE
    partner = jnp.where(
        lane < HALF, pltpu.roll(x, width - HALF, 1), pltpu.roll(x, HALF, 1)
    )
    return x * cosine + partner * sine


def toggled(me, k, count):
    found, bit = me, 1
    while bit < count:
        found = found + ((k // bit) % 2) * bit * (1 - 2 * ((me // bit) % 2))
        bit *= 2
    return found


def feed_kernel(
    peers, nt_ref, og_all, down_ref, gate_ref, up_ref,
    nt_all, gs_all, us_all, mid_all,
    nt_v, gs_v, us_v, mid_v, og_v, gate_v, up_v, down_v,
    load_sem, weight_sem, tile_sem, own_sem, keep_sem, nt_send, nt_recv,
):
    tokens = nt_ref.shape[0]
    inner = down_ref.shape[0]
    middle = tokens // 2
    square = peers == 4
    me = lax.axis_index("fs")
    bf16 = jnp.bfloat16

    def remote(src, dst, at, k):
        return pltpu.make_async_remote_copy(
            src_ref=src, dst_ref=dst, send_sem=nt_send.at[at], recv_sem=nt_recv.at[at],
            device_id={"fs": toggled(me, k, peers)}, device_id_type=MESH,
        )

    barrier = pltpu.get_barrier_semaphore()
    for k in range(1, peers):
        pl.semaphore_signal(barrier, inc=1, device_id={"fs": toggled(me, k, peers)}, device_id_type=MESH)
    pl.semaphore_wait(barrier, peers - 1)

    top, bottom = pl.ds(0, middle), pl.ds(middle, middle)
    reached = [1, 2] if square else list(range(1, peers))
    spread = {k: remote(nt_ref, nt_v.at[k], k, k) for k in reached}
    for k in reached:
        spread[k].start()
    if square:
        spread[3] = remote(nt_v.at[1, top], nt_v.at[3, top], 3, 2)
        spread[0] = remote(nt_v.at[2, bottom], nt_v.at[3, bottom], 0, 1)
    own = pltpu.make_async_copy(nt_ref, nt_v.at[0], own_sem.at[0])
    own.start()
    weights = [
        pltpu.make_async_copy(src, dst, weight_sem.at[i])
        for i, (src, dst) in enumerate(((gate_ref, gate_v), (up_ref, up_v), (down_ref, down_v)))
    ]
    for copy in weights:
        copy.start()

    def grads_of(k):
        return pltpu.make_async_copy(
            og_all.at[toggled(me, k, peers)], og_v.at[k % 2], load_sem.at[k % 2]
        )

    def keep(k):
        return pltpu.make_async_copy(nt_v.at[k], nt_all.at[k], keep_sem.at[k])

    grads_of(0).start()
    own.wait()
    for copy in weights:
        copy.wait()
    tile = 256 if inner % 256 == 0 else 128
    tiles = inner // tile

    def stores(k, at):
        return [
            pltpu.make_async_copy(src.at[:, at], dst.at[:, at], tile_sem.at[i, at.start // tile])
            for i, (src, dst) in enumerate(
                (
                    (gs_v, gs_all.at[k]),
                    (us_v, us_all.at[k]),
                    (mid_v, mid_all.at[toggled(me, k, peers)]),
                )
            )
        ]

    for k in range(peers):
        if square and k == 1:
            spread[1].wait_recv()
            spread[3].start()
            spread[2].wait_recv()
            spread[0].start()
        elif square and k == 3:
            spread[3].wait_recv()
            spread[0].wait_recv()
        elif not square and k > 0:
            spread[k].wait_recv()
        keep(k).start()
        grads_of(k).wait()
        if k + 1 < peers:
            grads_of(k + 1).start()

        def some(j, carry, k=k):
            at = pl.ds(pl.multiple_of(j * tile, tile), tile)
            gate = dot(nt_v[k], gate_v[:, at], NN)
            up = dot(nt_v[k], up_v[:, at], NN)
            grad = dot(og_v[k % 2], down_v[at, :], NT)
            sig = 1.0 / (1.0 + jnp.exp(-gate))
            silu = gate * sig
            if k > 0:
                for copy in stores(k - 1, at):
                    copy.wait()
            mid_v[:, at] = (silu * up).astype(bf16)
            gs_v[:, at] = (grad * up * sig * (1.0 + gate * (1.0 - sig))).astype(bf16)
            us_v[:, at] = (grad * silu).astype(bf16)
            for copy in stores(k, at):
                copy.start()
            return carry

        lax.fori_loop(0, tiles, some, 0)

    def settle(j, carry):
        at = pl.ds(pl.multiple_of(j * tile, tile), tile)
        for copy in stores(peers - 1, at):
            copy.wait()
        return carry

    lax.fori_loop(0, tiles, settle, 0)
    for k in range(peers):
        keep(k).wait()
    for copy in spread.values():
        copy.wait_send()


def feed(peers, nt, og_all, down, gate, up):
    tokens, width = nt.shape
    inner = down.shape[0]
    bf = jnp.bfloat16
    S = jax.ShapeDtypeStruct
    any_ = pl.BlockSpec(memory_space=pl.ANY)
    DMA = pltpu.SemaphoreType.DMA
    inner_shape = S((peers, tokens, inner), bf)
    return pl.pallas_call(
        functools.partial(feed_kernel, peers),
        in_specs=[any_] * 5,
        out_specs=[any_] * 4,
        out_shape=[S((peers, tokens, width), bf), inner_shape, inner_shape, inner_shape],
        scratch_shapes=[
            pltpu.VMEM((peers, tokens, width), bf),
            pltpu.VMEM((tokens, inner), bf), pltpu.VMEM((tokens, inner), bf), pltpu.VMEM((tokens, inner), bf),
            pltpu.VMEM((2, tokens, width), bf),
            pltpu.VMEM((width, inner), bf), pltpu.VMEM((width, inner), bf), pltpu.VMEM((inner, width), bf),
            DMA((2,)), DMA((3,)), DMA((3, 16)), DMA((1,)), DMA((peers,)),
            DMA((peers,)), DMA((peers,)),
        ],
        compiler_params=pltpu.CompilerParams(vmem_limit_bytes=FEED_VMEM, collective_id=1, has_side_effects=True),
        cost_estimate=cost(6 * peers * tokens * width * inner, 20 * width * inner, peers * tokens * inner),
    )(nt, og_all, down, gate, up)


def feed_back_kernel(
    peers, gs_all, us_all, mid_all, down_ref, gate_ref, up_ref,
    dn_own, dn_in, *rest,
):
    out_parts, rest = rest[:peers], rest[peers:]
    (gs_v, us_v, io, relay, out_v, gate_v, up_v, down_v,
     load_sem, weight_sem, out_sem, own_sem, dn_send, dn_recv) = rest
    tokens, inner = gs_v.shape[1:]
    width = gate_ref.shape[0]
    middle = tokens // 2
    square = peers == 4
    me = lax.axis_index("fs")
    bf16 = jnp.bfloat16

    def remote(src, dst, at, k):
        return pltpu.make_async_remote_copy(
            src_ref=src, dst_ref=dst, send_sem=dn_send.at[at], recv_sem=dn_recv.at[at],
            device_id={"fs": toggled(me, k, peers)}, device_id_type=MESH,
        )

    barrier = pltpu.get_barrier_semaphore()
    for k in range(1, peers):
        pl.semaphore_signal(barrier, inc=1, device_id={"fs": toggled(me, k, peers)}, device_id_type=MESH)
    pl.semaphore_wait(barrier, peers - 1)
    top, bottom = pl.ds(0, middle), pl.ds(middle, middle)

    def returns(k):
        if square and k == 3:
            return (remote(io.at[3, top], relay.at[0], 3, 1), remote(io.at[3, bottom], relay.at[1], 0, 2))
        return (remote(io.at[k], dn_in.at[k - 1], k, k),)

    order = [peers - 1, 0] + list(range(peers - 2, 0, -1))
    weights = [
        pltpu.make_async_copy(src, dst, weight_sem.at[i])
        for i, (src, dst) in enumerate(((gate_ref, gate_v), (up_ref, up_v), (down_ref, down_v)))
    ]
    for copy in weights:
        copy.start()

    def slopes_of(turn):
        k, slot = order[turn], turn % 2
        return [
            pltpu.make_async_copy(src.at[k], dst.at[slot], load_sem.at[i, slot])
            for i, (src, dst) in enumerate(((gs_all, gs_v), (us_all, us_v)))
        ]

    def units_of(turn):
        slab, slot = toggled(me, order[turn], peers), turn % 2
        return pltpu.make_async_copy(mid_all.at[slab], gs_v.at[slot], load_sem.at[0, slot])

    for copy in slopes_of(0):
        copy.start()
    wide = 256
    strips = width // wide
    weights[0].wait()
    weights[1].wait()
    for turn, k in enumerate(order):
        slot = turn % 2
        for copy in slopes_of(turn):
            copy.wait()
        if turn + 1 < peers:
            for copy in slopes_of(turn + 1):
                copy.start()
        if square and k == 2:
            returns(3)[0].wait_recv()
        if square and k == 1:
            returns(3)[1].wait_recv()

        def more(j, carry, k=k, slot=slot):
            at = pl.ds(pl.multiple_of(j * wide, wide), wide)
            part = dot(gs_v[slot], gate_v[at, :], NT) + dot(us_v[slot], up_v[at, :], NT)
            if square and k == 2:
                io[k, top, at] = (part[:middle] + relay[0, :, at].astype(jnp.float32)).astype(bf16)
                io[k, bottom, at] = part[middle:].astype(bf16)
            elif square and k == 1:
                io[k, top, at] = part[:middle].astype(bf16)
                io[k, bottom, at] = (part[middle:] + relay[1, :, at].astype(jnp.float32)).astype(bf16)
            else:
                io[k, :, at] = part.astype(bf16)
            return carry

        lax.fori_loop(0, strips, more, 0)
        if k == 0:
            pltpu.make_async_copy(io.at[0], dn_own, own_sem.at[0]).start()
        else:
            for copy in returns(k):
                copy.start()

    weights[2].wait()
    units_of(0).start()
    for turn, k in enumerate(order):
        slot = turn % 2
        units_of(turn).wait()
        if turn + 1 < peers:
            units_of(turn + 1).start()

        def out_copy(j, k=k):
            at = pl.ds(pl.multiple_of(j * wide, wide), wide)
            return pltpu.make_async_copy(out_v.at[j % 2], out_parts[k].at[:, at], out_sem.at[j % 2])

        def last(j, carry, slot=slot, out_copy=out_copy):
            at = pl.ds(pl.multiple_of(j * wide, wide), wide)
            found = dot(gs_v[slot], down_v[:, at], NN).astype(bf16)

            @pl.when(j >= 2)
            def _():
                out_copy(j - 2).wait()

            out_v[j % 2] = found
            out_copy(j).start()
            return carry

        lax.fori_loop(0, strips, last, 0)
        out_copy(strips - 2).wait()
        out_copy(strips - 1).wait()

    pltpu.make_async_copy(io.at[0], dn_own, own_sem.at[0]).wait()
    for k in range(1, peers):
        for copy in returns(k):
            copy.wait_send()
            if not (square and k == 3):
                copy.wait_recv()


def feed_back(peers, gs, us, mid, down, gate, up):
    tokens, inner = gs.shape[1:]
    width = gate.shape[0]
    bf = jnp.bfloat16
    S = jax.ShapeDtypeStruct
    any_ = pl.BlockSpec(memory_space=pl.ANY)
    DMA = pltpu.SemaphoreType.DMA
    halves = 2 if peers == 4 else peers - 1
    return pl.pallas_call(
        functools.partial(feed_back_kernel, peers),
        in_specs=[any_] * 6,
        out_specs=[any_] * (2 + peers),
        out_shape=[S((tokens, width), bf), S((halves, tokens, width), bf)] + [S((tokens, width), bf)] * peers,
        scratch_shapes=[
            pltpu.VMEM((2, tokens, inner), bf), pltpu.VMEM((2, tokens, inner), bf),
            pltpu.VMEM((peers, tokens, width), bf),
            pltpu.VMEM((2, tokens // 2, width), bf),
            pltpu.VMEM((2, tokens, 256), bf),
            pltpu.VMEM((width, inner), bf), pltpu.VMEM((width, inner), bf), pltpu.VMEM((inner, width), bf),
            DMA((2, 2)), DMA((3,)), DMA((2,)), DMA((1,)), DMA((peers,)), DMA((peers,)),
        ],
        compiler_params=pltpu.CompilerParams(vmem_limit_bytes=FEED_VMEM, collective_id=4, has_side_effects=True),
        cost_estimate=cost(6 * peers * tokens * width * inner, 20 * width * inner),
    )(gs, us, mid, down, gate, up)


def gate_fold_kernel(nt_ref, gs_ref, us_ref, gate_ref, up_ref):
    peers, tokens, block = nt_ref.shape
    inner = gs_ref.shape[2]
    total = peers * tokens
    turned = jnp.transpose(nt_ref[...].reshape(total, block))
    gate_ref[...] = dot(turned, gs_ref[...].reshape(total, inner), NN).astype(jnp.bfloat16)
    up_ref[...] = dot(turned, us_ref[...].reshape(total, inner), NN).astype(jnp.bfloat16)


def gate_fold(nt_all, gs, us):
    peers, tokens, width = nt_all.shape
    inner = gs.shape[2]
    block = 512
    fixed = pl.BlockSpec((peers, tokens, inner), lambda j: (0, 0, 0), pipeline_mode=pl.Buffered(1))
    return pl.pallas_call(
        gate_fold_kernel,
        grid=(width // block,),
        in_specs=[pl.BlockSpec((peers, tokens, block), lambda j: (0, 0, j)), fixed, fixed],
        out_specs=[pl.BlockSpec((block, inner), lambda j: (j, 0))] * 2,
        out_shape=[jax.ShapeDtypeStruct((width, inner), jnp.bfloat16)] * 2,
        compiler_params=params(),
        cost_estimate=cost(4 * peers * tokens * width * inner, 2 * (nt_all.size + 3 * gs.size)),
    )(nt_all, gs, us)


def down_fold_kernel(og_ref, mid_ref, out_ref):
    peers, tokens, tile = mid_ref.shape
    owned = out_ref.shape[2]
    turned = jnp.transpose(mid_ref[...].reshape(peers * tokens, tile))
    wide = og_ref.shape[2]
    acc = dot(turned, og_ref[...].reshape(peers * tokens, wide), NN).astype(jnp.bfloat16)
    for c in range(out_ref.shape[0]):
        out_ref[c] = acc[:, c * owned : (c + 1) * owned]


def down_fold(og_all, mid_all, chain):
    peers, tokens, width = og_all.shape
    inner = mid_all.shape[2]
    tile = 256 if inner % 256 == 0 else 128
    owned = width // chain
    wide = 1280
    return pl.pallas_call(
        down_fold_kernel,
        grid=(width // wide, inner // tile),
        in_specs=[
            pl.BlockSpec((peers, tokens, wide), lambda i, j: (0, 0, i)),
            pl.BlockSpec((peers, tokens, tile), lambda i, j: (0, 0, j)),
        ],
        out_specs=pl.BlockSpec((wide // owned, tile, owned), lambda i, j: (i, j, 0)),
        out_shape=jax.ShapeDtypeStruct((chain, inner, owned), jnp.bfloat16),
        compiler_params=params(),
        cost_estimate=cost(2 * peers * tokens * width * inner, 2 * (og_all.size + 3 * mid_all.size)),
    )(og_all, mid_all)


def front_kernel(peers, chain, count, batches, *refs):
    (hid, gains, q_w, k_w, v_w, o_w, gate_w, up_w, og, cos_ref, sin_ref, low_ref) = refs[:12]
    (w_in, o_full, gate_part, up_part, og_all, normed_o, q_o, line_o, sib_o, att_o, lse_o, gain_o) = refs[12:24]
    (w_v, nt_v, nt_b, q_v, att_v, line_v, sib_v, gains_v) = refs[24:32]
    (own_sem, out_sem, gain_s, gain_r, qkv_s, qkv_r, twin_s, twin_r, back_s, back_r,
     og_s, og_r, hop_s, hop_r, kin_s, kin_r) = refs[32:]
    tokens, width = nt_v.shape
    rows = q_w.shape[0]
    inner = gate_part.shape[1]
    length = tokens // batches
    slots = line_v.shape[0]
    window = count * length
    square = peers == 4
    bf16, f32 = jnp.bfloat16, jnp.float32
    me, place = lax.axis_index("fs"), lax.axis_index("ctx")
    core, plane = place % 2, place // 2
    parity = plane % 2
    twin = place + 1 - 2 * core
    partner = place + 2 - 4 * parity
    deep = place >= 2
    ahead = place + 2 < chain

    def send(src, dst, send_sem, recv_sem, target):
        return pltpu.make_async_remote_copy(
            src_ref=src, dst_ref=dst, send_sem=send_sem, recv_sem=recv_sem,
            device_id=target, device_id_type=MESH,
        )

    def owner(k):
        return toggled(me, k, peers)

    def along(k):
        return {"fs": owner(k)}

    for i in range(1, slots):

        @pl.when(plane < i)
        def _(i=i):
            line_v[i] = jnp.zeros(line_v.shape[1:], bf16)
            sib_v[i] = jnp.zeros(line_v.shape[1:], bf16)

    barrier = pltpu.get_barrier_semaphore()
    for k in range(1, peers):
        pl.semaphore_signal(barrier, inc=1, device_id=along(k), device_id_type=MESH)
    pl.semaphore_signal(barrier, inc=1, device_id={"ctx": twin}, device_id_type=MESH)

    @pl.when(deep)
    def _():
        pl.semaphore_signal(barrier, inc=1, device_id={"ctx": place - 2}, device_id_type=MESH)

    @pl.when(ahead)
    def _():
        pl.semaphore_signal(barrier, inc=1, device_id={"ctx": place + 2}, device_id_type=MESH)

    planes = chain // 2
    behind = (plane + planes - 1) // planes
    before = (2 * planes - 2 - plane) // planes
    pl.semaphore_wait(barrier, peers + behind + before)

    share = rows // 2
    half = share // 2
    mats = ((q_w, pl.ds(0, width)), (k_w, pl.ds(width, KV_WIDTH)), (v_w, pl.ds(width + KV_WIDTH, KV_WIDTH)))

    def block(k, at, size):
        return pl.ds(pl.multiple_of(owner(k) * rows + core * share + at, 16), size)

    def first_hop(k, m):
        src, cols = mats[m]
        mine = pl.ds(pl.multiple_of(core * share, 16), share)
        return send(src.at[mine, :], w_v.at[block(0, 0, share), cols], qkv_s.at[k, m], qkv_r.at[k, m], along(k))

    def relay(part, m):
        source, target = (1, 2) if part == 3 else (2, 1)
        where = w_v.at[block(source, 0 if part == 3 else half, half), mats[m][1]]
        return send(where, where, qkv_s.at[part, m], qkv_r.at[part, m], along(target))

    def to_twin(part, m):
        if square and part in (0, 3):
            rows_at = block(3, 0 if part == 3 else half, half)
        else:
            rows_at = block(part, 0, share)
        where = w_v.at[rows_at, mats[m][1]]
        return send(where, where, twin_s.at[part, m], twin_r.at[part, m], {"ctx": twin})

    reached = [1, 2] if square else list(range(1, peers))
    for k in reached:
        for m in range(3):
            first_hop(k, m).start()
    own_rows = pl.ds(pl.multiple_of(me * rows, 16), rows)
    own_loads = [
        pltpu.make_async_copy(src, w_v.at[own_rows, cols], own_sem.at[i])
        for i, (src, cols) in enumerate(mats)
    ]
    for copy in own_loads:
        copy.start()
    gain_moves = [send(gains, gains_v.at[me], gain_s.at[k], gain_r.at[k], along(k)) for k in range(1, peers)]
    for copy in gain_moves:
        copy.start()
    gains_v[me] = gains[...]
    for copy in gain_moves:
        copy.wait_recv()
    whole_gain = jnp.concatenate([gains_v[f] for f in range(peers)], axis=1)
    gain_o[...] = whole_gain

    chunk = 64

    def norm(i, carry):
        at = pl.ds(pl.multiple_of(i * chunk, chunk), chunk)
        x = hid[at, :].astype(f32)
        scale = lax.rsqrt(jnp.mean(x * x, axis=1, keepdims=True) + NORM_EPS)
        normed = (x * scale * whole_gain[0:1]).astype(bf16)
        nt_v[at, :] = normed
        for f in range(peers):
            nt_b[f, at, :] = normed[:, f * rows : (f + 1) * rows]
        return carry

    lax.fori_loop(0, tokens // chunk, norm, 0)
    normed_out = pltpu.make_async_copy(nt_v, normed_o, out_sem.at[0])
    normed_out.start()

    quarter = rows // 4
    sources = (o_w, gate_w, up_w)
    fulls = (o_full, gate_part, up_part)

    def region(m, k, c, p):
        return fulls[m].at[pl.ds(pl.multiple_of(owner(k) * rows + (c + 2 * p) * quarter, 16), quarter), :]

    def back_first(m, k):
        at = pl.ds(pl.multiple_of((core + 2 * parity) * quarter, 16), quarter)
        if m == 0:
            src = o_w.at[at, :]
        else:
            src = sources[m].at[at, pl.ds(pl.multiple_of(owner(k) * inner, 128), inner)]
        return send(src, region(m, 0, core, parity), back_s.at[0, m, k], back_r.at[0, m, k], along(k))

    def back_plane(m, k):
        where = region(m, k, core, parity)
        return send(where, where, back_s.at[1, m, k], back_r.at[1, m, k], {"ctx": partner})

    def back_twin(m, k, p, stage):
        where = region(m, k, core, p)
        return send(where, where, back_s.at[stage, m, k], back_r.at[stage, m, k], {"ctx": twin})

    others = range(1, peers)

    def spread_first(which):
        for m in which:
            for k in others:
                back_first(m, k).start()

    def spread_second(which):
        for m in which:
            for k in others:
                back_first(m, k).wait_recv()
                back_plane(m, k).start()
                back_twin(m, k, parity, 2).start()

    def spread_third(which):
        for m in which:
            for k in others:
                back_plane(m, k).wait_recv()
                back_twin(m, k, 1 - parity, 3).start()

    def og_hop(k):
        return send(og, og_all.at[me], og_s.at[k], og_r.at[k], along(k))

    middle = tokens // 2

    def og_relay(part):
        source, target = (1, 2) if part == 3 else (2, 1)
        where = og_all.at[owner(source), pl.ds(0 if part == 3 else middle, middle), :]
        return send(where, where, og_s.at[part], og_r.at[part], along(target))

    wide = STRIP
    tiles = w_v.shape[1] // wide

    def project(acc, bounce):
        def through(src, dst, sem):
            shape = src.shape
            there = bounce.at[pl.ds(0, shape[0]), pl.ds(0, shape[1])]
            copy = pltpu.make_async_copy(src, there, sem.at[3])
            copy.start()
            copy.wait()
            copy = pltpu.make_async_copy(there, dst, sem.at[4])
            copy.start()
            copy.wait()

        through(og, og_all.at[me], own_sem)
        through(o_w, o_full.at[own_rows, :], own_sem)
        mine = pl.ds(pl.multiple_of(me * inner, 128), inner)
        through(gate_w.at[:, mine], gate_part.at[own_rows, :], own_sem)
        through(up_w.at[:, mine], up_part.at[own_rows, :], own_sem)
        for copy in own_loads:
            copy.wait()

        def add(k):
            rows_at = pl.ds(pl.multiple_of(owner(k) * rows, 16), rows)

            def one(j, carry):
                at = pl.ds(pl.multiple_of(j * wide, wide), wide)
                part = dot(nt_b[owner(k)], w_v[rows_at, at], NN)
                acc[:, at] = part if k == 0 else acc[:, at] + part
                return carry

            lax.fori_loop(0, tiles, one, 0)

        add(0)
        if square:
            for k, part in ((1, 3), (2, 0)):
                for m in range(3):
                    first_hop(k, m).wait_recv()
                for m in range(3):
                    relay(part, m).start()
                    to_twin(k, m).start()
                if k == 2:
                    spread_first([0])
                for m in range(3):
                    to_twin(k, m).wait_recv()
                add(k)
            for part in (3, 0):
                for m in range(3):
                    relay(part, m).wait_recv()
                    to_twin(part, m).start()
            spread_first([1, 2])
            for k in (1, 2):
                og_hop(k).start()
            for part in (3, 0):
                for m in range(3):
                    to_twin(part, m).wait_recv()
            add(3)
        else:
            for k in others:
                for m in range(3):
                    first_hop(k, m).wait_recv()
                    to_twin(k, m).start()
                for m in range(3):
                    to_twin(k, m).wait_recv()
                add(k)
            spread_first([0, 1, 2])
            for k in others:
                og_hop(k).start()

        line_v[0, 0] = turn(acc[:, width : width + KV_WIDTH], cos_ref[...], sin_ref[...]).astype(bf16)
        line_v[0, 1] = acc[:, width + KV_WIDTH :].astype(bf16)

        @pl.when(ahead)
        def _():
            hop(0).start()

        kin(0).start()

        def finish(j, carry):
            at = pl.ds(pl.multiple_of(j * wide, wide), wide)
            q_v[:, at] = turn(acc[:, at], cos_ref[...], sin_ref[...]).astype(bf16)
            return carry

        lax.fori_loop(0, width // wide, finish, 0)

    def hop(i):
        return send(line_v.at[i], line_v.at[i + 1], hop_s.at[i], hop_r.at[i], {"ctx": place + 2})

    def kin(i):
        return send(line_v.at[i], sib_v.at[i], kin_s.at[i], kin_r.at[i], {"ctx": twin})

    pl.run_scoped(project, pltpu.VMEM((tokens, w_v.shape[1]), f32), pltpu.VMEM((rows, width), bf16))

    w_out = pltpu.make_async_copy(w_v, w_in, out_sem.at[1])
    w_out.start()
    q_out = pltpu.make_async_copy(q_v, q_o, out_sem.at[2])
    q_out.start()
    for i in range(1, slots):

        @pl.when(plane >= i)
        def _(i=i):
            hop(i - 1).wait_recv()
            kin(i).start()

        if i + 1 < slots:

            @pl.when((plane >= i) & ahead)
            def _(i=i):
                hop(i).start()

    kin(0).wait_recv()
    for i in range(1, slots):

        @pl.when(plane >= i)
        def _(i=i):
            kin(i).wait_recv()

    spread_second([0])
    line_out = pltpu.make_async_copy(line_v, line_o, out_sem.at[3])
    line_out.start()
    sib_out = pltpu.make_async_copy(sib_v, sib_o, out_sem.at[4])
    sib_out.start()

    def attention(keys, values, bias):
        for b in range(batches):
            here = pl.ds(b * length, length)
            for back in range(count):
                at_rows = pl.ds((count - 1 - back) * length, length)
                for kind, target in ((0, keys), (1, values)):
                    if back % 2 == 0:
                        found = line_v[back // 2, kind, here, :]
                    else:
                        found = sib_v[(back + 1) // 2 - core, kind, here, :]
                    for head in range(KEY_VALUE_HEADS):
                        target[head, at_rows, :] = found[:, head * HEAD_SIZE : (head + 1) * HEAD_SIZE]
            key_place = (place - count + 1) * length + lax.broadcasted_iota(jnp.int32, (length, window), 1)
            query_place = place * length + lax.broadcasted_iota(jnp.int32, (length, window), 0)
            seen = (key_place >= low_ref[b]) & (key_place <= query_place)
            bias[...] = jnp.where(seen, 0.0, MASK_VALUE_FILL)

            def pair_of_heads(pair, carry, b=b, here=here):
                cols = pl.ds(pl.multiple_of(pair * STRIP, STRIP), STRIP)
                strip = q_v[here, cols]
                mixed, sums = [], []
                for side in range(2):
                    key, value = keys[2 * pair + side], values[2 * pair + side]
                    for group in range(GROUPS):
                        at = (side * GROUPS + group) * HEAD_SIZE
                        scores = dot(strip[:, at : at + HEAD_SIZE], key, NT) * SCALE + bias[...]
                        peak = jnp.max(scores, axis=1, keepdims=True)
                        weights = jnp.exp(scores - peak)
                        total = jnp.sum(weights, axis=1, keepdims=True)
                        mixed.append(dot(weights.astype(bf16), value, NN) / total)
                        sums.append(peak + jnp.log(total))
                att_v[here, cols] = jnp.concatenate(mixed, axis=1).astype(bf16)
                spare = jnp.zeros((length, 128 - 2 * GROUPS), f32)
                turned = jnp.transpose(jnp.concatenate(sums + [spare], axis=1))
                lse_o[b, pair] = turned[: 2 * GROUPS]
                return carry

            lax.fori_loop(0, KEY_VALUE_HEADS // 2, pair_of_heads, 0)
            if b == 0:
                spread_second([1, 2])

    pl.run_scoped(
        attention,
        pltpu.VMEM((KEY_VALUE_HEADS, window, HEAD_SIZE), bf16),
        pltpu.VMEM((KEY_VALUE_HEADS, window, HEAD_SIZE), bf16),
        pltpu.VMEM((length, window), f32),
    )
    att_out = pltpu.make_async_copy(att_v, att_o, out_sem.at[5])
    att_out.start()
    spread_third([0])
    if square:
        for k, part in ((1, 3), (2, 0)):
            og_hop(k).wait_recv()
            og_relay(part).start()
    spread_third([1, 2])

    for copy in (normed_out, w_out, q_out, line_out, sib_out, att_out):
        copy.wait()
    for copy in gain_moves:
        copy.wait_send()
    for m in range(3):
        for k in reached:
            first_hop(k, m).wait_send()
            to_twin(k, m).wait_send()
        if square:
            for part in (3, 0):
                relay(part, m).wait_send()
                to_twin(part, m).wait_send()
    for k in reached:
        og_hop(k).wait_send()
        if not square:
            og_hop(k).wait_recv()
    if square:
        for part in (3, 0):
            og_relay(part).wait()
    for m in range(3):
        for k in others:
            back_first(m, k).wait_send()
            back_plane(m, k).wait_send()
            back_twin(m, k, parity, 2).wait()
            back_twin(m, k, 1 - parity, 3).wait()
    kin(0).wait_send()

    @pl.when(ahead)
    def _():
        hop(0).wait_send()

    for i in range(1, slots):

        @pl.when(plane >= i)
        def _(i=i):
            kin(i).wait_send()

        if i + 1 < slots:

            @pl.when((plane >= i) & ahead)
            def _(i=i):
                hop(i).wait_send()


def front(peers, chain, count, hidden, gains, weights, og, cosine, sine, low):
    batches, length, _ = low.shape
    tokens, width = hidden.shape
    rows = weights[0].shape[0]
    inner = weights[4].shape[1] // peers
    slots = (count - 1) // 2 + 1
    bf = jnp.bfloat16
    S = jax.ShapeDtypeStruct
    DMA = pltpu.SemaphoreType.DMA
    far = pl.BlockSpec(memory_space=pl.ANY)
    near = pl.BlockSpec(memory_space=pltpu.VMEM)
    whole = S((tokens, width), bf)
    line = (slots, 2, tokens, KV_WIDTH)
    return pl.pallas_call(
        functools.partial(front_kernel, peers, chain, count, batches),
        in_specs=[near, near] + [far] * 7 + [near] * 3,
        out_specs=[far] * 10 + [near, near],
        out_shape=[
            S((width, width + 2 * KV_WIDTH), bf),
            S((width, width), bf),
            S((width, inner), bf),
            S((width, inner), bf),
            S((peers, tokens, width), bf),
            whole,
            whole,
            S(line, bf),
            S(line, bf),
            whole,
            S((batches, KEY_VALUE_HEADS // 2, 2 * GROUPS, length), jnp.float32),
            S((8, width), jnp.float32),
        ],
        scratch_shapes=[
            pltpu.VMEM((width, width + 2 * KV_WIDTH), bf),
            pltpu.VMEM((tokens, width), bf),
            pltpu.VMEM((peers, tokens, rows), bf),
            pltpu.VMEM((tokens, width), bf),
            pltpu.VMEM((tokens, width), bf),
            pltpu.VMEM(line, bf),
            pltpu.VMEM(line, bf),
            pltpu.VMEM((peers, 8, rows), jnp.float32),
            DMA((5,)), DMA((6,)), DMA((peers,)), DMA((peers,)),
            DMA((peers, 3)), DMA((peers, 3)), DMA((peers, 3)), DMA((peers, 3)),
            DMA((4, 3, peers)), DMA((4, 3, peers)), DMA((peers,)), DMA((peers,)),
            DMA((slots,)), DMA((slots,)), DMA((slots,)), DMA((slots,)),
        ],
        compiler_params=pltpu.CompilerParams(
            vmem_limit_bytes=FEED_VMEM, collective_id=2, has_side_effects=True
        ),
        cost_estimate=cost(2 * tokens * width * 3840 * 10, 200 * tokens * width, QUERY_HEADS * tokens * count * length),
    )(hidden, gains, *weights, og, cosine, sine, low)


def back_kernel(peers, chain, count, batches, *refs):
    (normed, attended, d_attn, d_att, q_v, lse, low, cos_ref, sin_ref, scale, gain_two, line, sib, hid, w_in) = refs[:15]
    (slope_out, grad_o, grad_q, grad_kv, gain_out, far_o, far_q, far_kv, fs_o, fs_q, fs_kv, parts, odd_in, hop_in) = refs[15:29]
    (nb_o, z_o, z_q, z_kv, slopes_t, load_v, d_v, gain_v, gain_fs, gain_all) = refs[29:39]
    (far_s, far_r, fs_s, fs_r, zs_s, zs_r, load_sem, fsl_sem, part_sem, odd_s, odd_r, hop_s, hop_r, sum_sem, block_sem, gf_s, gf_r, ga_s, ga_r) = refs[39:]
    tokens, width = normed.shape
    rows = width // peers
    planes = chain // 2
    length = tokens // batches
    window = count * length
    reach = (count - 1) // 2
    bf16, f32 = jnp.bfloat16, jnp.float32
    me, place = lax.axis_index("fs"), lax.axis_index("ctx")
    core, plane = place % 2, place // 2
    twin = place + 1 - 2 * core
    deep, ahead = place >= 2, place + 2 < chain

    def send(src, dst, send_sem, recv_sem, target):
        return pltpu.make_async_remote_copy(
            src_ref=src, dst_ref=dst, send_sem=send_sem, recv_sem=recv_sem,
            device_id=target, device_id_type=MESH,
        )

    barrier = pltpu.get_barrier_semaphore()
    for k in range(1, peers):
        pl.semaphore_signal(barrier, inc=1, device_id={"fs": toggled(me, k, peers)}, device_id_type=MESH)
    for k in range(1, chain):
        pl.semaphore_signal(barrier, inc=1, device_id={"ctx": toggled(place, k, chain)}, device_id_type=MESH)
    pl.semaphore_wait(barrier, peers + chain - 2)

    kinds = {
        "o": (0, attended, far_o, fs_o, nb_o, z_o, grad_o),
    }

    def own_of(x):
        return kinds[x][2].shape[1]

    def turn_slopes(x):
        own = own_of(x)
        for p in range(planes):
            if x == "kv":
                half = own // 2
                sides = []
                for c in range(2):
                    at = (2 * p + c) * half
                    sides.append(
                        jnp.concatenate(
                            [
                                d_v[:, width + at : width + at + half],
                                d_v[:, width + KV_WIDTH + at : width + KV_WIDTH + at + half],
                            ],
                            axis=1,
                        )
                    )
            else:
                sides = [d_v[:, (2 * p + c) * own : (2 * p + c + 1) * own] for c in range(2)]
            first, second = (jnp.transpose(side.astype(f32)) for side in sides)
            slopes_t[0, p, :own] = jnp.where(core == 0, first, second).astype(bf16)
            slopes_t[1, p, :own] = jnp.where(core == 0, second, first).astype(bf16)

    def far_copy(x, t):
        i, _, far, _, nb, _, _ = kinds[x]
        return send(nb.at[t, pl.ds(0, own_of(x))], far.at[t], far_s.at[i, t], far_r.at[i, t], {"ctx": twin})

    def far_phase(x):
        _, left, _, _, nb, _, _ = kinds[x]
        own = own_of(x)
        for f in range(peers):

            def one(p, carry, f=f):
                t = f * planes + p
                part = dot(slopes_t[1, p, :own], left[:, f * rows : (f + 1) * rows], NN)
                nb[t, :own] = part.astype(bf16)
                far_copy(x, t).start()
                return carry

            lax.fori_loop(0, planes, one, 0)

    def fs_copy(x, f, p):
        i, _, _, fs, nb, _, _ = kinds[x]
        src = nb.at[f * planes + p, pl.ds(0, own_of(x))]
        return send(src, fs.at[me, p], fs_s.at[i, f, p], fs_r.at[i, me, p], {"fs": f})

    def fs_arrival(x, s, p):
        i, _, _, fs, nb, _, _ = kinds[x]
        src = nb.at[p, pl.ds(0, own_of(x))]
        return send(src, fs.at[s, p], fs_s.at[i, s, p], fs_r.at[i, s, p], {"fs": s})

    def near_phase(x):
        _, left, far, _, nb, _, _ = kinds[x]
        own = own_of(x)
        total = peers * planes

        def load(t):
            slot = t % 2
            return pltpu.make_async_copy(far.at[t], load_v.at[slot, pl.ds(0, own)], load_sem.at[slot])

        far_copy(x, 0).wait_recv()
        load(0).start()
        for f in range(peers):

            def one(p, carry, f=f):
                t = f * planes + p

                @pl.when(t + 1 < total)
                def _():
                    far_copy(x, t + 1).wait_recv()
                    load(t + 1).start()

                part = dot(slopes_t[0, p, :own], left[:, f * rows : (f + 1) * rows], NN)
                load(t).wait()
                far_copy(x, t).wait_send()
                nb[t, :own] = (part + load_v[t % 2, :own].astype(f32)).astype(bf16)

                @pl.when(f != me)
                def _():
                    fs_copy(x, f, p).start()

                return carry

            lax.fori_loop(0, planes, one, 0)

    def z_copy(x, p):
        i, _, _, _, nb, z, _ = kinds[x]
        src = nb.at[me * planes + p, pl.ds(0, own_of(x))]
        return send(src, z.at[plane], zs_s.at[i, p], zs_r.at[i, plane], {"ctx": 2 * p + core})

    def z_arrival(x, p):
        i, _, _, _, nb, z, _ = kinds[x]
        src = nb.at[me * planes + p, pl.ds(0, own_of(x))]
        return send(src, z.at[p], zs_s.at[i, p], zs_r.at[i, p], {"ctx": 2 * p + core})

    def z_phase(x, fs_load):
        _, _, _, fs, nb, _, tot = kinds[x]
        own = own_of(x)

        def one(p, carry):
            for s in range(peers):
                there = pltpu.make_async_copy(fs.at[s, p], fs_load.at[s, pl.ds(0, own)], fsl_sem.at[s])

                @pl.when(s != me)
                def _(s=s, there=there):
                    fs_arrival(x, s, p).wait_recv()
                    there.start()

            fs_load[me, :own] = nb[me * planes + p, :own]
            for s in range(peers):
                there = pltpu.make_async_copy(fs.at[s, p], fs_load.at[s, pl.ds(0, own)], fsl_sem.at[s])

                @pl.when(s != me)
                def _(there=there):
                    there.wait()

            total = fs_load[0, :own].astype(f32)
            for s in range(1, peers):
                total = total + fs_load[s, :own].astype(f32)

            @pl.when(p == plane)
            def _():
                tot[...] = total

            @pl.when(p != plane)
            def _():
                nb[me * planes + p, :own] = total.astype(bf16)
                z_copy(x, p).start()

            return carry

        lax.fori_loop(0, planes, one, 0)

    def finish(x):
        _, _, _, _, _, z, tot = kinds[x]
        total = tot[...]
        for p in range(planes):

            @pl.when(p != plane)
            def _(p=p):
                z_arrival(x, p).wait_recv()

            @pl.when(p == plane)
            def _(p=p):
                z[p] = jnp.zeros(z.shape[1:], bf16)

            total = total + z[p].astype(f32)
        tot[...] = total

    def settle(x):
        for p in range(planes):
            for f in range(peers):

                @pl.when(f != me)
                def _(f=f, p=p):
                    fs_copy(x, f, p).wait_send()

            @pl.when(p != plane)
            def _(p=p):
                z_copy(x, p).wait_send()

    def part_store(b, part_v):
        return pltpu.make_async_copy(part_v, parts.at[:, :, pl.ds(b * length, length)], part_sem.at[0])

    def attention(keys, values, bias, key_sums, value_sums, part_v, block_v):
        def one_batch(b):
            here = pl.ds(b * length, length)

            def fetch(back):
                if back % 2 == 0:
                    src = line.at[back // 2, :, here]
                else:
                    src = sib.at[(back + 1) // 2 - core, :, here]
                return pltpu.make_async_copy(src, block_v.at[back % 2], block_sem.at[back % 2])

            fetch(0).start()
            for back in range(count):
                if back + 1 < count:
                    fetch(back + 1).start()
                fetch(back).wait()
                at_rows = pl.ds((count - 1 - back) * length, length)
                for kind, target in ((0, keys), (1, values)):
                    found = block_v[back % 2, kind]
                    for head in range(KEY_VALUE_HEADS):
                        target[head, at_rows, :] = found[:, head * HEAD_SIZE : (head + 1) * HEAD_SIZE]
            key_place = (place - count + 1) * length + lax.broadcasted_iota(jnp.int32, (window, length), 0)
            query_place = place * length + lax.broadcasted_iota(jnp.int32, (window, length), 1)
            seen = (key_place >= low[b]) & (key_place <= query_place)
            bias[...] = jnp.where(seen, 0.0, MASK_VALUE_FILL)

            def pair_of_heads(pair, carry):
                cols = pl.ds(pl.multiple_of(pair * STRIP, STRIP), STRIP)
                strip, slope = q_v[here, cols], d_att[here, cols]
                products = slope.astype(f32) * attended[here, cols].astype(f32)
                heads = [
                    jnp.sum(products[:, h * HEAD_SIZE : (h + 1) * HEAD_SIZE], axis=1, keepdims=True)
                    for h in range(2 * GROUPS)
                ]
                spare = jnp.zeros((length, 128 - 2 * GROUPS), f32)
                deltas = jnp.transpose(jnp.concatenate(heads + [spare], axis=1))
                sums = lse[b, pair]
                turned = []
                for side in range(2):
                    key, value = keys[2 * pair + side], values[2 * pair + side]
                    key_sum = jnp.zeros((window, HEAD_SIZE), f32)
                    value_sum = jnp.zeros((window, HEAD_SIZE), f32)
                    for group in range(GROUPS):
                        row = side * GROUPS + group
                        query = strip[:, row * HEAD_SIZE : (row + 1) * HEAD_SIZE]
                        gradient = slope[:, row * HEAD_SIZE : (row + 1) * HEAD_SIZE]
                        chances = jnp.exp(dot(key, query, NT) * SCALE + bias[...] - sums[row : row + 1, :])
                        value_sum = value_sum + dot(chances.astype(bf16), gradient, NN)
                        steep = dot(value, gradient, NT) - deltas[row : row + 1, :]
                        steep = (chances * steep).astype(bf16)
                        key_sum = key_sum + dot(steep, query, NN)
                        turned.append(dot(steep, key, TN) * SCALE)
                    key_sums[2 * pair + side] = (key_sum * SCALE).astype(bf16)
                    value_sums[2 * pair + side] = value_sum.astype(bf16)
                whole = jnp.concatenate(turned, axis=1)
                d_v[here, cols] = turn(whole, cos_ref[here, :], -sin_ref[here, :]).astype(bf16)
                return carry

            lax.fori_loop(0, KEY_VALUE_HEADS // 2, pair_of_heads, 0)
            if b > 0:
                part_store(b - 1, part_v).wait()
            for back in range(count):
                at_rows = pl.ds((count - 1 - back) * length, length)
                for kind, found in ((0, key_sums), (1, value_sums)):
                    part_v[back, kind] = jnp.concatenate(
                        [found[h, at_rows, :] for h in range(KEY_VALUE_HEADS)], axis=1
                    )
            part_store(b, part_v).start()

        for b in range(batches):
            one_batch(b)
            if b == 0:
                near_phase("o")
        part_store(batches - 1, part_v).wait()

    def odd_copy(i):
        return send(parts.at[2 * i + 1], odd_in.at[i], odd_s.at[i], odd_r.at[i], {"ctx": twin})

    def hop_copy(step, sum_v):
        return send(sum_v.at[3 + step % 2], hop_in.at[step], hop_s.at[step], hop_r.at[step], {"ctx": place - 2})

    def gathered(step, sum_v):
        def fill(slot, src, sem):
            return pltpu.make_async_copy(src, sum_v.at[slot], sum_sem.at[sem])

        fill(0, parts.at[2 * step], 0).start()
        fill(0, parts.at[2 * step], 0).wait()
        if step < reach:

            @pl.when(core == 0)
            def _():
                fill(1, odd_in.at[step], 1).start()
                fill(1, odd_in.at[step], 1).wait()

        else:

            @pl.when(core == 0)
            def _():
                sum_v[1] = jnp.zeros(sum_v.shape[1:], bf16)

        if step > 0:

            @pl.when(core == 1)
            def _():
                fill(1, odd_in.at[step - 1], 1).start()
                fill(1, odd_in.at[step - 1], 1).wait()

        else:

            @pl.when(core == 1)
            def _():
                sum_v[1] = jnp.zeros(sum_v.shape[1:], bf16)

    def hop_out(step, sum_v):
        gathered(step, sum_v)
        if step < reach:

            @pl.when(ahead)
            def _():
                hop_copy(step + 1, sum_v).wait_recv()
                came = pltpu.make_async_copy(hop_in.at[step + 1], sum_v.at[2], sum_sem.at[2])
                came.start()
                came.wait()

            @pl.when(place + 2 >= chain)
            def _():
                sum_v[2] = jnp.zeros(sum_v.shape[1:], bf16)

        small = tokens // 4

        def one(i, carry):
            at = pl.ds(pl.multiple_of((i % 4) * small, small), small)
            kind = i // 4
            total = sum_v[0, kind, at, :].astype(f32) + sum_v[1, kind, at, :].astype(f32)
            if step < reach:
                total = total + sum_v[2, kind, at, :].astype(f32)
            if step > 0:
                sum_v[3 + step % 2, kind, at, :] = total.astype(bf16)
            else:

                @pl.when(kind == 0)
                def _():
                    turned = turn(total, cos_ref[at, :], -sin_ref[at, :])
                    d_v[at, width : width + KV_WIDTH] = turned.astype(bf16)

                @pl.when(kind == 1)
                def _():
                    d_v[at, width + KV_WIDTH :] = total.astype(bf16)

            return carry

        if step > 0 and step + 2 <= reach:

            @pl.when(deep)
            def _():
                hop_copy(step + 2, sum_v).wait_send()

        lax.fori_loop(0, 8, one, 0)
        if step > 0:

            @pl.when(deep)
            def _():
                hop_copy(step, sum_v).start()

    first_load = pltpu.make_async_copy(d_attn, d_v.at[:, pl.ds(0, width)], load_sem.at[0])
    first_load.start()
    first_load.wait()
    turn_slopes("o")
    far_phase("o")
    pl.run_scoped(
        attention,
        pltpu.VMEM((KEY_VALUE_HEADS, window, HEAD_SIZE), bf16),
        pltpu.VMEM((KEY_VALUE_HEADS, window, HEAD_SIZE), bf16),
        pltpu.VMEM((window, length), f32),
        pltpu.VMEM((KEY_VALUE_HEADS, window, HEAD_SIZE), bf16),
        pltpu.VMEM((KEY_VALUE_HEADS, window, HEAD_SIZE), bf16),
        pltpu.VMEM((count, 2, length, KV_WIDTH), bf16),
        pltpu.VMEM((2, 2, length, KV_WIDTH), bf16),
    )
    def remainder(nb_q, nb_kv, sum_v, fs_load):
        kinds["q"] = (1, normed, far_q, fs_q, nb_q, z_q, grad_q)
        kinds["kv"] = (2, normed, far_kv, fs_kv, nb_kv, z_kv, grad_kv)
        for i in range(reach):
            odd_copy(i).start()
        turn_slopes("q")
        far_phase("q")
        for i in range(reach):
            odd_copy(i).wait_recv()
        hop_out(reach, sum_v)
        near_phase("q")
        for step in range(reach - 1, 0, -1):
            hop_out(step, sum_v)
        hop_out(0, sum_v)
        turn_slopes("kv")
        far_phase("kv")

        def slope_body(w_block, h_block, out):
            found = dot(d_v[...], w_block[...], NT)
            out[...] = found
            at = pl.ds(pl.multiple_of(pl.program_id(0) * 256, 256), 256)
            gain_v[0:1, at] = jnp.sum(found * h_block[...].astype(f32) * scale[...], axis=0, keepdims=True)

        pltpu.emit_pipeline(
            slope_body,
            grid=(width // 256,),
            in_specs=[
                pl.BlockSpec((256, w_in.shape[1]), lambda j: (j, 0)),
                pl.BlockSpec((tokens, 256), lambda j: (0, j)),
            ],
            out_specs=[pl.BlockSpec((tokens, 256), lambda j: (0, j))],
        )(w_in, hid, slope_out)
        gain_v[1:2, :] = gain_two[...]
        near_phase("kv")
        z_phase("o", fs_load)

        for f in range(peers):
            gain_fs[f, 0:2] = gain_v[0:2, f * rows : (f + 1) * rows]

        def gain_hop(f):
            return send(gain_fs.at[f], gain_all.at[chain + me], gf_s.at[f], gf_r.at[me], {"fs": f})

        def gain_arrival(s):
            return send(gain_fs.at[s], gain_all.at[chain + s], gf_s.at[s], gf_r.at[s], {"fs": s})

        for f in range(peers):

            @pl.when(f != me)
            def _(f=f):
                gain_hop(f).start()

        mine = gain_fs[me]
        for s in range(peers):

            @pl.when(s != me)
            def _(s=s):
                gain_arrival(s).wait_recv()

            @pl.when(s == me)
            def _(s=s):
                gain_all[chain + s] = jnp.zeros(gain_all.shape[1:], f32)

            mine = mine + gain_all[chain + s]
        gain_all[place] = mine

        def gain_spread(k):
            return send(gain_all.at[place], gain_all.at[place], ga_s.at[k], ga_r.at[k], {"ctx": toggled(place, k, chain)})

        for k in range(1, chain):
            gain_spread(k).start()
        z_phase("q", fs_load)
        for k in range(1, chain):
            gain_spread(k).wait_recv()
        total = gain_all[0]
        for c in range(1, chain):
            total = total + gain_all[c]
        gain_out[...] = total
        z_phase("kv", fs_load)
        finish("o")
        finish("q")
        finish("kv")

        settle("o")
        settle("q")
        settle("kv")
        for i in range(reach):
            odd_copy(i).wait_send()
        for step in range(min(reach, 2), 0, -1):

            @pl.when(deep)
            def _(step=step):
                hop_copy(step, sum_v).wait_send()

        for f in range(peers):

            @pl.when(f != me)
            def _(f=f):
                gain_hop(f).wait_send()

        for k in range(1, chain):
            gain_spread(k).wait_send()

    pl.run_scoped(
        remainder,
        pltpu.VMEM(nb_o.shape, bf16),
        pltpu.VMEM((nb_o.shape[0],) + z_kv.shape[1:], bf16),
        pltpu.VMEM((5, 2, tokens, KV_WIDTH), bf16),
        pltpu.VMEM((peers,) + z_o.shape[1:], bf16),
    )


def back(peers, chain, count, normed, attended, d_attn, d_att, queries, lse, low, cosine, sine, scale, gain_two, line, sib, hidden, w_in):
    tokens, width = normed.shape
    batches = low.shape[0]
    length = tokens // batches
    window = count * length
    planes, rows = chain // 2, width // peers
    own, own_kv = width // chain, 2 * KV_WIDTH // chain
    reach = (count - 1) // 2
    bf, f32 = jnp.bfloat16, jnp.float32
    S = jax.ShapeDtypeStruct
    DMA = pltpu.SemaphoreType.DMA
    far = pl.BlockSpec(memory_space=pl.ANY)
    near = pl.BlockSpec(memory_space=pltpu.VMEM)
    tiles = peers * planes
    return pl.pallas_call(
        functools.partial(back_kernel, peers, chain, count, batches),
        in_specs=[near, near, far] + [near] * 8 + [far] * 4,
        out_specs=[far] + [near] * 4 + [far] * 9,
        out_shape=[
            S((tokens, width), f32),
            S((own, rows), f32),
            S((own, rows), f32),
            S((own_kv, rows), f32),
            S((8, rows), f32),
            S((tiles, own, rows), bf),
            S((tiles, own, rows), bf),
            S((tiles, own_kv, rows), bf),
            S((peers, planes, own, rows), bf),
            S((peers, planes, own, rows), bf),
            S((peers, planes, own_kv, rows), bf),
            S((count, 2, tokens, KV_WIDTH), bf),
            S((reach, 2, tokens, KV_WIDTH), bf),
            S((reach + 1, 2, tokens, KV_WIDTH), bf),
        ],
        scratch_shapes=[
            pltpu.VMEM((tiles, own, rows), bf),
            pltpu.VMEM((planes, own, rows), bf),
            pltpu.VMEM((planes, own, rows), bf),
            pltpu.VMEM((planes, own_kv, rows), bf),
            pltpu.VMEM((2, planes, own, tokens), bf),
            pltpu.VMEM((2, own, rows), bf),
            pltpu.VMEM((tokens, width + 2 * KV_WIDTH), bf),
            pltpu.VMEM((8, width), f32),
            pltpu.VMEM((peers, 8, rows), f32),
            pltpu.VMEM((chain + peers, 8, rows), f32),
            DMA((3, tiles)), DMA((3, tiles)), DMA((3, peers, planes)), DMA((3, peers, planes)),
            DMA((3, planes)), DMA((3, planes)), DMA((2,)), DMA((peers,)), DMA((1,)),
            DMA((reach,)), DMA((reach,)), DMA((reach + 1,)), DMA((reach + 1,)), DMA((3,)), DMA((2,)),
            DMA((peers,)), DMA((peers,)), DMA((chain,)), DMA((chain,)),
        ],
        compiler_params=pltpu.CompilerParams(
            vmem_limit_bytes=FEED_VMEM, collective_id=3, has_side_effects=True
        ),
        cost_estimate=cost(2 * tokens * width * 3840 * 20, 200 * tokens * width, QUERY_HEADS * tokens * window),
    )(normed, attended, d_attn, d_att, queries, lse, low, cosine, sine, scale, gain_two, line, sib, hidden, w_in)


def boundaries(lengths, positions):
    cut_points = jnp.cumsum(lengths)[:-1]
    passed = positions[:, None] >= cut_points[None, :]
    return jnp.max(jnp.where(passed, cut_points[None, :], 0), axis=1)


def matmul(left, right):
    return dot(left, right, NN)


def matmul_back(gradient, weight):
    return dot(gradient, weight, NT)


def on_device(
    hidden_in,
    doc_lengths,
    attn_gain,
    query_weight,
    key_matrix,
    value_matrix,
    output_weight,
    mlp_gain,
    gate_weight,
    up_weight,
    down_weight,
    out_grad,
):
    owners, chain = lax.axis_size("fs"), lax.axis_size("ctx")
    owner, place = lax.axis_index("fs"), lax.axis_index("ctx")
    core = place % 2
    planes = chain // 2
    batches, length, width = hidden_in.shape
    tokens = batches * length
    rows = query_weight.shape[0]
    inner = down_weight.shape[0]
    count = min(WINDOW // length + 1, chain)

    def across(x, k):
        return lax.ppermute(x, "fs", [(i, i ^ k) for i in range(owners)])

    grads_in = out_grad.reshape(tokens, width)

    positions = place * length + jnp.arange(length, dtype=jnp.int32)
    starts = jax.vmap(lambda lengths: boundaries(lengths, positions))(doc_lengths)
    low = jnp.maximum(starts, positions[None, :] - (WINDOW - 1))
    frequency = ROPE_THETA ** (-2.0 * jnp.arange(HALF, dtype=jnp.float32) / HEAD_SIZE)
    turns = (positions[None, :] - starts).reshape(tokens).astype(jnp.float32)
    angles = turns[:, None] * frequency[None, :]
    cosine, sine = jnp.cos(angles), jnp.sin(angles)
    cosine = jnp.tile(jnp.concatenate([cosine, cosine], axis=1), (1, STRIP // HEAD_SIZE))
    sine = jnp.tile(jnp.concatenate([-sine, sine], axis=1), (1, STRIP // HEAD_SIZE))

    gains = jnp.concatenate([jnp.stack([attn_gain, mlp_gain]).astype(jnp.float32), jnp.zeros((6, rows))])
    (
        in_full, out_full, gate_full, up_full, grads_all, normed, queries, line, kin, attended_rows, lse, gain_rows
    ) = front(
        owners,
        chain,
        count,
        hidden_in.reshape(tokens, width),
        gains,
        (query_weight, key_matrix, value_matrix, output_weight, gate_weight, up_weight),
        grads_in,
        cosine,
        sine,
        low[:, :, None],
    )
    gain_one, gain_two = gain_rows[0], gain_rows[1]

    x = hidden_in.reshape(tokens, width).astype(jnp.float32)
    scale_one = lax.rsqrt(jnp.mean(x * x, axis=1, keepdims=True) + NORM_EPS)
    projected = matmul(attended_rows, out_full)
    residual = x + projected
    scale_two = lax.rsqrt(jnp.mean(residual * residual, axis=1, keepdims=True) + NORM_EPS)
    normed_two = (residual * scale_two * gain_two).astype(jnp.bfloat16)

    normed_all, gate_slopes, up_slopes, mid = feed(
        owners, normed_two, grads_all, down_weight, gate_full, up_full
    )
    gate_part, up_part = gate_fold(normed_all, gate_slopes, up_slopes)
    gate_slopes, up_slopes, gate_part, up_part = lax.optimization_barrier(
        (gate_slopes, up_slopes, gate_part, up_part)
    )
    own_part, in_parts, *out_parts = feed_back(
        owners, gate_slopes, up_slopes, mid, down_weight, gate_full, up_full
    )
    came = [across(out_parts[k], k) for k in range(1, owners)]
    normed_two_grad = own_part.astype(jnp.float32) + jnp.sum(in_parts.astype(jnp.float32), axis=0)

    spans = chain // owners
    gate_mine = lax.psum_scatter(gate_part, "ctx", scatter_dimension=0, tiled=True)
    up_mine = lax.psum_scatter(up_part, "ctx", scatter_dimension=0, tiled=True)
    mid = lax.optimization_barrier((mid, own_part))[0]
    down_part = down_fold(grads_all, mid, chain)
    down_grad = lax.psum_scatter(down_part, "ctx", scatter_dimension=0, tiled=True)[0]
    down_grad = down_grad.astype(jnp.float32)
    slot = place % spans
    strip = inner // spans
    pieces = []
    for k in range(spans):
        cut = ((slot + k) % spans) * strip
        piece = [lax.dynamic_slice_in_dim(m, cut, strip, 1) for m in (gate_mine, up_mine)]
        pieces.append(jnp.stack(piece))

    scaled_two = normed_two_grad * gain_two
    residual_grad = grads_in.astype(jnp.float32) + scale_two * (
        scaled_two
        - residual * scale_two * scale_two * jnp.mean(scaled_two * residual, axis=1, keepdims=True)
    )
    gain_two_part = jnp.sum(normed_two_grad * residual * scale_two, axis=0)
    attn_grad = residual_grad.astype(jnp.bfloat16)
    attended_grad = matmul_back(attn_grad, out_full).astype(jnp.bfloat16)
    attended_grad, *pieces = lax.optimization_barrier((attended_grad, *pieces))
    moved = []
    for k in range(spans):
        moves = [
            (f * chain + c, (c // spans) * chain + f * spans + (c % spans + k) % spans)
            for f in range(owners)
            for c in range(chain)
        ]
        moved.append(lax.ppermute(pieces[k], ("fs", "ctx"), moves))
    ended = back(
        owners,
        chain,
        count,
        normed,
        attended_rows,
        attn_grad,
        attended_grad,
        queries,
        lse,
        low[:, None, :],
        cosine,
        sine,
        scale_one,
        gain_two_part[None, :],
        line,
        kin,
        hidden_in.reshape(tokens, width),
        in_full,
    )
    normed_grad, output_turned, query_turned, kv_turned, gain_grads = ended[:5]
    residual_late = lax.optimization_barrier((residual, normed_grad))[0]
    hidden_out = residual_late + out_parts[0].astype(jnp.float32)
    for part in came:
        hidden_out = hidden_out + part.astype(jnp.float32)
    output_grad, query_grad = output_turned.T, query_turned.T
    kv_own = KV_WIDTH // chain
    key_grad, value_grad = kv_turned[:kv_own].T, kv_turned[kv_own:].T
    gate_grad = jnp.zeros((spans,) + (gate_mine.shape[0], strip), jnp.float32)
    up_grad = gate_grad
    for k in range(spans):
        piece = moved[k].astype(jnp.float32)
        to = (slot - k) % spans
        gate_grad = lax.dynamic_update_slice_in_dim(gate_grad, piece[:1], to, 0)
        up_grad = lax.dynamic_update_slice_in_dim(up_grad, piece[1:], to, 0)
    gate_grad = gate_grad.reshape(rows, strip)
    up_grad = up_grad.reshape(rows, strip)
    scaled_one = normed_grad * gain_one
    hidden_grad = residual_grad + scale_one * (
        scaled_one - x * scale_one * scale_one * jnp.mean(scaled_one * x, axis=1, keepdims=True)
    )
    return (
        hidden_out.reshape(batches, length, width),
        hidden_grad.reshape(batches, length, width),
        gain_grads[0],
        query_grad,
        key_grad,
        value_grad,
        output_grad,
        gain_grads[1],
        gate_grad,
        up_grad,
        down_grad,
    )


def solution(mesh):
    tokens_spec = P("fs", "ctx", None)
    rows_spec = P("fs", None)
    block_spec = P("fs", "ctx")
    return jax.shard_map(
        on_device,
        mesh=mesh,
        in_specs=(
            tokens_spec,
            rows_spec,
            P("fs"),
            rows_spec,
            rows_spec,
            rows_spec,
            rows_spec,
            P("fs"),
            rows_spec,
            rows_spec,
            rows_spec,
            tokens_spec,
        ),
        out_specs=(
            tokens_spec,
            tokens_spec,
            P("fs"),
            block_spec,
            block_spec,
            block_spec,
            block_spec,
            P("fs"),
            block_spec,
            block_spec,
            block_spec,
        ),
        check_vma=False,
    )
```

```python
import functools
import math

import jax
import jax.numpy as jnp
from jax import lax
from jax.experimental import pallas as pl
from jax.experimental.pallas import tpu as pltpu
from jax.sharding import PartitionSpec as P

MODEL_WIDTH = 2560
QUERY_HEADS = 32
KEY_VALUE_HEADS = 8
HEAD_SIZE = 80
WINDOW = 1024
GROUPS = QUERY_HEADS // KEY_VALUE_HEADS
HALF = HEAD_SIZE // 2
KV_WIDTH = KEY_VALUE_HEADS * HEAD_SIZE
STRIP = 640
HALF_KV = KV_WIDTH // 2
SCALE = 1.0 / math.sqrt(HEAD_SIZE)

NORM_EPS = 1e-05
ROPE_THETA = 1000000.0
MASK_VALUE_FILL = -1e30
VMEM = 60 * 1024 * 1024
FEED_VMEM = 62 * 1024 * 1024
MESH = pl.DeviceIdType.MESH

NT = (((1,), (1,)), ((), ()))
TN = (((0,), (0,)), ((), ()))
NN = (((1,), (0,)), ((), ()))


def dot(left, right, dims):
    return lax.dot_general(left, right, dims, preferred_element_type=jnp.float32)


def params(**more):
    return pltpu.CompilerParams(vmem_limit_bytes=VMEM, **more)


def cost(flops, moved, exps=0):
    return pl.CostEstimate(flops=int(flops), bytes_accessed=int(moved), transcendentals=int(exps))


def turn(x, cosine, sine):
    width = x.shape[1]
    lane = lax.broadcasted_iota(jnp.int32, x.shape, 1) % HEAD_SIZE
    partner = jnp.where(
        lane < HALF, pltpu.roll(x, width - HALF, 1), pltpu.roll(x, HALF, 1)
    )
    return x * cosine + partner * sine


def toggled(me, k, count):
    found, bit = me, 1
    while bit < count:
        found = found + ((k // bit) % 2) * bit * (1 - 2 * ((me // bit) % 2))
        bit *= 2
    return found


def feed_kernel(
    peers, nt_ref, og_all, down_ref, gate_ref, up_ref,
    nt_all, gs_all, us_all, mid_all,
    nt_v, gs_v, us_v, mid_v, og_v, gate_v, up_v, down_v,
    load_sem, weight_sem, tile_sem, own_sem, keep_sem, nt_send, nt_recv,
):
    tokens = nt_ref.shape[0]
    inner = down_ref.shape[0]
    middle = tokens // 2
    square = peers == 4
    me = lax.axis_index("fs")
    bf16 = jnp.bfloat16

    def remote(src, dst, at, k):
        return pltpu.make_async_remote_copy(
            src_ref=src, dst_ref=dst, send_sem=nt_send.at[at], recv_sem=nt_recv.at[at],
            device_id={"fs": toggled(me, k, peers)}, device_id_type=MESH,
        )

    barrier = pltpu.get_barrier_semaphore()
    for k in range(1, peers):
        pl.semaphore_signal(barrier, inc=1, device_id={"fs": toggled(me, k, peers)}, device_id_type=MESH)
    pl.semaphore_wait(barrier, peers - 1)

    top, bottom, whole = pl.ds(0, middle), pl.ds(middle, middle), pl.ds(0, tokens)
    if square:
        spread = {}
        for k in (1, 2):
            spread[k] = remote(nt_ref.at[top], nt_v.at[k, top], k, k)
            spread[k + 4] = remote(nt_ref.at[bottom], nt_v.at[k, bottom], k + 4, k)
        for k in (1, 2, 5, 6):
            spread[k].start()
        spread[3] = remote(nt_v.at[1, top], nt_v.at[3, top], 3, 2)
        spread[0] = remote(nt_v.at[2, bottom], nt_v.at[3, bottom], 0, 1)
    else:
        spread = {k: remote(nt_ref, nt_v.at[k], k, k) for k in range(1, peers)}
        for copy in spread.values():
            copy.start()
    own = pltpu.make_async_copy(nt_ref, nt_v.at[0], own_sem.at[0])
    own.start()
    weights = [
        pltpu.make_async_copy(src, dst, weight_sem.at[i])
        for i, (src, dst) in enumerate(((gate_ref, gate_v), (up_ref, up_v), (down_ref, down_v)))
    ]
    for copy in weights:
        copy.start()

    def grads_of(k):
        return pltpu.make_async_copy(
            og_all.at[toggled(me, k, peers)], og_v.at[k % 2], load_sem.at[k % 2]
        )

    def keep(k):
        return pltpu.make_async_copy(nt_v.at[k], nt_all.at[k], keep_sem.at[k])

    grads_of(0).start()
    own.wait()
    for copy in weights:
        copy.wait()
    tile = 256 if inner % 256 == 0 else 128
    tiles = inner // tile

    def stores(unit, at):
        k, part = unit
        sem = 1 if part is bottom else 0
        return [
            pltpu.make_async_copy(src.at[part, at], dst.at[part, at], tile_sem.at[sem, i, at.start // tile])
            for i, (src, dst) in enumerate(
                (
                    (gs_v, gs_all.at[k]),
                    (us_v, us_all.at[k]),
                    (mid_v, mid_all.at[toggled(me, k, peers)]),
                )
            )
        ]

    def work(unit, before):
        k, part = unit

        def some(j, carry):
            at = pl.ds(pl.multiple_of(j * tile, tile), tile)
            gate = dot(nt_v[k, part], gate_v[:, at], NN)
            up = dot(nt_v[k, part], up_v[:, at], NN)
            grad = dot(og_v[k % 2, part], down_v[at, :], NT)
            sig = 1.0 / (1.0 + jnp.exp(-gate))
            silu = gate * sig
            for other in before:
                for copy in stores(other, at):
                    copy.wait()
            mid_v[part, at] = (silu * up).astype(bf16)
            gs_v[part, at] = (grad * up * sig * (1.0 + gate * (1.0 - sig))).astype(bf16)
            us_v[part, at] = (grad * silu).astype(bf16)
            for copy in stores(unit, at):
                copy.start()
            return carry

        lax.fori_loop(0, tiles, some, 0)

    keep(0).start()
    if square:
        grads_of(1).start()
        grads_of(0).wait()
        work((0, whole), [])
        grads_of(2).start()
        spread[1].wait_recv()
        spread[3].start()
        grads_of(1).wait()
        work((1, top), [(0, whole)])
        spread[2].wait_recv()
        grads_of(2).wait()
        work((2, top), [(1, top)])
        spread[5].wait_recv()
        spread[6].wait_recv()
        spread[0].start()
        keep(1).start()
        keep(2).start()
        work((1, bottom), [])
        grads_of(3).start()
        work((2, bottom), [(1, bottom)])
        spread[3].wait_recv()
        spread[0].wait_recv()
        keep(3).start()
        grads_of(3).wait()
        work((3, whole), [(2, top), (2, bottom)])
    else:
        for k in range(peers):
            if k > 0:
                spread[k].wait_recv()
                keep(k).start()
            grads_of(k).wait()
            if k + 1 < peers:
                grads_of(k + 1).start()
            work((k, whole), [(k - 1, whole)] if k > 0 else [])

    def settle(j, carry):
        at = pl.ds(pl.multiple_of(j * tile, tile), tile)
        for copy in stores((peers - 1, whole), at):
            copy.wait()
        return carry

    lax.fori_loop(0, tiles, settle, 0)
    for k in range(peers):
        keep(k).wait()
    for copy in spread.values():
        copy.wait_send()


def feed(peers, nt, og_all, down, gate, up):
    tokens, width = nt.shape
    inner = down.shape[0]
    bf = jnp.bfloat16
    S = jax.ShapeDtypeStruct
    any_ = pl.BlockSpec(memory_space=pl.ANY)
    DMA = pltpu.SemaphoreType.DMA
    inner_shape = S((peers, tokens, inner), bf)
    return pl.pallas_call(
        functools.partial(feed_kernel, peers),
        in_specs=[any_] * 5,
        out_specs=[any_] * 4,
        out_shape=[S((peers, tokens, width), bf), inner_shape, inner_shape, inner_shape],
        scratch_shapes=[
            pltpu.VMEM((peers, tokens, width), bf),
            pltpu.VMEM((tokens, inner), bf), pltpu.VMEM((tokens, inner), bf), pltpu.VMEM((tokens, inner), bf),
            pltpu.VMEM((2, tokens, width), bf),
            pltpu.VMEM((width, inner), bf), pltpu.VMEM((width, inner), bf), pltpu.VMEM((inner, width), bf),
            DMA((2,)), DMA((3,)), DMA((2, 3, 16)), DMA((1,)), DMA((peers,)),
            DMA((2 * peers,)), DMA((2 * peers,)),
        ],
        compiler_params=pltpu.CompilerParams(vmem_limit_bytes=FEED_VMEM, collective_id=1, has_side_effects=True),
        cost_estimate=cost(6 * peers * tokens * width * inner, 20 * width * inner, peers * tokens * inner),
    )(nt, og_all, down, gate, up)


def feed_back_kernel(
    peers, gs_all, us_all, mid_all, down_ref, gate_ref, up_ref,
    dn_own, dn_in, *rest,
):
    out_parts, rest = rest[:peers], rest[peers:]
    (gs_v, us_v, io, relay, out_v, gate_v, up_v, down_v,
     load_sem, weight_sem, out_sem, own_sem, dn_send, dn_recv) = rest
    tokens, inner = gs_v.shape[1:]
    width = gate_ref.shape[0]
    middle = tokens // 2
    square = peers == 4
    me = lax.axis_index("fs")
    bf16 = jnp.bfloat16

    def remote(src, dst, at, k):
        return pltpu.make_async_remote_copy(
            src_ref=src, dst_ref=dst, send_sem=dn_send.at[at], recv_sem=dn_recv.at[at],
            device_id={"fs": toggled(me, k, peers)}, device_id_type=MESH,
        )

    barrier = pltpu.get_barrier_semaphore()
    for k in range(1, peers):
        pl.semaphore_signal(barrier, inc=1, device_id={"fs": toggled(me, k, peers)}, device_id_type=MESH)
    pl.semaphore_wait(barrier, peers - 1)
    top, bottom = pl.ds(0, middle), pl.ds(middle, middle)

    def returns(k):
        if square and k == 3:
            return (remote(io.at[3, top], relay.at[0], 3, 1), remote(io.at[3, bottom], relay.at[1], 0, 2))
        parts = [pl.ds(0, width // 2), pl.ds(width // 2, width // 2)]
        return tuple(
            remote(io.at[k, :, part], dn_in.at[k - 1, :, part], k + i * peers, k)
            for i, part in enumerate(parts)
        )

    order = [peers - 1, 0] + list(range(peers - 2, 0, -1))
    weights = [
        pltpu.make_async_copy(src, dst, weight_sem.at[i])
        for i, (src, dst) in enumerate(((gate_ref, gate_v), (up_ref, up_v), (down_ref, down_v)))
    ]
    for copy in weights:
        copy.start()

    def slopes_of(turn):
        k, slot = order[turn], turn % 2
        return [
            pltpu.make_async_copy(src.at[k], dst.at[slot], load_sem.at[i, slot])
            for i, (src, dst) in enumerate(((gs_all, gs_v), (us_all, us_v)))
        ]

    def units_of(turn):
        slab, slot = toggled(me, order[turn], peers), turn % 2
        return pltpu.make_async_copy(mid_all.at[slab], gs_v.at[slot], load_sem.at[0, slot])

    for copy in slopes_of(0):
        copy.start()
    wide = 256
    strips = width // wide
    weights[0].wait()
    weights[1].wait()
    for turn, k in enumerate(order):
        slot = turn % 2
        for copy in slopes_of(turn):
            copy.wait()
        if turn + 1 < peers:
            for copy in slopes_of(turn + 1):
                copy.start()
        if square and k == 2:
            returns(3)[0].wait_recv()
        if square and k == 1:
            returns(3)[1].wait_recv()

        def more(j, carry, k=k, slot=slot):
            at = pl.ds(pl.multiple_of(j * wide, wide), wide)
            part = dot(gs_v[slot], gate_v[at, :], NT) + dot(us_v[slot], up_v[at, :], NT)
            if square and k == 2:
                io[k, top, at] = (part[:middle] + relay[0, :, at].astype(jnp.float32)).astype(bf16)
                io[k, bottom, at] = part[middle:].astype(bf16)
            elif square and k == 1:
                io[k, top, at] = part[:middle].astype(bf16)
                io[k, bottom, at] = (part[middle:] + relay[1, :, at].astype(jnp.float32)).astype(bf16)
            else:
                io[k, :, at] = part.astype(bf16)
            return carry

        if k == 0 or (square and k == 3):
            lax.fori_loop(0, strips, more, 0)
        else:
            lax.fori_loop(0, strips // 2, more, 0)
            returns(k)[0].start()
            lax.fori_loop(strips // 2, strips, more, 0)
            returns(k)[1].start()
        if k == 0:
            pltpu.make_async_copy(io.at[0], dn_own, own_sem.at[0]).start()
        elif square and k == 3:
            for copy in returns(k):
                copy.start()

    weights[2].wait()
    units_of(0).start()
    for turn, k in enumerate(order):
        slot = turn % 2
        units_of(turn).wait()
        if turn + 1 < peers:
            units_of(turn + 1).start()

        def out_copy(j, k=k):
            at = pl.ds(pl.multiple_of(j * wide, wide), wide)
            return pltpu.make_async_copy(out_v.at[j % 2], out_parts[k].at[:, at], out_sem.at[j % 2])

        def last(j, carry, slot=slot, out_copy=out_copy):
            at = pl.ds(pl.multiple_of(j * wide, wide), wide)
            found = dot(gs_v[slot], down_v[:, at], NN).astype(bf16)

            @pl.when(j >= 2)
            def _():
                out_copy(j - 2).wait()

            out_v[j % 2] = found
            out_copy(j).start()
            return carry

        lax.fori_loop(0, strips, last, 0)
        out_copy(strips - 2).wait()
        out_copy(strips - 1).wait()

    pltpu.make_async_copy(io.at[0], dn_own, own_sem.at[0]).wait()
    for k in range(1, peers):
        for copy in returns(k):
            copy.wait_send()
            if not (square and k == 3):
                copy.wait_recv()


def feed_back(peers, gs, us, mid, down, gate, up):
    tokens, inner = gs.shape[1:]
    width = gate.shape[0]
    bf = jnp.bfloat16
    S = jax.ShapeDtypeStruct
    any_ = pl.BlockSpec(memory_space=pl.ANY)
    DMA = pltpu.SemaphoreType.DMA
    halves = 2 if peers == 4 else peers - 1
    return pl.pallas_call(
        functools.partial(feed_back_kernel, peers),
        in_specs=[any_] * 6,
        out_specs=[any_] * (2 + peers),
        out_shape=[S((tokens, width), bf), S((halves, tokens, width), bf)] + [S((tokens, width), bf)] * peers,
        scratch_shapes=[
            pltpu.VMEM((2, tokens, inner), bf), pltpu.VMEM((2, tokens, inner), bf),
            pltpu.VMEM((peers, tokens, width), bf),
            pltpu.VMEM((2, tokens // 2, width), bf),
            pltpu.VMEM((2, tokens, 256), bf),
            pltpu.VMEM((width, inner), bf), pltpu.VMEM((width, inner), bf), pltpu.VMEM((inner, width), bf),
            DMA((2, 2)), DMA((3,)), DMA((2,)), DMA((1,)), DMA((2 * peers,)), DMA((2 * peers,)),
        ],
        compiler_params=pltpu.CompilerParams(vmem_limit_bytes=FEED_VMEM, collective_id=4, has_side_effects=True),
        cost_estimate=cost(6 * peers * tokens * width * inner, 20 * width * inner),
    )(gs, us, mid, down, gate, up)


def gate_fold_kernel(nt_ref, gs_ref, us_ref, gate_ref, up_ref):
    peers, tokens, block = nt_ref.shape
    inner = gs_ref.shape[2]
    total = peers * tokens
    turned = jnp.transpose(nt_ref[...].reshape(total, block))
    gate_ref[...] = dot(turned, gs_ref[...].reshape(total, inner), NN).astype(jnp.bfloat16)
    up_ref[...] = dot(turned, us_ref[...].reshape(total, inner), NN).astype(jnp.bfloat16)


def gate_fold(nt_all, gs, us):
    peers, tokens, width = nt_all.shape
    inner = gs.shape[2]
    block = 512
    fixed = pl.BlockSpec((peers, tokens, inner), lambda j: (0, 0, 0), pipeline_mode=pl.Buffered(1))
    return pl.pallas_call(
        gate_fold_kernel,
        grid=(width // block,),
        in_specs=[pl.BlockSpec((peers, tokens, block), lambda j: (0, 0, j)), fixed, fixed],
        out_specs=[pl.BlockSpec((block, inner), lambda j: (j, 0))] * 2,
        out_shape=[jax.ShapeDtypeStruct((width, inner), jnp.bfloat16)] * 2,
        compiler_params=params(),
        cost_estimate=cost(4 * peers * tokens * width * inner, 2 * (nt_all.size + 3 * gs.size)),
    )(nt_all, gs, us)


def down_fold_kernel(og_ref, mid_ref, out_ref):
    peers, tokens, tile = mid_ref.shape
    owned = out_ref.shape[2]
    turned = jnp.transpose(mid_ref[...].reshape(peers * tokens, tile))
    wide = og_ref.shape[2]
    acc = dot(turned, og_ref[...].reshape(peers * tokens, wide), NN).astype(jnp.bfloat16)
    for c in range(out_ref.shape[0]):
        out_ref[c] = acc[:, c * owned : (c + 1) * owned]


def down_fold(og_all, mid_all, chain):
    peers, tokens, width = og_all.shape
    inner = mid_all.shape[2]
    tile = 256 if inner % 256 == 0 else 128
    owned = width // chain
    wide = 1280
    return pl.pallas_call(
        down_fold_kernel,
        grid=(width // wide, inner // tile),
        in_specs=[
            pl.BlockSpec((peers, tokens, wide), lambda i, j: (0, 0, i)),
            pl.BlockSpec((peers, tokens, tile), lambda i, j: (0, 0, j)),
        ],
        out_specs=pl.BlockSpec((wide // owned, tile, owned), lambda i, j: (i, j, 0)),
        out_shape=jax.ShapeDtypeStruct((chain, inner, owned), jnp.bfloat16),
        compiler_params=params(),
        cost_estimate=cost(2 * peers * tokens * width * inner, 2 * (og_all.size + 3 * mid_all.size)),
    )(og_all, mid_all)


def front_kernel(peers, chain, count, batches, *refs):
    (hid, gains, q_w, k_w, v_w, o_w, gate_w, up_w, og, cos_ref, sin_ref, low_ref) = refs[:12]
    (w_in, o_full, gate_part, up_part, og_all, normed_o, q_o, line_o, sib_o, att_o, lse_o, gain_o) = refs[12:24]
    (w_v, nt_v, nt_b, q_v, att_v, line_v, sib_v, gains_v) = refs[24:32]
    (own_sem, out_sem, gain_s, gain_r, qkv_s, qkv_r, twin_s, twin_r, back_s, back_r,
     og_s, og_r, hop_s, hop_r, kin_s, kin_r) = refs[32:]
    tokens, width = nt_v.shape
    rows = q_w.shape[0]
    inner = gate_part.shape[1]
    length = tokens // batches
    slots = line_v.shape[0]
    window = count * length
    square = peers == 4
    bf16, f32 = jnp.bfloat16, jnp.float32
    me, place = lax.axis_index("fs"), lax.axis_index("ctx")
    core, plane = place % 2, place // 2
    parity = plane % 2
    twin = place + 1 - 2 * core
    partner = place + 2 - 4 * parity
    deep = place >= 2
    ahead = place + 2 < chain

    def send(src, dst, send_sem, recv_sem, target):
        return pltpu.make_async_remote_copy(
            src_ref=src, dst_ref=dst, send_sem=send_sem, recv_sem=recv_sem,
            device_id=target, device_id_type=MESH,
        )

    def owner(k):
        return toggled(me, k, peers)

    def along(k):
        return {"fs": owner(k)}

    for i in range(1, slots):

        @pl.when(plane < i)
        def _(i=i):
            line_v[i] = jnp.zeros(line_v.shape[1:], bf16)
            sib_v[i] = jnp.zeros(line_v.shape[1:], bf16)

    barrier = pltpu.get_barrier_semaphore()
    for k in range(1, peers):
        pl.semaphore_signal(barrier, inc=1, device_id=along(k), device_id_type=MESH)
    pl.semaphore_signal(barrier, inc=1, device_id={"ctx": twin}, device_id_type=MESH)

    @pl.when(deep)
    def _():
        pl.semaphore_signal(barrier, inc=1, device_id={"ctx": place - 2}, device_id_type=MESH)

    @pl.when(ahead)
    def _():
        pl.semaphore_signal(barrier, inc=1, device_id={"ctx": place + 2}, device_id_type=MESH)

    planes = chain // 2
    behind = (plane + planes - 1) // planes
    before = (2 * planes - 2 - plane) // planes
    pl.semaphore_wait(barrier, peers + behind + before)

    share = rows // 2
    half = share // 2
    mats = ((q_w, pl.ds(0, width)), (k_w, pl.ds(width, KV_WIDTH)), (v_w, pl.ds(width + KV_WIDTH, KV_WIDTH)))

    def block(k, at, size):
        return pl.ds(pl.multiple_of(owner(k) * rows + core * share + at, 16), size)

    def first_hop(k, m):
        src, cols = mats[m]
        mine = pl.ds(pl.multiple_of(core * share, 16), share)
        return send(src.at[mine, :], w_v.at[block(0, 0, share), cols], qkv_s.at[k, m], qkv_r.at[k, m], along(k))

    def relay(part, m):
        source, target = (1, 2) if part == 3 else (2, 1)
        where = w_v.at[block(source, 0 if part == 3 else half, half), mats[m][1]]
        return send(where, where, qkv_s.at[part, m], qkv_r.at[part, m], along(target))

    def to_twin(part, m):
        if square and part in (0, 3):
            rows_at = block(3, 0 if part == 3 else half, half)
        else:
            rows_at = block(part, 0, share)
        where = w_v.at[rows_at, mats[m][1]]
        return send(where, where, twin_s.at[part, m], twin_r.at[part, m], {"ctx": twin})

    reached = [1, 2] if square else list(range(1, peers))
    for k in reached:
        for m in range(3):
            first_hop(k, m).start()
    own_rows = pl.ds(pl.multiple_of(me * rows, 16), rows)
    own_loads = [
        pltpu.make_async_copy(src, w_v.at[own_rows, cols], own_sem.at[i])
        for i, (src, cols) in enumerate(mats)
    ]
    for copy in own_loads:
        copy.start()
    gain_moves = [send(gains, gains_v.at[me], gain_s.at[k], gain_r.at[k], along(k)) for k in range(1, peers)]
    for copy in gain_moves:
        copy.start()
    gains_v[me] = gains[...]
    for copy in gain_moves:
        copy.wait_recv()
    whole_gain = jnp.concatenate([gains_v[f] for f in range(peers)], axis=1)
    gain_o[...] = whole_gain

    chunk = 64

    def norm(i, carry):
        at = pl.ds(pl.multiple_of(i * chunk, chunk), chunk)
        x = hid[at, :].astype(f32)
        scale = lax.rsqrt(jnp.mean(x * x, axis=1, keepdims=True) + NORM_EPS)
        normed = (x * scale * whole_gain[0:1]).astype(bf16)
        nt_v[at, :] = normed
        for f in range(peers):
            nt_b[f, at, :] = normed[:, f * rows : (f + 1) * rows]
        return carry

    lax.fori_loop(0, tokens // chunk, norm, 0)
    normed_out = pltpu.make_async_copy(nt_v, normed_o, out_sem.at[0])
    normed_out.start()

    quarter = rows // 4
    sources = (o_w, gate_w, up_w)
    fulls = (o_full, gate_part, up_part)

    def region(m, k, c, p):
        return fulls[m].at[pl.ds(pl.multiple_of(owner(k) * rows + (c + 2 * p) * quarter, 16), quarter), :]

    def back_first(m, k):
        at = pl.ds(pl.multiple_of((core + 2 * parity) * quarter, 16), quarter)
        if m == 0:
            src = o_w.at[at, :]
        else:
            src = sources[m].at[at, pl.ds(pl.multiple_of(owner(k) * inner, 128), inner)]
        return send(src, region(m, 0, core, parity), back_s.at[0, m, k], back_r.at[0, m, k], along(k))

    def back_plane(m, k):
        where = region(m, k, core, parity)
        return send(where, where, back_s.at[1, m, k], back_r.at[1, m, k], {"ctx": partner})

    def back_twin(m, k, p, stage):
        where = region(m, k, core, p)
        return send(where, where, back_s.at[stage, m, k], back_r.at[stage, m, k], {"ctx": twin})

    others = range(1, peers)

    def spread_first(which):
        for m in which:
            for k in others:
                back_first(m, k).start()

    def spread_second(which):
        for m in which:
            for k in others:
                back_first(m, k).wait_recv()
                back_plane(m, k).start()
                back_twin(m, k, parity, 2).start()

    def spread_third(which):
        for m in which:
            for k in others:
                back_plane(m, k).wait_recv()
                back_twin(m, k, 1 - parity, 3).start()

    def og_hop(k):
        return send(og, og_all.at[me], og_s.at[k], og_r.at[k], along(k))

    middle = tokens // 2

    def og_relay(part):
        source, target = (1, 2) if part == 3 else (2, 1)
        where = og_all.at[owner(source), pl.ds(0 if part == 3 else middle, middle), :]
        return send(where, where, og_s.at[part], og_r.at[part], along(target))

    wide = STRIP
    tiles = w_v.shape[1] // wide

    def project(acc, bounce):
        def through(src, dst, sem):
            shape = src.shape
            there = bounce.at[pl.ds(0, shape[0]), pl.ds(0, shape[1])]
            copy = pltpu.make_async_copy(src, there, sem.at[3])
            copy.start()
            copy.wait()
            copy = pltpu.make_async_copy(there, dst, sem.at[4])
            copy.start()
            copy.wait()

        through(og, og_all.at[me], own_sem)
        through(o_w, o_full.at[own_rows, :], own_sem)
        mine = pl.ds(pl.multiple_of(me * inner, 128), inner)
        through(gate_w.at[:, mine], gate_part.at[own_rows, :], own_sem)
        through(up_w.at[:, mine], up_part.at[own_rows, :], own_sem)
        for copy in own_loads:
            copy.wait()

        def add(k):
            rows_at = pl.ds(pl.multiple_of(owner(k) * rows, 16), rows)

            def one(j, carry):
                at = pl.ds(pl.multiple_of(j * wide, wide), wide)
                part = dot(nt_b[owner(k)], w_v[rows_at, at], NN)
                acc[:, at] = part if k == 0 else acc[:, at] + part
                return carry

            lax.fori_loop(0, tiles, one, 0)

        add(0)
        if square:
            for k, part in ((1, 3), (2, 0)):
                for m in range(3):
                    first_hop(k, m).wait_recv()
                for m in range(3):
                    relay(part, m).start()
                    to_twin(k, m).start()
                if k == 2:
                    spread_first([0])
                for m in range(3):
                    to_twin(k, m).wait_recv()
                add(k)
            for part in (3, 0):
                for m in range(3):
                    relay(part, m).wait_recv()
                    to_twin(part, m).start()
            spread_first([1, 2])
            for k in (1, 2):
                og_hop(k).start()
            for part in (3, 0):
                for m in range(3):
                    to_twin(part, m).wait_recv()
            add(3)
        else:
            for k in others:
                for m in range(3):
                    first_hop(k, m).wait_recv()
                    to_twin(k, m).start()
                for m in range(3):
                    to_twin(k, m).wait_recv()
                add(k)
            spread_first([0, 1, 2])
            for k in others:
                og_hop(k).start()

        line_v[0, 0] = turn(acc[:, width : width + KV_WIDTH], cos_ref[...], sin_ref[...]).astype(bf16)
        line_v[0, 1] = acc[:, width + KV_WIDTH :].astype(bf16)

        @pl.when(ahead)
        def _():
            hop(0).start()

        kin(0).start()

        def finish(j, carry):
            at = pl.ds(pl.multiple_of(j * wide, wide), wide)
            q_v[:, at] = turn(acc[:, at], cos_ref[...], sin_ref[...]).astype(bf16)
            return carry

        lax.fori_loop(0, width // wide, finish, 0)

    def hop(i):
        return send(line_v.at[i], line_v.at[i + 1], hop_s.at[i], hop_r.at[i], {"ctx": place + 2})

    def kin(i):
        return send(line_v.at[i], sib_v.at[i], kin_s.at[i], kin_r.at[i], {"ctx": twin})

    pl.run_scoped(project, pltpu.VMEM((tokens, w_v.shape[1]), f32), pltpu.VMEM((rows, width), bf16))

    w_out = pltpu.make_async_copy(w_v, w_in, out_sem.at[1])
    w_out.start()
    q_out = pltpu.make_async_copy(q_v, q_o, out_sem.at[2])
    q_out.start()
    for i in range(1, slots):

        @pl.when(plane >= i)
        def _(i=i):
            hop(i - 1).wait_recv()
            kin(i).start()

        if i + 1 < slots:

            @pl.when((plane >= i) & ahead)
            def _(i=i):
                hop(i).start()

    kin(0).wait_recv()
    for i in range(1, slots):

        @pl.when(plane >= i)
        def _(i=i):
            kin(i).wait_recv()

    spread_second([0])
    line_out = pltpu.make_async_copy(line_v, line_o, out_sem.at[3])
    line_out.start()
    sib_out = pltpu.make_async_copy(sib_v, sib_o, out_sem.at[4])
    sib_out.start()

    def attention(keys, values, bias):
        for b in range(batches):
            here = pl.ds(b * length, length)
            for back in range(count):
                at_rows = pl.ds((count - 1 - back) * length, length)
                for kind, target in ((0, keys), (1, values)):
                    if back % 2 == 0:
                        found = line_v[back // 2, kind, here, :]
                    else:
                        found = sib_v[(back + 1) // 2 - core, kind, here, :]
                    for head in range(KEY_VALUE_HEADS):
                        target[head, at_rows, :] = found[:, head * HEAD_SIZE : (head + 1) * HEAD_SIZE]
            key_place = (place - count + 1) * length + lax.broadcasted_iota(jnp.int32, (length, window), 1)
            query_place = place * length + lax.broadcasted_iota(jnp.int32, (length, window), 0)
            seen = (key_place >= low_ref[b]) & (key_place <= query_place)
            bias[...] = jnp.where(seen, 0.0, MASK_VALUE_FILL)

            def pair_of_heads(pair, carry, b=b, here=here):
                cols = pl.ds(pl.multiple_of(pair * STRIP, STRIP), STRIP)
                strip = q_v[here, cols]
                mixed, sums = [], []
                for side in range(2):
                    key, value = keys[2 * pair + side], values[2 * pair + side]
                    for group in range(GROUPS):
                        at = (side * GROUPS + group) * HEAD_SIZE
                        scores = dot(strip[:, at : at + HEAD_SIZE], key, NT) * SCALE + bias[...]
                        peak = jnp.max(scores, axis=1, keepdims=True)
                        weights = jnp.exp(scores - peak)
                        total = jnp.sum(weights, axis=1, keepdims=True)
                        mixed.append(dot(weights.astype(bf16), value, NN) / total)
                        sums.append(peak + jnp.log(total))
                att_v[here, cols] = jnp.concatenate(mixed, axis=1).astype(bf16)
                spare = jnp.zeros((length, 128 - 2 * GROUPS), f32)
                turned = jnp.transpose(jnp.concatenate(sums + [spare], axis=1))
                lse_o[b, pair] = turned[: 2 * GROUPS]
                return carry

            lax.fori_loop(0, KEY_VALUE_HEADS // 2, pair_of_heads, 0)
            if b == 0:
                spread_second([1, 2])

    pl.run_scoped(
        attention,
        pltpu.VMEM((KEY_VALUE_HEADS, window, HEAD_SIZE), bf16),
        pltpu.VMEM((KEY_VALUE_HEADS, window, HEAD_SIZE), bf16),
        pltpu.VMEM((length, window), f32),
    )
    att_out = pltpu.make_async_copy(att_v, att_o, out_sem.at[5])
    att_out.start()
    spread_third([0])
    if square:
        for k, part in ((1, 3), (2, 0)):
            og_hop(k).wait_recv()
            og_relay(part).start()
    spread_third([1, 2])

    for copy in (normed_out, w_out, q_out, line_out, sib_out, att_out):
        copy.wait()
    for copy in gain_moves:
        copy.wait_send()
    for m in range(3):
        for k in reached:
            first_hop(k, m).wait_send()
            to_twin(k, m).wait_send()
        if square:
            for part in (3, 0):
                relay(part, m).wait_send()
                to_twin(part, m).wait_send()
    for k in reached:
        og_hop(k).wait_send()
        if not square:
            og_hop(k).wait_recv()
    if square:
        for part in (3, 0):
            og_relay(part).wait()
    for m in range(3):
        for k in others:
            back_first(m, k).wait_send()
            back_plane(m, k).wait_send()
            back_twin(m, k, parity, 2).wait()
            back_twin(m, k, 1 - parity, 3).wait()
    kin(0).wait_send()

    @pl.when(ahead)
    def _():
        hop(0).wait_send()

    for i in range(1, slots):

        @pl.when(plane >= i)
        def _(i=i):
            kin(i).wait_send()

        if i + 1 < slots:

            @pl.when((plane >= i) & ahead)
            def _(i=i):
                hop(i).wait_send()


def front(peers, chain, count, hidden, gains, weights, og, cosine, sine, low):
    batches, length, _ = low.shape
    tokens, width = hidden.shape
    rows = weights[0].shape[0]
    inner = weights[4].shape[1] // peers
    slots = (count - 1) // 2 + 1
    bf = jnp.bfloat16
    S = jax.ShapeDtypeStruct
    DMA = pltpu.SemaphoreType.DMA
    far = pl.BlockSpec(memory_space=pl.ANY)
    near = pl.BlockSpec(memory_space=pltpu.VMEM)
    whole = S((tokens, width), bf)
    line = (slots, 2, tokens, KV_WIDTH)
    return pl.pallas_call(
        functools.partial(front_kernel, peers, chain, count, batches),
        in_specs=[near, near] + [far] * 7 + [near] * 3,
        out_specs=[far] * 10 + [near, near],
        out_shape=[
            S((width, width + 2 * KV_WIDTH), bf),
            S((width, width), bf),
            S((width, inner), bf),
            S((width, inner), bf),
            S((peers, tokens, width), bf),
            whole,
            whole,
            S(line, bf),
            S(line, bf),
            whole,
            S((batches, KEY_VALUE_HEADS // 2, 2 * GROUPS, length), jnp.float32),
            S((8, width), jnp.float32),
        ],
        scratch_shapes=[
            pltpu.VMEM((width, width + 2 * KV_WIDTH), bf),
            pltpu.VMEM((tokens, width), bf),
            pltpu.VMEM((peers, tokens, rows), bf),
            pltpu.VMEM((tokens, width), bf),
            pltpu.VMEM((tokens, width), bf),
            pltpu.VMEM(line, bf),
            pltpu.VMEM(line, bf),
            pltpu.VMEM((peers, 8, rows), jnp.float32),
            DMA((5,)), DMA((6,)), DMA((peers,)), DMA((peers,)),
            DMA((peers, 3)), DMA((peers, 3)), DMA((peers, 3)), DMA((peers, 3)),
            DMA((4, 3, peers)), DMA((4, 3, peers)), DMA((peers,)), DMA((peers,)),
            DMA((slots,)), DMA((slots,)), DMA((slots,)), DMA((slots,)),
        ],
        compiler_params=pltpu.CompilerParams(
            vmem_limit_bytes=FEED_VMEM, collective_id=2, has_side_effects=True
        ),
        cost_estimate=cost(2 * tokens * width * 3840 * 10, 200 * tokens * width, QUERY_HEADS * tokens * count * length),
    )(hidden, gains, *weights, og, cosine, sine, low)


def back_kernel(peers, chain, count, batches, *refs):
    (normed, attended, d_attn, d_att, q_v, lse, low, cos_ref, sin_ref, scale, gain_two, line, sib, hid, w_in) = refs[:15]
    (slope_out, grad_o, grad_q, grad_kv, gain_out, far_o, far_q, far_kv, fs_o, fs_q, fs_kv, parts, odd_in, hop_in) = refs[15:29]
    (nb_o, z_o, z_q, z_kv, slopes_t, load_v, d_v, gain_v, gain_fs, gain_all) = refs[29:39]
    (far_s, far_r, fs_s, fs_r, zs_s, zs_r, load_sem, fsl_sem, part_sem, odd_s, odd_r, hop_s, hop_r, sum_sem, block_sem, gf_s, gf_r, ga_s, ga_r) = refs[39:]
    tokens, width = normed.shape
    rows = width // peers
    planes = chain // 2
    length = tokens // batches
    window = count * length
    reach = (count - 1) // 2
    bf16, f32 = jnp.bfloat16, jnp.float32
    me, place = lax.axis_index("fs"), lax.axis_index("ctx")
    core, plane = place % 2, place // 2
    twin = place + 1 - 2 * core
    deep, ahead = place >= 2, place + 2 < chain

    def send(src, dst, send_sem, recv_sem, target):
        return pltpu.make_async_remote_copy(
            src_ref=src, dst_ref=dst, send_sem=send_sem, recv_sem=recv_sem,
            device_id=target, device_id_type=MESH,
        )

    barrier = pltpu.get_barrier_semaphore()
    for k in range(1, peers):
        pl.semaphore_signal(barrier, inc=1, device_id={"fs": toggled(me, k, peers)}, device_id_type=MESH)
    for k in range(1, chain):
        pl.semaphore_signal(barrier, inc=1, device_id={"ctx": toggled(place, k, chain)}, device_id_type=MESH)
    pl.semaphore_wait(barrier, peers + chain - 2)

    kinds = {
        "o": (0, attended, far_o, fs_o, nb_o, z_o, grad_o),
    }

    def own_of(x):
        return kinds[x][2].shape[1]

    def turn_slopes(x):
        own = own_of(x)
        for p in range(planes):
            if x == "kv":
                half = own // 2
                sides = []
                for c in range(2):
                    at = (2 * p + c) * half
                    sides.append(
                        jnp.concatenate(
                            [
                                d_v[:, width + at : width + at + half],
                                d_v[:, width + KV_WIDTH + at : width + KV_WIDTH + at + half],
                            ],
                            axis=1,
                        )
                    )
            else:
                sides = [d_v[:, (2 * p + c) * own : (2 * p + c + 1) * own] for c in range(2)]
            first, second = (jnp.transpose(side.astype(f32)) for side in sides)
            slopes_t[0, p, :own] = jnp.where(core == 0, first, second).astype(bf16)
            slopes_t[1, p, :own] = jnp.where(core == 0, second, first).astype(bf16)

    def far_copy(x, t):
        i, _, far, _, nb, _, _ = kinds[x]
        return send(nb.at[t, pl.ds(0, own_of(x))], far.at[t], far_s.at[i, t], far_r.at[i, t], {"ctx": twin})

    def far_phase(x):
        _, left, _, _, nb, _, _ = kinds[x]
        own = own_of(x)
        for f in range(peers):

            def one(p, carry, f=f):
                t = f * planes + p
                part = dot(slopes_t[1, p, :own], left[:, f * rows : (f + 1) * rows], NN)
                nb[t, :own] = part.astype(bf16)
                far_copy(x, t).start()
                return carry

            lax.fori_loop(0, planes, one, 0)

    def fs_copy(x, f, p):
        i, _, _, fs, nb, _, _ = kinds[x]
        src = nb.at[f * planes + p, pl.ds(0, own_of(x))]
        return send(src, fs.at[me, p], fs_s.at[i, f, p], fs_r.at[i, me, p], {"fs": f})

    def fs_arrival(x, s, p):
        i, _, _, fs, nb, _, _ = kinds[x]
        src = nb.at[p, pl.ds(0, own_of(x))]
        return send(src, fs.at[s, p], fs_s.at[i, s, p], fs_r.at[i, s, p], {"fs": s})

    def near_phase(x):
        _, left, far, _, nb, _, _ = kinds[x]
        own = own_of(x)
        total = peers * planes

        def load(t):
            slot = t % 2
            return pltpu.make_async_copy(far.at[t], load_v.at[slot, pl.ds(0, own)], load_sem.at[slot])

        far_copy(x, 0).wait_recv()
        load(0).start()
        for f in range(peers):

            def one(p, carry, f=f):
                t = f * planes + p

                @pl.when(t + 1 < total)
                def _():
                    far_copy(x, t + 1).wait_recv()
                    load(t + 1).start()

                part = dot(slopes_t[0, p, :own], left[:, f * rows : (f + 1) * rows], NN)
                load(t).wait()
                far_copy(x, t).wait_send()
                nb[t, :own] = (part + load_v[t % 2, :own].astype(f32)).astype(bf16)

                @pl.when(f != me)
                def _():
                    fs_copy(x, f, p).start()

                return carry

            lax.fori_loop(0, planes, one, 0)

    def z_copy(x, p):
        i, _, _, _, nb, z, _ = kinds[x]
        src = nb.at[me * planes + p, pl.ds(0, own_of(x))]
        return send(src, z.at[plane], zs_s.at[i, p], zs_r.at[i, plane], {"ctx": 2 * p + core})

    def z_arrival(x, p):
        i, _, _, _, nb, z, _ = kinds[x]
        src = nb.at[me * planes + p, pl.ds(0, own_of(x))]
        return send(src, z.at[p], zs_s.at[i, p], zs_r.at[i, p], {"ctx": 2 * p + core})

    def z_phase(x, fs_load):
        _, _, _, fs, nb, _, tot = kinds[x]
        own = own_of(x)

        def one(p, carry):
            for s in range(peers):
                there = pltpu.make_async_copy(fs.at[s, p], fs_load.at[s, pl.ds(0, own)], fsl_sem.at[s])

                @pl.when(s != me)
                def _(s=s, there=there):
                    fs_arrival(x, s, p).wait_recv()
                    there.start()

            fs_load[me, :own] = nb[me * planes + p, :own]
            for s in range(peers):
                there = pltpu.make_async_copy(fs.at[s, p], fs_load.at[s, pl.ds(0, own)], fsl_sem.at[s])

                @pl.when(s != me)
                def _(there=there):
                    there.wait()

            total = fs_load[0, :own].astype(f32)
            for s in range(1, peers):
                total = total + fs_load[s, :own].astype(f32)

            @pl.when(p == plane)
            def _():
                tot[...] = total

            @pl.when(p != plane)
            def _():
                nb[me * planes + p, :own] = total.astype(bf16)
                z_copy(x, p).start()

            return carry

        lax.fori_loop(0, planes, one, 0)

    def finish(x):
        _, _, _, _, _, z, tot = kinds[x]
        total = tot[...]
        for p in range(planes):

            @pl.when(p != plane)
            def _(p=p):
                z_arrival(x, p).wait_recv()

            @pl.when(p == plane)
            def _(p=p):
                z[p] = jnp.zeros(z.shape[1:], bf16)

            total = total + z[p].astype(f32)
        tot[...] = total

    def settle(x):
        for p in range(planes):
            for f in range(peers):

                @pl.when(f != me)
                def _(f=f, p=p):
                    fs_copy(x, f, p).wait_send()

            @pl.when(p != plane)
            def _(p=p):
                z_copy(x, p).wait_send()

    def part_store(b, part_v):
        return pltpu.make_async_copy(part_v, parts.at[:, :, pl.ds(b * length, length)], part_sem.at[0])

    def attention(keys, values, bias, key_sums, value_sums, part_v, block_v):
        def one_batch(b):
            here = pl.ds(b * length, length)

            def fetch(back):
                if back % 2 == 0:
                    src = line.at[back // 2, :, here]
                else:
                    src = sib.at[(back + 1) // 2 - core, :, here]
                return pltpu.make_async_copy(src, block_v.at[back % 2], block_sem.at[back % 2])

            fetch(0).start()
            for back in range(count):
                if back + 1 < count:
                    fetch(back + 1).start()
                fetch(back).wait()
                at_rows = pl.ds((count - 1 - back) * length, length)
                for kind, target in ((0, keys), (1, values)):
                    found = block_v[back % 2, kind]
                    for head in range(KEY_VALUE_HEADS):
                        target[head, at_rows, :] = found[:, head * HEAD_SIZE : (head + 1) * HEAD_SIZE]
            key_place = (place - count + 1) * length + lax.broadcasted_iota(jnp.int32, (window, length), 0)
            query_place = place * length + lax.broadcasted_iota(jnp.int32, (window, length), 1)
            seen = (key_place >= low[b]) & (key_place <= query_place)
            bias[...] = jnp.where(seen, 0.0, MASK_VALUE_FILL)

            def pair_of_heads(pair, carry):
                cols = pl.ds(pl.multiple_of(pair * STRIP, STRIP), STRIP)
                strip, slope = q_v[here, cols], d_att[here, cols]
                products = slope.astype(f32) * attended[here, cols].astype(f32)
                heads = [
                    jnp.sum(products[:, h * HEAD_SIZE : (h + 1) * HEAD_SIZE], axis=1, keepdims=True)
                    for h in range(2 * GROUPS)
                ]
                spare = jnp.zeros((length, 128 - 2 * GROUPS), f32)
                deltas = jnp.transpose(jnp.concatenate(heads + [spare], axis=1))
                sums = lse[b, pair]
                turned = []
                for side in range(2):
                    key, value = keys[2 * pair + side], values[2 * pair + side]
                    key_sum = jnp.zeros((window, HEAD_SIZE), f32)
                    value_sum = jnp.zeros((window, HEAD_SIZE), f32)
                    for group in range(GROUPS):
                        row = side * GROUPS + group
                        query = strip[:, row * HEAD_SIZE : (row + 1) * HEAD_SIZE]
                        gradient = slope[:, row * HEAD_SIZE : (row + 1) * HEAD_SIZE]
                        chances = jnp.exp(dot(key, query, NT) * SCALE + bias[...] - sums[row : row + 1, :])
                        value_sum = value_sum + dot(chances.astype(bf16), gradient, NN)
                        steep = dot(value, gradient, NT) - deltas[row : row + 1, :]
                        steep = (chances * steep).astype(bf16)
                        key_sum = key_sum + dot(steep, query, NN)
                        turned.append(dot(steep, key, TN) * SCALE)
                    key_sums[2 * pair + side] = (key_sum * SCALE).astype(bf16)
                    value_sums[2 * pair + side] = value_sum.astype(bf16)
                whole = jnp.concatenate(turned, axis=1)
                d_v[here, cols] = turn(whole, cos_ref[here, :], -sin_ref[here, :]).astype(bf16)
                return carry

            lax.fori_loop(0, KEY_VALUE_HEADS // 2, pair_of_heads, 0)
            if b > 0:
                part_store(b - 1, part_v).wait()
            for back in range(count):
                at_rows = pl.ds((count - 1 - back) * length, length)
                for kind, found in ((0, key_sums), (1, value_sums)):
                    part_v[back, kind] = jnp.concatenate(
                        [found[h, at_rows, :] for h in range(KEY_VALUE_HEADS)], axis=1
                    )
            part_store(b, part_v).start()

        for b in range(batches):
            one_batch(b)
            if b == 0:
                near_phase("o")
        part_store(batches - 1, part_v).wait()

    def odd_copy(i):
        return send(parts.at[2 * i + 1], odd_in.at[i], odd_s.at[i], odd_r.at[i], {"ctx": twin})

    def hop_copy(step, sum_v):
        return send(sum_v.at[3 + step % 2], hop_in.at[step], hop_s.at[step], hop_r.at[step], {"ctx": place - 2})

    def gathered(step, sum_v):
        def fill(slot, src, sem):
            return pltpu.make_async_copy(src, sum_v.at[slot], sum_sem.at[sem])

        fill(0, parts.at[2 * step], 0).start()
        fill(0, parts.at[2 * step], 0).wait()
        if step < reach:

            @pl.when(core == 0)
            def _():
                fill(1, odd_in.at[step], 1).start()
                fill(1, odd_in.at[step], 1).wait()

        else:

            @pl.when(core == 0)
            def _():
                sum_v[1] = jnp.zeros(sum_v.shape[1:], bf16)

        if step > 0:

            @pl.when(core == 1)
            def _():
                fill(1, odd_in.at[step - 1], 1).start()
                fill(1, odd_in.at[step - 1], 1).wait()

        else:

            @pl.when(core == 1)
            def _():
                sum_v[1] = jnp.zeros(sum_v.shape[1:], bf16)

    def hop_out(step, sum_v):
        gathered(step, sum_v)
        if step < reach:

            @pl.when(ahead)
            def _():
                hop_copy(step + 1, sum_v).wait_recv()
                came = pltpu.make_async_copy(hop_in.at[step + 1], sum_v.at[2], sum_sem.at[2])
                came.start()
                came.wait()

            @pl.when(place + 2 >= chain)
            def _():
                sum_v[2] = jnp.zeros(sum_v.shape[1:], bf16)

        small = tokens // 4

        def one(i, carry):
            at = pl.ds(pl.multiple_of((i % 4) * small, small), small)
            kind = i // 4
            total = sum_v[0, kind, at, :].astype(f32) + sum_v[1, kind, at, :].astype(f32)
            if step < reach:
                total = total + sum_v[2, kind, at, :].astype(f32)
            if step > 0:
                sum_v[3 + step % 2, kind, at, :] = total.astype(bf16)
            else:

                @pl.when(kind == 0)
                def _():
                    turned = turn(total, cos_ref[at, :], -sin_ref[at, :])
                    d_v[at, width : width + KV_WIDTH] = turned.astype(bf16)

                @pl.when(kind == 1)
                def _():
                    d_v[at, width + KV_WIDTH :] = total.astype(bf16)

            return carry

        if step > 0 and step + 2 <= reach:

            @pl.when(deep)
            def _():
                hop_copy(step + 2, sum_v).wait_send()

        lax.fori_loop(0, 8, one, 0)
        if step > 0:

            @pl.when(deep)
            def _():
                hop_copy(step, sum_v).start()

    first_load = pltpu.make_async_copy(d_attn, d_v.at[:, pl.ds(0, width)], load_sem.at[0])
    first_load.start()
    first_load.wait()
    turn_slopes("o")
    far_phase("o")
    pl.run_scoped(
        attention,
        pltpu.VMEM((KEY_VALUE_HEADS, window, HEAD_SIZE), bf16),
        pltpu.VMEM((KEY_VALUE_HEADS, window, HEAD_SIZE), bf16),
        pltpu.VMEM((window, length), f32),
        pltpu.VMEM((KEY_VALUE_HEADS, window, HEAD_SIZE), bf16),
        pltpu.VMEM((KEY_VALUE_HEADS, window, HEAD_SIZE), bf16),
        pltpu.VMEM((count, 2, length, KV_WIDTH), bf16),
        pltpu.VMEM((2, 2, length, KV_WIDTH), bf16),
    )
    def remainder(nb_q, nb_kv, sum_v, fs_load):
        kinds["q"] = (1, normed, far_q, fs_q, nb_q, z_q, grad_q)
        kinds["kv"] = (2, normed, far_kv, fs_kv, nb_kv, z_kv, grad_kv)
        for i in range(reach):
            odd_copy(i).start()
        turn_slopes("q")
        far_phase("q")
        for i in range(reach):
            odd_copy(i).wait_recv()
        hop_out(reach, sum_v)
        near_phase("q")
        for step in range(reach - 1, 0, -1):
            hop_out(step, sum_v)
        hop_out(0, sum_v)
        turn_slopes("kv")
        far_phase("kv")

        def slope_body(w_block, h_block, out):
            found = dot(d_v[...], w_block[...], NT)
            out[...] = found
            at = pl.ds(pl.multiple_of(pl.program_id(0) * 256, 256), 256)
            gain_v[0:1, at] = jnp.sum(found * h_block[...].astype(f32) * scale[...], axis=0, keepdims=True)

        pltpu.emit_pipeline(
            slope_body,
            grid=(width // 256,),
            in_specs=[
                pl.BlockSpec((256, w_in.shape[1]), lambda j: (j, 0)),
                pl.BlockSpec((tokens, 256), lambda j: (0, j)),
            ],
            out_specs=[pl.BlockSpec((tokens, 256), lambda j: (0, j))],
        )(w_in, hid, slope_out)
        gain_v[1:2, :] = gain_two[...]
        near_phase("kv")
        z_phase("o", fs_load)

        for f in range(peers):
            gain_fs[f, 0:2] = gain_v[0:2, f * rows : (f + 1) * rows]

        def gain_hop(f):
            return send(gain_fs.at[f], gain_all.at[chain + me], gf_s.at[f], gf_r.at[me], {"fs": f})

        def gain_arrival(s):
            return send(gain_fs.at[s], gain_all.at[chain + s], gf_s.at[s], gf_r.at[s], {"fs": s})

        for f in range(peers):

            @pl.when(f != me)
            def _(f=f):
                gain_hop(f).start()

        mine = gain_fs[me]
        for s in range(peers):

            @pl.when(s != me)
            def _(s=s):
                gain_arrival(s).wait_recv()

            @pl.when(s == me)
            def _(s=s):
                gain_all[chain + s] = jnp.zeros(gain_all.shape[1:], f32)

            mine = mine + gain_all[chain + s]
        gain_all[place] = mine

        def gain_spread(k):
            return send(gain_all.at[place], gain_all.at[place], ga_s.at[k], ga_r.at[k], {"ctx": toggled(place, k, chain)})

        for k in range(1, chain):
            gain_spread(k).start()
        z_phase("q", fs_load)
        for k in range(1, chain):
            gain_spread(k).wait_recv()
        total = gain_all[0]
        for c in range(1, chain):
            total = total + gain_all[c]
        gain_out[...] = total
        z_phase("kv", fs_load)
        finish("o")
        finish("q")
        finish("kv")

        settle("o")
        settle("q")
        settle("kv")
        for i in range(reach):
            odd_copy(i).wait_send()
        for step in range(min(reach, 2), 0, -1):

            @pl.when(deep)
            def _(step=step):
                hop_copy(step, sum_v).wait_send()

        for f in range(peers):

            @pl.when(f != me)
            def _(f=f):
                gain_hop(f).wait_send()

        for k in range(1, chain):
            gain_spread(k).wait_send()

    pl.run_scoped(
        remainder,
        pltpu.VMEM(nb_o.shape, bf16),
        pltpu.VMEM((nb_o.shape[0],) + z_kv.shape[1:], bf16),
        pltpu.VMEM((5, 2, tokens, KV_WIDTH), bf16),
        pltpu.VMEM((peers,) + z_o.shape[1:], bf16),
    )


def back(peers, chain, count, normed, attended, d_attn, d_att, queries, lse, low, cosine, sine, scale, gain_two, line, sib, hidden, w_in):
    tokens, width = normed.shape
    batches = low.shape[0]
    length = tokens // batches
    window = count * length
    planes, rows = chain // 2, width // peers
    own, own_kv = width // chain, 2 * KV_WIDTH // chain
    reach = (count - 1) // 2
    bf, f32 = jnp.bfloat16, jnp.float32
    S = jax.ShapeDtypeStruct
    DMA = pltpu.SemaphoreType.DMA
    far = pl.BlockSpec(memory_space=pl.ANY)
    near = pl.BlockSpec(memory_space=pltpu.VMEM)
    tiles = peers * planes
    return pl.pallas_call(
        functools.partial(back_kernel, peers, chain, count, batches),
        in_specs=[near, near, far] + [near] * 8 + [far] * 4,
        out_specs=[far] + [near] * 4 + [far] * 9,
        out_shape=[
            S((tokens, width), f32),
            S((own, rows), f32),
            S((own, rows), f32),
            S((own_kv, rows), f32),
            S((8, rows), f32),
            S((tiles, own, rows), bf),
            S((tiles, own, rows), bf),
            S((tiles, own_kv, rows), bf),
            S((peers, planes, own, rows), bf),
            S((peers, planes, own, rows), bf),
            S((peers, planes, own_kv, rows), bf),
            S((count, 2, tokens, KV_WIDTH), bf),
            S((reach, 2, tokens, KV_WIDTH), bf),
            S((reach + 1, 2, tokens, KV_WIDTH), bf),
        ],
        scratch_shapes=[
            pltpu.VMEM((tiles, own, rows), bf),
            pltpu.VMEM((planes, own, rows), bf),
            pltpu.VMEM((planes, own, rows), bf),
            pltpu.VMEM((planes, own_kv, rows), bf),
            pltpu.VMEM((2, planes, own, tokens), bf),
            pltpu.VMEM((2, own, rows), bf),
            pltpu.VMEM((tokens, width + 2 * KV_WIDTH), bf),
            pltpu.VMEM((8, width), f32),
            pltpu.VMEM((peers, 8, rows), f32),
            pltpu.VMEM((chain + peers, 8, rows), f32),
            DMA((3, tiles)), DMA((3, tiles)), DMA((3, peers, planes)), DMA((3, peers, planes)),
            DMA((3, planes)), DMA((3, planes)), DMA((2,)), DMA((peers,)), DMA((1,)),
            DMA((reach,)), DMA((reach,)), DMA((reach + 1,)), DMA((reach + 1,)), DMA((3,)), DMA((2,)),
            DMA((peers,)), DMA((peers,)), DMA((chain,)), DMA((chain,)),
        ],
        compiler_params=pltpu.CompilerParams(
            vmem_limit_bytes=FEED_VMEM, collective_id=3, has_side_effects=True
        ),
        cost_estimate=cost(2 * tokens * width * 3840 * 20, 200 * tokens * width, QUERY_HEADS * tokens * window),
    )(normed, attended, d_attn, d_att, queries, lse, low, cosine, sine, scale, gain_two, line, sib, hidden, w_in)


def boundaries(lengths, positions):
    cut_points = jnp.cumsum(lengths)[:-1]
    passed = positions[:, None] >= cut_points[None, :]
    return jnp.max(jnp.where(passed, cut_points[None, :], 0), axis=1)


def matmul(left, right):
    return dot(left, right, NN)


def matmul_back(gradient, weight):
    return dot(gradient, weight, NT)


def on_device(
    hidden_in,
    doc_lengths,
    attn_gain,
    query_weight,
    key_matrix,
    value_matrix,
    output_weight,
    mlp_gain,
    gate_weight,
    up_weight,
    down_weight,
    out_grad,
):
    owners, chain = lax.axis_size("fs"), lax.axis_size("ctx")
    owner, place = lax.axis_index("fs"), lax.axis_index("ctx")
    core = place % 2
    planes = chain // 2
    batches, length, width = hidden_in.shape
    tokens = batches * length
    rows = query_weight.shape[0]
    inner = down_weight.shape[0]
    count = min(WINDOW // length + 1, chain)

    def across(x, k):
        return lax.ppermute(x, "fs", [(i, i ^ k) for i in range(owners)])

    grads_in = out_grad.reshape(tokens, width)

    positions = place * length + jnp.arange(length, dtype=jnp.int32)
    starts = jax.vmap(lambda lengths: boundaries(lengths, positions))(doc_lengths)
    low = jnp.maximum(starts, positions[None, :] - (WINDOW - 1))
    frequency = ROPE_THETA ** (-2.0 * jnp.arange(HALF, dtype=jnp.float32) / HEAD_SIZE)
    turns = (positions[None, :] - starts).reshape(tokens).astype(jnp.float32)
    angles = turns[:, None] * frequency[None, :]
    cosine, sine = jnp.cos(angles), jnp.sin(angles)
    cosine = jnp.tile(jnp.concatenate([cosine, cosine], axis=1), (1, STRIP // HEAD_SIZE))
    sine = jnp.tile(jnp.concatenate([-sine, sine], axis=1), (1, STRIP // HEAD_SIZE))

    gains = jnp.concatenate([jnp.stack([attn_gain, mlp_gain]).astype(jnp.float32), jnp.zeros((6, rows))])
    (
        in_full, out_full, gate_full, up_full, grads_all, normed, queries, line, kin, attended_rows, lse, gain_rows
    ) = front(
        owners,
        chain,
        count,
        hidden_in.reshape(tokens, width),
        gains,
        (query_weight, key_matrix, value_matrix, output_weight, gate_weight, up_weight),
        grads_in,
        cosine,
        sine,
        low[:, :, None],
    )
    gain_one, gain_two = gain_rows[0], gain_rows[1]

    x = hidden_in.reshape(tokens, width).astype(jnp.float32)
    scale_one = lax.rsqrt(jnp.mean(x * x, axis=1, keepdims=True) + NORM_EPS)
    projected = matmul(attended_rows, out_full)
    residual = x + projected
    scale_two = lax.rsqrt(jnp.mean(residual * residual, axis=1, keepdims=True) + NORM_EPS)
    normed_two = (residual * scale_two * gain_two).astype(jnp.bfloat16)

    normed_all, gate_slopes, up_slopes, mid = feed(
        owners, normed_two, grads_all, down_weight, gate_full, up_full
    )
    gate_part, up_part = gate_fold(normed_all, gate_slopes, up_slopes)
    gate_slopes, up_slopes, gate_part, up_part = lax.optimization_barrier(
        (gate_slopes, up_slopes, gate_part, up_part)
    )
    own_part, in_parts, *out_parts = feed_back(
        owners, gate_slopes, up_slopes, mid, down_weight, gate_full, up_full
    )
    came = [across(out_parts[k], k) for k in range(1, owners)]
    normed_two_grad = own_part.astype(jnp.float32) + jnp.sum(in_parts.astype(jnp.float32), axis=0)

    spans = chain // owners
    gate_mine = lax.psum_scatter(gate_part, "ctx", scatter_dimension=0, tiled=True)
    up_mine = lax.psum_scatter(up_part, "ctx", scatter_dimension=0, tiled=True)
    mid = lax.optimization_barrier((mid, own_part))[0]
    down_part = down_fold(grads_all, mid, chain)
    down_grad = lax.psum_scatter(down_part, "ctx", scatter_dimension=0, tiled=True)[0]
    down_grad = down_grad.astype(jnp.float32)
    slot = place % spans
    strip = inner // spans
    pieces = []
    for k in range(spans):
        cut = ((slot + k) % spans) * strip
        piece = [lax.dynamic_slice_in_dim(m, cut, strip, 1) for m in (gate_mine, up_mine)]
        pieces.append(jnp.stack(piece))

    scaled_two = normed_two_grad * gain_two
    residual_grad = grads_in.astype(jnp.float32) + scale_two * (
        scaled_two
        - residual * scale_two * scale_two * jnp.mean(scaled_two * residual, axis=1, keepdims=True)
    )
    gain_two_part = jnp.sum(normed_two_grad * residual * scale_two, axis=0)
    attn_grad = residual_grad.astype(jnp.bfloat16)
    attended_grad = matmul_back(attn_grad, out_full).astype(jnp.bfloat16)
    attended_grad, *pieces = lax.optimization_barrier((attended_grad, *pieces))
    moved = []
    for k in range(spans):
        moves = [
            (f * chain + c, (c // spans) * chain + f * spans + (c % spans + k) % spans)
            for f in range(owners)
            for c in range(chain)
        ]
        moved.append(lax.ppermute(pieces[k], ("fs", "ctx"), moves))
    ended = back(
        owners,
        chain,
        count,
        normed,
        attended_rows,
        attn_grad,
        attended_grad,
        queries,
        lse,
        low[:, None, :],
        cosine,
        sine,
        scale_one,
        gain_two_part[None, :],
        line,
        kin,
        hidden_in.reshape(tokens, width),
        in_full,
    )
    normed_grad, output_turned, query_turned, kv_turned, gain_grads = ended[:5]
    residual_late = lax.optimization_barrier((residual, normed_grad))[0]
    hidden_out = residual_late + out_parts[0].astype(jnp.float32)
    for part in came:
        hidden_out = hidden_out + part.astype(jnp.float32)
    output_grad, query_grad = output_turned.T, query_turned.T
    kv_own = KV_WIDTH // chain
    key_grad, value_grad = kv_turned[:kv_own].T, kv_turned[kv_own:].T
    gate_grad = jnp.zeros((spans,) + (gate_mine.shape[0], strip), jnp.float32)
    up_grad = gate_grad
    for k in range(spans):
        piece = moved[k].astype(jnp.float32)
        to = (slot - k) % spans
        gate_grad = lax.dynamic_update_slice_in_dim(gate_grad, piece[:1], to, 0)
        up_grad = lax.dynamic_update_slice_in_dim(up_grad, piece[1:], to, 0)
    gate_grad = gate_grad.reshape(rows, strip)
    up_grad = up_grad.reshape(rows, strip)
    scaled_one = normed_grad * gain_one
    hidden_grad = residual_grad + scale_one * (
        scaled_one - x * scale_one * scale_one * jnp.mean(scaled_one * x, axis=1, keepdims=True)
    )
    return (
        hidden_out.reshape(batches, length, width),
        hidden_grad.reshape(batches, length, width),
        gain_grads[0],
        query_grad,
        key_grad,
        value_grad,
        output_grad,
        gain_grads[1],
        gate_grad,
        up_grad,
        down_grad,
    )


def solution(mesh):
    tokens_spec = P("fs", "ctx", None)
    rows_spec = P("fs", None)
    block_spec = P("fs", "ctx")
    return jax.shard_map(
        on_device,
        mesh=mesh,
        in_specs=(
            tokens_spec,
            rows_spec,
            P("fs"),
            rows_spec,
            rows_spec,
            rows_spec,
            rows_spec,
            P("fs"),
            rows_spec,
            rows_spec,
            rows_spec,
            tokens_spec,
        ),
        out_specs=(
            tokens_spec,
            tokens_spec,
            P("fs"),
            block_spec,
            block_spec,
            block_spec,
            block_spec,
            P("fs"),
            block_spec,
            block_spec,
            block_spec,
        ),
        check_vma=False,
    )
```

```python
import functools
import math

import jax
import jax.numpy as jnp
from jax import lax
from jax.experimental import pallas as pl
from jax.experimental.pallas import tpu as pltpu
from jax.sharding import PartitionSpec as P

MODEL_WIDTH = 2560
QUERY_HEADS = 32
KEY_VALUE_HEADS = 8
HEAD_SIZE = 80
WINDOW = 1024
GROUPS = QUERY_HEADS // KEY_VALUE_HEADS
HALF = HEAD_SIZE // 2
KV_WIDTH = KEY_VALUE_HEADS * HEAD_SIZE
STRIP = 640
HALF_KV = KV_WIDTH // 2
SCALE = 1.0 / math.sqrt(HEAD_SIZE)

NORM_EPS = 1e-05
ROPE_THETA = 1000000.0
MASK_VALUE_FILL = -1e30
VMEM = 60 * 1024 * 1024
FEED_VMEM = 62 * 1024 * 1024
MESH = pl.DeviceIdType.MESH

NT = (((1,), (1,)), ((), ()))
TN = (((0,), (0,)), ((), ()))
NN = (((1,), (0,)), ((), ()))


def dot(left, right, dims):
    return lax.dot_general(left, right, dims, preferred_element_type=jnp.float32)


def params(**more):
    return pltpu.CompilerParams(vmem_limit_bytes=VMEM, **more)


def cost(flops, moved, exps=0):
    return pl.CostEstimate(flops=int(flops), bytes_accessed=int(moved), transcendentals=int(exps))


def turn(x, cosine, sine):
    width = x.shape[1]
    lane = lax.broadcasted_iota(jnp.int32, x.shape, 1) % HEAD_SIZE
    partner = jnp.where(
        lane < HALF, pltpu.roll(x, width - HALF, 1), pltpu.roll(x, HALF, 1)
    )
    return x * cosine + partner * sine


def toggled(me, k, count):
    found, bit = me, 1
    while bit < count:
        found = found + ((k // bit) % 2) * bit * (1 - 2 * ((me // bit) % 2))
        bit *= 2
    return found


def feed_kernel(
    peers, nt_ref, og_all, down_ref, gate_ref, up_ref,
    nt_all, gs_all, us_all, mid_all,
    nt_v, gs_v, us_v, mid_v, og_v, gate_v, up_v, down_v,
    load_sem, weight_sem, tile_sem, own_sem, keep_sem, nt_send, nt_recv,
):
    tokens = nt_ref.shape[0]
    inner = down_ref.shape[0]
    middle = tokens // 2
    square = peers == 4
    me = lax.axis_index("fs")
    bf16 = jnp.bfloat16

    def remote(src, dst, at, k):
        return pltpu.make_async_remote_copy(
            src_ref=src, dst_ref=dst, send_sem=nt_send.at[at], recv_sem=nt_recv.at[at],
            device_id={"fs": toggled(me, k, peers)}, device_id_type=MESH,
        )

    barrier = pltpu.get_barrier_semaphore()
    for k in range(1, peers):
        pl.semaphore_signal(barrier, inc=1, device_id={"fs": toggled(me, k, peers)}, device_id_type=MESH)
    pl.semaphore_wait(barrier, peers - 1)

    top, bottom, whole = pl.ds(0, middle), pl.ds(middle, middle), pl.ds(0, tokens)
    if square:
        spread = {}
        for k in (1, 2):
            spread[k] = remote(nt_ref.at[top], nt_v.at[k, top], k, k)
            spread[k + 4] = remote(nt_ref.at[bottom], nt_v.at[k, bottom], k + 4, k)
        for k in (1, 2, 5, 6):
            spread[k].start()
        spread[3] = remote(nt_v.at[1, top], nt_v.at[3, top], 3, 2)
        spread[0] = remote(nt_v.at[2, bottom], nt_v.at[3, bottom], 0, 1)
    else:
        spread = {k: remote(nt_ref, nt_v.at[k], k, k) for k in range(1, peers)}
        for copy in spread.values():
            copy.start()
    own = pltpu.make_async_copy(nt_ref, nt_v.at[0], own_sem.at[0])
    own.start()
    weights = [
        pltpu.make_async_copy(src, dst, weight_sem.at[i])
        for i, (src, dst) in enumerate(((gate_ref, gate_v), (up_ref, up_v), (down_ref, down_v)))
    ]
    for copy in weights:
        copy.start()

    def grads_of(k):
        return pltpu.make_async_copy(
            og_all.at[toggled(me, k, peers)], og_v.at[k % 2], load_sem.at[k % 2]
        )

    def keep(k):
        return pltpu.make_async_copy(nt_v.at[k], nt_all.at[k], keep_sem.at[k])

    grads_of(0).start()
    own.wait()
    for copy in weights:
        copy.wait()
    tile = 256 if inner % 256 == 0 else 128
    tiles = inner // tile

    def stores(unit, at):
        k, part = unit
        sem = 1 if part is bottom else 0
        return [
            pltpu.make_async_copy(src.at[part, at], dst.at[part, at], tile_sem.at[sem, i, at.start // tile])
            for i, (src, dst) in enumerate(
                (
                    (gs_v, gs_all.at[k]),
                    (us_v, us_all.at[k]),
                    (mid_v, mid_all.at[toggled(me, k, peers)]),
                )
            )
        ]

    def work(unit, before):
        k, part = unit

        def some(j, carry):
            at = pl.ds(pl.multiple_of(j * tile, tile), tile)
            gate = dot(nt_v[k, part], gate_v[:, at], NN)
            up = dot(nt_v[k, part], up_v[:, at], NN)
            grad = dot(og_v[k % 2, part], down_v[at, :], NT)
            sig = 1.0 / (1.0 + jnp.exp(-gate))
            silu = gate * sig
            for other in before:
                for copy in stores(other, at):
                    copy.wait()
            mid_v[part, at] = (silu * up).astype(bf16)
            gs_v[part, at] = (grad * up * sig * (1.0 + gate * (1.0 - sig))).astype(bf16)
            us_v[part, at] = (grad * silu).astype(bf16)
            for copy in stores(unit, at):
                copy.start()
            return carry

        lax.fori_loop(0, tiles, some, 0)

    keep(0).start()
    if square:
        grads_of(1).start()
        grads_of(0).wait()
        work((0, whole), [])
        grads_of(2).start()
        spread[1].wait_recv()
        spread[3].start()
        grads_of(1).wait()
        work((1, top), [(0, whole)])
        spread[2].wait_recv()
        grads_of(2).wait()
        work((2, top), [(1, top)])
        spread[5].wait_recv()
        spread[6].wait_recv()
        spread[0].start()
        keep(1).start()
        keep(2).start()
        work((1, bottom), [])
        grads_of(3).start()
        work((2, bottom), [(1, bottom)])
        spread[3].wait_recv()
        spread[0].wait_recv()
        keep(3).start()
        grads_of(3).wait()
        work((3, whole), [(2, top), (2, bottom)])
    else:
        for k in range(peers):
            if k > 0:
                spread[k].wait_recv()
                keep(k).start()
            grads_of(k).wait()
            if k + 1 < peers:
                grads_of(k + 1).start()
            work((k, whole), [(k - 1, whole)] if k > 0 else [])

    def settle(j, carry):
        at = pl.ds(pl.multiple_of(j * tile, tile), tile)
        for copy in stores((peers - 1, whole), at):
            copy.wait()
        return carry

    lax.fori_loop(0, tiles, settle, 0)
    for k in range(peers):
        keep(k).wait()
    for copy in spread.values():
        copy.wait_send()


def feed(peers, nt, og_all, down, gate, up):
    tokens, width = nt.shape
    inner = down.shape[0]
    bf = jnp.bfloat16
    S = jax.ShapeDtypeStruct
    any_ = pl.BlockSpec(memory_space=pl.ANY)
    DMA = pltpu.SemaphoreType.DMA
    inner_shape = S((peers, tokens, inner), bf)
    return pl.pallas_call(
        functools.partial(feed_kernel, peers),
        in_specs=[any_] * 5,
        out_specs=[any_] * 4,
        out_shape=[S((peers, tokens, width), bf), inner_shape, inner_shape, inner_shape],
        scratch_shapes=[
            pltpu.VMEM((peers, tokens, width), bf),
            pltpu.VMEM((tokens, inner), bf), pltpu.VMEM((tokens, inner), bf), pltpu.VMEM((tokens, inner), bf),
            pltpu.VMEM((2, tokens, width), bf),
            pltpu.VMEM((width, inner), bf), pltpu.VMEM((width, inner), bf), pltpu.VMEM((inner, width), bf),
            DMA((2,)), DMA((3,)), DMA((2, 3, 16)), DMA((1,)), DMA((peers,)),
            DMA((2 * peers,)), DMA((2 * peers,)),
        ],
        compiler_params=pltpu.CompilerParams(vmem_limit_bytes=FEED_VMEM, collective_id=1, has_side_effects=True),
        cost_estimate=cost(6 * peers * tokens * width * inner, 20 * width * inner, peers * tokens * inner),
    )(nt, og_all, down, gate, up)


def feed_back_kernel(
    peers, gs_all, us_all, mid_all, down_ref, gate_ref, up_ref,
    dn_own, dn_in, *rest,
):
    out_parts, rest = rest[:peers], rest[peers:]
    (gs_v, us_v, io, relay, out_v, gate_v, up_v, down_v,
     load_sem, weight_sem, out_sem, own_sem, dn_send, dn_recv) = rest
    tokens, inner = gs_v.shape[1:]
    width = gate_ref.shape[0]
    middle = tokens // 2
    square = peers == 4
    me = lax.axis_index("fs")
    bf16 = jnp.bfloat16

    def remote(src, dst, at, k):
        return pltpu.make_async_remote_copy(
            src_ref=src, dst_ref=dst, send_sem=dn_send.at[at], recv_sem=dn_recv.at[at],
            device_id={"fs": toggled(me, k, peers)}, device_id_type=MESH,
        )

    barrier = pltpu.get_barrier_semaphore()
    for k in range(1, peers):
        pl.semaphore_signal(barrier, inc=1, device_id={"fs": toggled(me, k, peers)}, device_id_type=MESH)
    pl.semaphore_wait(barrier, peers - 1)
    top, bottom = pl.ds(0, middle), pl.ds(middle, middle)

    def returns(k):
        if square and k == 3:
            return (remote(io.at[3, top], relay.at[0], 3, 1), remote(io.at[3, bottom], relay.at[1], 0, 2))
        parts = [pl.ds(0, width // 2), pl.ds(width // 2, width // 2)]
        return tuple(
            remote(io.at[k, :, part], dn_in.at[k - 1, :, part], k + i * peers, k)
            for i, part in enumerate(parts)
        )

    order = [peers - 1, 0] + list(range(peers - 2, 0, -1))
    weights = [
        pltpu.make_async_copy(src, dst, weight_sem.at[i])
        for i, (src, dst) in enumerate(((gate_ref, gate_v), (up_ref, up_v), (down_ref, down_v)))
    ]
    for copy in weights:
        copy.start()

    def slopes_of(turn):
        k, slot = order[turn], turn % 2
        return [
            pltpu.make_async_copy(src.at[k], dst.at[slot], load_sem.at[i, slot])
            for i, (src, dst) in enumerate(((gs_all, gs_v), (us_all, us_v)))
        ]

    def units_of(turn):
        slab, slot = toggled(me, order[turn], peers), turn % 2
        return pltpu.make_async_copy(mid_all.at[slab], gs_v.at[slot], load_sem.at[0, slot])

    for copy in slopes_of(0):
        copy.start()
    wide = 256
    strips = width // wide
    weights[0].wait()
    weights[1].wait()
    for turn, k in enumerate(order):
        slot = turn % 2
        for copy in slopes_of(turn):
            copy.wait()
        if turn + 1 < peers:
            for copy in slopes_of(turn + 1):
                copy.start()
        if square and k == 2:
            returns(3)[0].wait_recv()
        if square and k == 1:
            returns(3)[1].wait_recv()

        def more(j, carry, k=k, slot=slot):
            at = pl.ds(pl.multiple_of(j * wide, wide), wide)
            part = dot(gs_v[slot], gate_v[at, :], NT) + dot(us_v[slot], up_v[at, :], NT)
            if square and k == 2:
                io[k, top, at] = (part[:middle] + relay[0, :, at].astype(jnp.float32)).astype(bf16)
                io[k, bottom, at] = part[middle:].astype(bf16)
            elif square and k == 1:
                io[k, top, at] = part[:middle].astype(bf16)
                io[k, bottom, at] = (part[middle:] + relay[1, :, at].astype(jnp.float32)).astype(bf16)
            else:
                io[k, :, at] = part.astype(bf16)
            return carry

        if k == 0 or (square and k == 3):
            lax.fori_loop(0, strips, more, 0)
        else:
            lax.fori_loop(0, strips // 2, more, 0)
            returns(k)[0].start()
            lax.fori_loop(strips // 2, strips, more, 0)
            returns(k)[1].start()
        if k == 0:
            pltpu.make_async_copy(io.at[0], dn_own, own_sem.at[0]).start()
        elif square and k == 3:
            for copy in returns(k):
                copy.start()

    weights[2].wait()
    units_of(0).start()
    for turn, k in enumerate(order):
        slot = turn % 2
        units_of(turn).wait()
        if turn + 1 < peers:
            units_of(turn + 1).start()

        def out_copy(j, k=k):
            at = pl.ds(pl.multiple_of(j * wide, wide), wide)
            return pltpu.make_async_copy(out_v.at[j % 2], out_parts[k].at[:, at], out_sem.at[j % 2])

        def last(j, carry, slot=slot, out_copy=out_copy):
            at = pl.ds(pl.multiple_of(j * wide, wide), wide)
            found = dot(gs_v[slot], down_v[:, at], NN).astype(bf16)

            @pl.when(j >= 2)
            def _():
                out_copy(j - 2).wait()

            out_v[j % 2] = found
            out_copy(j).start()
            return carry

        lax.fori_loop(0, strips, last, 0)
        out_copy(strips - 2).wait()
        out_copy(strips - 1).wait()

    pltpu.make_async_copy(io.at[0], dn_own, own_sem.at[0]).wait()
    for k in range(1, peers):
        for copy in returns(k):
            copy.wait_send()
            if not (square and k == 3):
                copy.wait_recv()


def feed_back(peers, gs, us, mid, down, gate, up):
    tokens, inner = gs.shape[1:]
    width = gate.shape[0]
    bf = jnp.bfloat16
    S = jax.ShapeDtypeStruct
    any_ = pl.BlockSpec(memory_space=pl.ANY)
    DMA = pltpu.SemaphoreType.DMA
    halves = 2 if peers == 4 else peers - 1
    return pl.pallas_call(
        functools.partial(feed_back_kernel, peers),
        in_specs=[any_] * 6,
        out_specs=[any_] * (2 + peers),
        out_shape=[S((tokens, width), bf), S((halves, tokens, width), bf)] + [S((tokens, width), bf)] * peers,
        scratch_shapes=[
            pltpu.VMEM((2, tokens, inner), bf), pltpu.VMEM((2, tokens, inner), bf),
            pltpu.VMEM((peers, tokens, width), bf),
            pltpu.VMEM((2, tokens // 2, width), bf),
            pltpu.VMEM((2, tokens, 256), bf),
            pltpu.VMEM((width, inner), bf), pltpu.VMEM((width, inner), bf), pltpu.VMEM((inner, width), bf),
            DMA((2, 2)), DMA((3,)), DMA((2,)), DMA((1,)), DMA((2 * peers,)), DMA((2 * peers,)),
        ],
        compiler_params=pltpu.CompilerParams(vmem_limit_bytes=FEED_VMEM, collective_id=4, has_side_effects=True),
        cost_estimate=cost(6 * peers * tokens * width * inner, 20 * width * inner),
    )(gs, us, mid, down, gate, up)


def gate_fold_kernel(nt_ref, gs_ref, us_ref, gate_ref, up_ref):
    peers, tokens, block = nt_ref.shape
    inner = gs_ref.shape[2]
    total = peers * tokens
    turned = jnp.transpose(nt_ref[...].reshape(total, block))
    gate_ref[...] = dot(turned, gs_ref[...].reshape(total, inner), NN).astype(jnp.bfloat16)
    up_ref[...] = dot(turned, us_ref[...].reshape(total, inner), NN).astype(jnp.bfloat16)


def gate_fold(nt_all, gs, us):
    peers, tokens, width = nt_all.shape
    inner = gs.shape[2]
    block = 512
    fixed = pl.BlockSpec((peers, tokens, inner), lambda j: (0, 0, 0), pipeline_mode=pl.Buffered(1))
    return pl.pallas_call(
        gate_fold_kernel,
        grid=(width // block,),
        in_specs=[pl.BlockSpec((peers, tokens, block), lambda j: (0, 0, j)), fixed, fixed],
        out_specs=[pl.BlockSpec((block, inner), lambda j: (j, 0))] * 2,
        out_shape=[jax.ShapeDtypeStruct((width, inner), jnp.bfloat16)] * 2,
        compiler_params=params(),
        cost_estimate=cost(4 * peers * tokens * width * inner, 2 * (nt_all.size + 3 * gs.size)),
    )(nt_all, gs, us)


def down_fold_kernel(og_ref, mid_ref, out_ref):
    peers, tokens, tile = mid_ref.shape
    owned = out_ref.shape[2]
    turned = jnp.transpose(mid_ref[...].reshape(peers * tokens, tile))
    wide = og_ref.shape[2]
    acc = dot(turned, og_ref[...].reshape(peers * tokens, wide), NN).astype(jnp.bfloat16)
    for c in range(out_ref.shape[0]):
        out_ref[c] = acc[:, c * owned : (c + 1) * owned]


def down_fold(og_all, mid_all, chain):
    peers, tokens, width = og_all.shape
    inner = mid_all.shape[2]
    tile = 256 if inner % 256 == 0 else 128
    owned = width // chain
    wide = 1280
    return pl.pallas_call(
        down_fold_kernel,
        grid=(width // wide, inner // tile),
        in_specs=[
            pl.BlockSpec((peers, tokens, wide), lambda i, j: (0, 0, i)),
            pl.BlockSpec((peers, tokens, tile), lambda i, j: (0, 0, j)),
        ],
        out_specs=pl.BlockSpec((wide // owned, tile, owned), lambda i, j: (i, j, 0)),
        out_shape=jax.ShapeDtypeStruct((chain, inner, owned), jnp.bfloat16),
        compiler_params=params(),
        cost_estimate=cost(2 * peers * tokens * width * inner, 2 * (og_all.size + 3 * mid_all.size)),
    )(og_all, mid_all)


def front_kernel(peers, chain, count, batches, *refs):
    (hid, gains, q_w, k_w, v_w, o_w, gate_w, up_w, og, cos_ref, sin_ref, low_ref) = refs[:12]
    (w_in, o_full, gate_part, up_part, og_all, normed_o, q_o, line_o, sib_o, att_o, lse_o, gain_o) = refs[12:24]
    (w_v, nt_v, nt_b, q_v, att_v, line_v, sib_v, gains_v) = refs[24:32]
    (own_sem, out_sem, gain_s, gain_r, qkv_s, qkv_r, twin_s, twin_r, back_s, back_r,
     og_s, og_r, hop_s, hop_r, kin_s, kin_r) = refs[32:]
    tokens, width = nt_v.shape
    rows = q_w.shape[0]
    inner = gate_part.shape[1]
    length = tokens // batches
    slots = line_v.shape[0]
    window = count * length
    square = peers == 4
    bf16, f32 = jnp.bfloat16, jnp.float32
    me, place = lax.axis_index("fs"), lax.axis_index("ctx")
    core, plane = place % 2, place // 2
    parity = plane % 2
    twin = place + 1 - 2 * core
    partner = place + 2 - 4 * parity
    deep = place >= 2
    ahead = place + 2 < chain

    def send(src, dst, send_sem, recv_sem, target):
        return pltpu.make_async_remote_copy(
            src_ref=src, dst_ref=dst, send_sem=send_sem, recv_sem=recv_sem,
            device_id=target, device_id_type=MESH,
        )

    def owner(k):
        return toggled(me, k, peers)

    def along(k):
        return {"fs": owner(k)}

    for i in range(1, slots):

        @pl.when(plane < i)
        def _(i=i):
            line_v[i] = jnp.zeros(line_v.shape[1:], bf16)
            sib_v[i] = jnp.zeros(line_v.shape[1:], bf16)

    barrier = pltpu.get_barrier_semaphore()
    for k in range(1, peers):
        pl.semaphore_signal(barrier, inc=1, device_id=along(k), device_id_type=MESH)
    pl.semaphore_signal(barrier, inc=1, device_id={"ctx": twin}, device_id_type=MESH)

    @pl.when(deep)
    def _():
        pl.semaphore_signal(barrier, inc=1, device_id={"ctx": place - 2}, device_id_type=MESH)

    @pl.when(ahead)
    def _():
        pl.semaphore_signal(barrier, inc=1, device_id={"ctx": place + 2}, device_id_type=MESH)

    planes = chain // 2
    behind = (plane + planes - 1) // planes
    before = (2 * planes - 2 - plane) // planes
    pl.semaphore_wait(barrier, peers + behind + before)

    share = rows // 2
    half = share // 2
    mats = ((q_w, pl.ds(0, width)), (k_w, pl.ds(width, KV_WIDTH)), (v_w, pl.ds(width + KV_WIDTH, KV_WIDTH)))

    def block(k, at, size):
        return pl.ds(pl.multiple_of(owner(k) * rows + core * share + at, 16), size)

    def first_hop(k, m):
        src, cols = mats[m]
        mine = pl.ds(pl.multiple_of(core * share, 16), share)
        return send(src.at[mine, :], w_v.at[block(0, 0, share), cols], qkv_s.at[k, m], qkv_r.at[k, m], along(k))

    def relay(part, m):
        source, target = (1, 2) if part == 3 else (2, 1)
        where = w_v.at[block(source, 0 if part == 3 else half, half), mats[m][1]]
        return send(where, where, qkv_s.at[part, m], qkv_r.at[part, m], along(target))

    def to_twin(part, m):
        if square and part in (0, 3):
            rows_at = block(3, 0 if part == 3 else half, half)
        else:
            rows_at = block(part, 0, share)
        where = w_v.at[rows_at, mats[m][1]]
        return send(where, where, twin_s.at[part, m], twin_r.at[part, m], {"ctx": twin})

    reached = [1, 2] if square else list(range(1, peers))
    for k in reached:
        for m in range(3):
            first_hop(k, m).start()
    own_rows = pl.ds(pl.multiple_of(me * rows, 16), rows)
    own_loads = [
        pltpu.make_async_copy(src, w_v.at[own_rows, cols], own_sem.at[i])
        for i, (src, cols) in enumerate(mats)
    ]
    for copy in own_loads:
        copy.start()
    gain_moves = [send(gains, gains_v.at[me], gain_s.at[k], gain_r.at[k], along(k)) for k in range(1, peers)]
    for copy in gain_moves:
        copy.start()
    gains_v[me] = gains[...]
    for copy in gain_moves:
        copy.wait_recv()
    whole_gain = jnp.concatenate([gains_v[f] for f in range(peers)], axis=1)
    gain_o[...] = whole_gain

    chunk = 64

    def norm(i, carry):
        at = pl.ds(pl.multiple_of(i * chunk, chunk), chunk)
        x = hid[at, :].astype(f32)
        scale = lax.rsqrt(jnp.mean(x * x, axis=1, keepdims=True) + NORM_EPS)
        normed = (x * scale * whole_gain[0:1]).astype(bf16)
        nt_v[at, :] = normed
        for f in range(peers):
            nt_b[f, at, :] = normed[:, f * rows : (f + 1) * rows]
        return carry

    lax.fori_loop(0, tokens // chunk, norm, 0)
    normed_out = pltpu.make_async_copy(nt_v, normed_o, out_sem.at[0])
    normed_out.start()

    quarter = rows // 4
    sources = (o_w, gate_w, up_w)
    fulls = (o_full, gate_part, up_part)

    def region(m, k, c, p):
        return fulls[m].at[pl.ds(pl.multiple_of(owner(k) * rows + (c + 2 * p) * quarter, 16), quarter), :]

    def back_first(m, k):
        at = pl.ds(pl.multiple_of((core + 2 * parity) * quarter, 16), quarter)
        if m == 0:
            src = o_w.at[at, :]
        else:
            src = sources[m].at[at, pl.ds(pl.multiple_of(owner(k) * inner, 128), inner)]
        return send(src, region(m, 0, core, parity), back_s.at[0, m, k], back_r.at[0, m, k], along(k))

    def back_plane(m, k):
        where = region(m, k, core, parity)
        return send(where, where, back_s.at[1, m, k], back_r.at[1, m, k], {"ctx": partner})

    def back_twin(m, k, p, stage):
        where = region(m, k, core, p)
        return send(where, where, back_s.at[stage, m, k], back_r.at[stage, m, k], {"ctx": twin})

    others = range(1, peers)

    def spread_first(which):
        for m in which:
            for k in others:
                back_first(m, k).start()

    def spread_second(which):
        for m in which:
            for k in others:
                back_first(m, k).wait_recv()
                back_plane(m, k).start()
                back_twin(m, k, parity, 2).start()

    def spread_third(which):
        for m in which:
            for k in others:
                back_plane(m, k).wait_recv()
                back_twin(m, k, 1 - parity, 3).start()

    def og_hop(k):
        return send(og, og_all.at[me], og_s.at[k], og_r.at[k], along(k))

    middle = tokens // 2

    def og_relay(part):
        source, target = (1, 2) if part == 3 else (2, 1)
        where = og_all.at[owner(source), pl.ds(0 if part == 3 else middle, middle), :]
        return send(where, where, og_s.at[part], og_r.at[part], along(target))

    wide = STRIP
    tiles = w_v.shape[1] // wide

    def project(acc, bounce):
        def through(src, dst, sem):
            shape = src.shape
            there = bounce.at[pl.ds(0, shape[0]), pl.ds(0, shape[1])]
            copy = pltpu.make_async_copy(src, there, sem.at[3])
            copy.start()
            copy.wait()
            copy = pltpu.make_async_copy(there, dst, sem.at[4])
            copy.start()
            copy.wait()

        through(og, og_all.at[me], own_sem)
        through(o_w, o_full.at[own_rows, :], own_sem)
        mine = pl.ds(pl.multiple_of(me * inner, 128), inner)
        through(gate_w.at[:, mine], gate_part.at[own_rows, :], own_sem)
        through(up_w.at[:, mine], up_part.at[own_rows, :], own_sem)
        for copy in own_loads:
            copy.wait()

        def add(k):
            rows_at = pl.ds(pl.multiple_of(owner(k) * rows, 16), rows)

            def one(j, carry):
                at = pl.ds(pl.multiple_of(j * wide, wide), wide)
                part = dot(nt_b[owner(k)], w_v[rows_at, at], NN)
                acc[:, at] = part if k == 0 else acc[:, at] + part
                return carry

            lax.fori_loop(0, tiles, one, 0)

        add(0)
        if square:
            for k, part in ((1, 3), (2, 0)):
                for m in range(3):
                    first_hop(k, m).wait_recv()
                for m in range(3):
                    relay(part, m).start()
                    to_twin(k, m).start()
                if k == 2:
                    spread_first([0])
                for m in range(3):
                    to_twin(k, m).wait_recv()
                add(k)
            for part in (3, 0):
                for m in range(3):
                    relay(part, m).wait_recv()
                    to_twin(part, m).start()
            spread_first([1, 2])
            for k in (1, 2):
                og_hop(k).start()
            for part in (3, 0):
                for m in range(3):
                    to_twin(part, m).wait_recv()
            add(3)
        else:
            for k in others:
                for m in range(3):
                    first_hop(k, m).wait_recv()
                    to_twin(k, m).start()
                for m in range(3):
                    to_twin(k, m).wait_recv()
                add(k)
            spread_first([0, 1, 2])
            for k in others:
                og_hop(k).start()

        line_v[0, 0] = turn(acc[:, width : width + KV_WIDTH], cos_ref[...], sin_ref[...]).astype(bf16)
        line_v[0, 1] = acc[:, width + KV_WIDTH :].astype(bf16)

        @pl.when(ahead)
        def _():
            hop(0).start()

        kin(0).start()

        def finish(j, carry):
            at = pl.ds(pl.multiple_of(j * wide, wide), wide)
            q_v[:, at] = turn(acc[:, at], cos_ref[...], sin_ref[...]).astype(bf16)
            return carry

        lax.fori_loop(0, width // wide, finish, 0)

    def hop(i):
        return send(line_v.at[i], line_v.at[i + 1], hop_s.at[i], hop_r.at[i], {"ctx": place + 2})

    def kin(i):
        return send(line_v.at[i], sib_v.at[i], kin_s.at[i], kin_r.at[i], {"ctx": twin})

    pl.run_scoped(project, pltpu.VMEM((tokens, w_v.shape[1]), f32), pltpu.VMEM((rows, width), bf16))

    w_out = pltpu.make_async_copy(w_v, w_in, out_sem.at[1])
    w_out.start()
    q_out = pltpu.make_async_copy(q_v, q_o, out_sem.at[2])
    q_out.start()
    for i in range(1, slots):

        @pl.when(plane >= i)
        def _(i=i):
            hop(i - 1).wait_recv()
            kin(i).start()

        if i + 1 < slots:

            @pl.when((plane >= i) & ahead)
            def _(i=i):
                hop(i).start()

    kin(0).wait_recv()
    for i in range(1, slots):

        @pl.when(plane >= i)
        def _(i=i):
            kin(i).wait_recv()

    spread_second([0])
    line_out = pltpu.make_async_copy(line_v, line_o, out_sem.at[3])
    line_out.start()
    sib_out = pltpu.make_async_copy(sib_v, sib_o, out_sem.at[4])
    sib_out.start()

    def attention(keys, values, bias):
        for b in range(batches):
            here = pl.ds(b * length, length)
            for back in range(count):
                at_rows = pl.ds((count - 1 - back) * length, length)
                for kind, target in ((0, keys), (1, values)):
                    if back % 2 == 0:
                        found = line_v[back // 2, kind, here, :]
                    else:
                        found = sib_v[(back + 1) // 2 - core, kind, here, :]
                    for head in range(KEY_VALUE_HEADS):
                        target[head, at_rows, :] = found[:, head * HEAD_SIZE : (head + 1) * HEAD_SIZE]
            key_place = (place - count + 1) * length + lax.broadcasted_iota(jnp.int32, (length, window), 1)
            query_place = place * length + lax.broadcasted_iota(jnp.int32, (length, window), 0)
            seen = (key_place >= low_ref[b]) & (key_place <= query_place)
            bias[...] = jnp.where(seen, 0.0, MASK_VALUE_FILL)

            def pair_of_heads(pair, carry, b=b, here=here):
                cols = pl.ds(pl.multiple_of(pair * STRIP, STRIP), STRIP)
                strip = q_v[here, cols]
                mixed, sums = [], []
                for side in range(2):
                    key, value = keys[2 * pair + side], values[2 * pair + side]
                    for group in range(GROUPS):
                        at = (side * GROUPS + group) * HEAD_SIZE
                        scores = dot(strip[:, at : at + HEAD_SIZE], key, NT) * SCALE + bias[...]
                        peak = jnp.max(scores, axis=1, keepdims=True)
                        weights = jnp.exp(scores - peak)
                        total = jnp.sum(weights, axis=1, keepdims=True)
                        mixed.append(dot(weights.astype(bf16), value, NN) / total)
                        sums.append(peak + jnp.log(total))
                att_v[here, cols] = jnp.concatenate(mixed, axis=1).astype(bf16)
                spare = jnp.zeros((length, 128 - 2 * GROUPS), f32)
                turned = jnp.transpose(jnp.concatenate(sums + [spare], axis=1))
                lse_o[b, pair] = turned[: 2 * GROUPS]
                return carry

            lax.fori_loop(0, KEY_VALUE_HEADS // 2, pair_of_heads, 0)
            if b == 0:
                spread_second([1, 2])

    pl.run_scoped(
        attention,
        pltpu.VMEM((KEY_VALUE_HEADS, window, HEAD_SIZE), bf16),
        pltpu.VMEM((KEY_VALUE_HEADS, window, HEAD_SIZE), bf16),
        pltpu.VMEM((length, window), f32),
    )
    att_out = pltpu.make_async_copy(att_v, att_o, out_sem.at[5])
    att_out.start()
    spread_third([0])
    if square:
        for k, part in ((1, 3), (2, 0)):
            og_hop(k).wait_recv()
            og_relay(part).start()
    spread_third([1, 2])

    for copy in (normed_out, w_out, q_out, line_out, sib_out, att_out):
        copy.wait()
    for copy in gain_moves:
        copy.wait_send()
    for m in range(3):
        for k in reached:
            first_hop(k, m).wait_send()
            to_twin(k, m).wait_send()
        if square:
            for part in (3, 0):
                relay(part, m).wait_send()
                to_twin(part, m).wait_send()
    for k in reached:
        og_hop(k).wait_send()
        if not square:
            og_hop(k).wait_recv()
    if square:
        for part in (3, 0):
            og_relay(part).wait()
    for m in range(3):
        for k in others:
            back_first(m, k).wait_send()
            back_plane(m, k).wait_send()
            back_twin(m, k, parity, 2).wait()
            back_twin(m, k, 1 - parity, 3).wait()
    kin(0).wait_send()

    @pl.when(ahead)
    def _():
        hop(0).wait_send()

    for i in range(1, slots):

        @pl.when(plane >= i)
        def _(i=i):
            kin(i).wait_send()

        if i + 1 < slots:

            @pl.when((plane >= i) & ahead)
            def _(i=i):
                hop(i).wait_send()


def front(peers, chain, count, hidden, gains, weights, og, cosine, sine, low):
    batches, length, _ = low.shape
    tokens, width = hidden.shape
    rows = weights[0].shape[0]
    inner = weights[4].shape[1] // peers
    slots = (count - 1) // 2 + 1
    bf = jnp.bfloat16
    S = jax.ShapeDtypeStruct
    DMA = pltpu.SemaphoreType.DMA
    far = pl.BlockSpec(memory_space=pl.ANY)
    near = pl.BlockSpec(memory_space=pltpu.VMEM)
    whole = S((tokens, width), bf)
    line = (slots, 2, tokens, KV_WIDTH)
    return pl.pallas_call(
        functools.partial(front_kernel, peers, chain, count, batches),
        in_specs=[near, near] + [far] * 7 + [near] * 3,
        out_specs=[far] * 10 + [near, near],
        out_shape=[
            S((width, width + 2 * KV_WIDTH), bf),
            S((width, width), bf),
            S((width, inner), bf),
            S((width, inner), bf),
            S((peers, tokens, width), bf),
            whole,
            whole,
            S(line, bf),
            S(line, bf),
            whole,
            S((batches, KEY_VALUE_HEADS // 2, 2 * GROUPS, length), jnp.float32),
            S((8, width), jnp.float32),
        ],
        scratch_shapes=[
            pltpu.VMEM((width, width + 2 * KV_WIDTH), bf),
            pltpu.VMEM((tokens, width), bf),
            pltpu.VMEM((peers, tokens, rows), bf),
            pltpu.VMEM((tokens, width), bf),
            pltpu.VMEM((tokens, width), bf),
            pltpu.VMEM(line, bf),
            pltpu.VMEM(line, bf),
            pltpu.VMEM((peers, 8, rows), jnp.float32),
            DMA((5,)), DMA((6,)), DMA((peers,)), DMA((peers,)),
            DMA((peers, 3)), DMA((peers, 3)), DMA((peers, 3)), DMA((peers, 3)),
            DMA((4, 3, peers)), DMA((4, 3, peers)), DMA((peers,)), DMA((peers,)),
            DMA((slots,)), DMA((slots,)), DMA((slots,)), DMA((slots,)),
        ],
        compiler_params=pltpu.CompilerParams(
            vmem_limit_bytes=FEED_VMEM, collective_id=2, has_side_effects=True
        ),
        cost_estimate=cost(2 * tokens * width * 3840 * 10, 200 * tokens * width, QUERY_HEADS * tokens * count * length),
    )(hidden, gains, *weights, og, cosine, sine, low)


def back_kernel(peers, chain, count, batches, *refs):
    (normed, attended, d_attn, d_att, q_v, lse, low, cos_ref, sin_ref, scale, gain_two, line, sib, hid, w_in) = refs[:15]
    (slope_out, grad_o, grad_q, grad_kv, gain_out, far_o, far_q, far_kv, fs_o, fs_q, fs_kv, parts, odd_in, hop_in) = refs[15:29]
    (nb_o, z_o, z_q, z_kv, slopes_t, load_v, d_v, gain_v, gain_fs, gain_all) = refs[29:39]
    (far_s, far_r, fs_s, fs_r, zs_s, zs_r, load_sem, fsl_sem, part_sem, odd_s, odd_r, hop_s, hop_r, sum_sem, block_sem, gf_s, gf_r, ga_s, ga_r) = refs[39:]
    tokens, width = normed.shape
    rows = width // peers
    planes = chain // 2
    length = tokens // batches
    window = count * length
    reach = (count - 1) // 2
    bf16, f32 = jnp.bfloat16, jnp.float32
    me, place = lax.axis_index("fs"), lax.axis_index("ctx")
    core, plane = place % 2, place // 2
    twin = place + 1 - 2 * core
    deep, ahead = place >= 2, place + 2 < chain

    def send(src, dst, send_sem, recv_sem, target):
        return pltpu.make_async_remote_copy(
            src_ref=src, dst_ref=dst, send_sem=send_sem, recv_sem=recv_sem,
            device_id=target, device_id_type=MESH,
        )

    barrier = pltpu.get_barrier_semaphore()
    for k in range(1, peers):
        pl.semaphore_signal(barrier, inc=1, device_id={"fs": toggled(me, k, peers)}, device_id_type=MESH)
    for k in range(1, chain):
        pl.semaphore_signal(barrier, inc=1, device_id={"ctx": toggled(place, k, chain)}, device_id_type=MESH)
    pl.semaphore_wait(barrier, peers + chain - 2)

    kinds = {
        "o": (0, attended, far_o, fs_o, nb_o, z_o, grad_o),
    }

    def own_of(x):
        return kinds[x][2].shape[1]

    def turn_slopes(x):
        own = own_of(x)
        for p in range(planes):
            if x == "kv":
                half = own // 2
                sides = []
                for c in range(2):
                    at = (2 * p + c) * half
                    sides.append(
                        jnp.concatenate(
                            [
                                d_v[:, width + at : width + at + half],
                                d_v[:, width + KV_WIDTH + at : width + KV_WIDTH + at + half],
                            ],
                            axis=1,
                        )
                    )
            else:
                sides = [d_v[:, (2 * p + c) * own : (2 * p + c + 1) * own] for c in range(2)]
            first, second = (jnp.transpose(side.astype(f32)) for side in sides)
            slopes_t[0, p, :own] = jnp.where(core == 0, first, second).astype(bf16)
            slopes_t[1, p, :own] = jnp.where(core == 0, second, first).astype(bf16)

    def far_copy(x, t):
        i, _, far, _, nb, _, _ = kinds[x]
        return send(nb.at[t, pl.ds(0, own_of(x))], far.at[t], far_s.at[i, t], far_r.at[i, t], {"ctx": twin})

    def far_phase(x):
        _, left, _, _, nb, _, _ = kinds[x]
        own = own_of(x)
        for f in range(peers):

            def one(p, carry, f=f):
                t = f * planes + p
                part = dot(slopes_t[1, p, :own], left[:, f * rows : (f + 1) * rows], NN)
                nb[t, :own] = part.astype(bf16)
                far_copy(x, t).start()
                return carry

            lax.fori_loop(0, planes, one, 0)

    def fs_copy(x, f, p):
        i, _, _, fs, nb, _, _ = kinds[x]
        src = nb.at[f * planes + p, pl.ds(0, own_of(x))]
        return send(src, fs.at[me, p], fs_s.at[i, f, p], fs_r.at[i, me, p], {"fs": f})

    def fs_arrival(x, s, p):
        i, _, _, fs, nb, _, _ = kinds[x]
        src = nb.at[p, pl.ds(0, own_of(x))]
        return send(src, fs.at[s, p], fs_s.at[i, s, p], fs_r.at[i, s, p], {"fs": s})

    def near_phase(x):
        _, left, far, _, nb, _, _ = kinds[x]
        own = own_of(x)
        total = peers * planes

        def load(t):
            slot = t % 2
            return pltpu.make_async_copy(far.at[t], load_v.at[slot, pl.ds(0, own)], load_sem.at[slot])

        far_copy(x, 0).wait_recv()
        load(0).start()
        for f in range(peers):

            def one(p, carry, f=f):
                t = f * planes + p

                @pl.when(t + 1 < total)
                def _():
                    far_copy(x, t + 1).wait_recv()
                    load(t + 1).start()

                part = dot(slopes_t[0, p, :own], left[:, f * rows : (f + 1) * rows], NN)
                load(t).wait()
                far_copy(x, t).wait_send()
                nb[t, :own] = (part + load_v[t % 2, :own].astype(f32)).astype(bf16)

                @pl.when(f != me)
                def _():
                    fs_copy(x, f, p).start()

                return carry

            lax.fori_loop(0, planes, one, 0)

    def z_copy(x, p):
        i, _, _, _, nb, z, _ = kinds[x]
        src = nb.at[me * planes + p, pl.ds(0, own_of(x))]
        return send(src, z.at[plane], zs_s.at[i, p], zs_r.at[i, plane], {"ctx": 2 * p + core})

    def z_arrival(x, p):
        i, _, _, _, nb, z, _ = kinds[x]
        src = nb.at[me * planes + p, pl.ds(0, own_of(x))]
        return send(src, z.at[p], zs_s.at[i, p], zs_r.at[i, p], {"ctx": 2 * p + core})

    def z_phase(x, fs_load):
        _, _, _, fs, nb, _, tot = kinds[x]
        own = own_of(x)

        def one(p, carry):
            for s in range(peers):
                there = pltpu.make_async_copy(fs.at[s, p], fs_load.at[s, pl.ds(0, own)], fsl_sem.at[s])

                @pl.when(s != me)
                def _(s=s, there=there):
                    fs_arrival(x, s, p).wait_recv()
                    there.start()

            fs_load[me, :own] = nb[me * planes + p, :own]
            for s in range(peers):
                there = pltpu.make_async_copy(fs.at[s, p], fs_load.at[s, pl.ds(0, own)], fsl_sem.at[s])

                @pl.when(s != me)
                def _(there=there):
                    there.wait()

            total = fs_load[0, :own].astype(f32)
            for s in range(1, peers):
                total = total + fs_load[s, :own].astype(f32)

            @pl.when(p == plane)
            def _():
                tot[...] = total

            @pl.when(p != plane)
            def _():
                nb[me * planes + p, :own] = total.astype(bf16)
                z_copy(x, p).start()

            return carry

        lax.fori_loop(0, planes, one, 0)

    def finish(x):
        _, _, _, _, _, z, tot = kinds[x]
        total = tot[...]
        for p in range(planes):

            @pl.when(p != plane)
            def _(p=p):
                z_arrival(x, p).wait_recv()

            @pl.when(p == plane)
            def _(p=p):
                z[p] = jnp.zeros(z.shape[1:], bf16)

            total = total + z[p].astype(f32)
        tot[...] = total

    def settle(x):
        for p in range(planes):
            for f in range(peers):

                @pl.when(f != me)
                def _(f=f, p=p):
                    fs_copy(x, f, p).wait_send()

            @pl.when(p != plane)
            def _(p=p):
                z_copy(x, p).wait_send()

    def part_store(b, part_v):
        return pltpu.make_async_copy(part_v, parts.at[:, :, pl.ds(b * length, length)], part_sem.at[0])

    def attention(keys, values, bias, key_sums, value_sums, part_v, block_v):
        def one_batch(b):
            here = pl.ds(b * length, length)

            def fetch(back):
                if back % 2 == 0:
                    src = line.at[back // 2, :, here]
                else:
                    src = sib.at[(back + 1) // 2 - core, :, here]
                return pltpu.make_async_copy(src, block_v.at[back % 2], block_sem.at[back % 2])

            fetch(0).start()
            for back in range(count):
                if back + 1 < count:
                    fetch(back + 1).start()
                fetch(back).wait()
                at_rows = pl.ds((count - 1 - back) * length, length)
                for kind, target in ((0, keys), (1, values)):
                    found = block_v[back % 2, kind]
                    for head in range(KEY_VALUE_HEADS):
                        target[head, at_rows, :] = found[:, head * HEAD_SIZE : (head + 1) * HEAD_SIZE]
            key_place = (place - count + 1) * length + lax.broadcasted_iota(jnp.int32, (window, length), 0)
            query_place = place * length + lax.broadcasted_iota(jnp.int32, (window, length), 1)
            seen = (key_place >= low[b]) & (key_place <= query_place)
            bias[...] = jnp.where(seen, 0.0, MASK_VALUE_FILL)

            def pair_of_heads(pair, carry):
                cols = pl.ds(pl.multiple_of(pair * STRIP, STRIP), STRIP)
                strip, slope = q_v[here, cols], d_att[here, cols]
                products = slope.astype(f32) * attended[here, cols].astype(f32)
                heads = [
                    jnp.sum(products[:, h * HEAD_SIZE : (h + 1) * HEAD_SIZE], axis=1, keepdims=True)
                    for h in range(2 * GROUPS)
                ]
                spare = jnp.zeros((length, 128 - 2 * GROUPS), f32)
                deltas = jnp.transpose(jnp.concatenate(heads + [spare], axis=1))
                sums = lse[b, pair]
                turned = []
                for side in range(2):
                    key, value = keys[2 * pair + side], values[2 * pair + side]
                    key_sum = jnp.zeros((window, HEAD_SIZE), f32)
                    value_sum = jnp.zeros((window, HEAD_SIZE), f32)
                    for group in range(GROUPS):
                        row = side * GROUPS + group
                        query = strip[:, row * HEAD_SIZE : (row + 1) * HEAD_SIZE]
                        gradient = slope[:, row * HEAD_SIZE : (row + 1) * HEAD_SIZE]
                        chances = jnp.exp(dot(key, query, NT) * SCALE + bias[...] - sums[row : row + 1, :])
                        value_sum = value_sum + dot(chances.astype(bf16), gradient, NN)
                        steep = dot(value, gradient, NT) - deltas[row : row + 1, :]
                        steep = (chances * steep).astype(bf16)
                        key_sum = key_sum + dot(steep, query, NN)
                        turned.append(dot(steep, key, TN) * SCALE)
                    key_sums[2 * pair + side] = (key_sum * SCALE).astype(bf16)
                    value_sums[2 * pair + side] = value_sum.astype(bf16)
                whole = jnp.concatenate(turned, axis=1)
                d_v[here, cols] = turn(whole, cos_ref[here, :], -sin_ref[here, :]).astype(bf16)
                return carry

            lax.fori_loop(0, KEY_VALUE_HEADS // 2, pair_of_heads, 0)
            if b > 0:
                part_store(b - 1, part_v).wait()
            for back in range(count):
                at_rows = pl.ds((count - 1 - back) * length, length)
                for kind, found in ((0, key_sums), (1, value_sums)):
                    part_v[back, kind] = jnp.concatenate(
                        [found[h, at_rows, :] for h in range(KEY_VALUE_HEADS)], axis=1
                    )
            part_store(b, part_v).start()

        for b in range(batches):
            one_batch(b)
            if b == 0:
                near_phase("o")
        part_store(batches - 1, part_v).wait()

    def odd_copy(i):
        return send(parts.at[2 * i + 1], odd_in.at[i], odd_s.at[i], odd_r.at[i], {"ctx": twin})

    def hop_copy(step, sum_v):
        return send(sum_v.at[3 + step % 2], hop_in.at[step], hop_s.at[step], hop_r.at[step], {"ctx": place - 2})

    def gathered(step, sum_v):
        def fill(slot, src, sem):
            return pltpu.make_async_copy(src, sum_v.at[slot], sum_sem.at[sem])

        fill(0, parts.at[2 * step], 0).start()
        fill(0, parts.at[2 * step], 0).wait()
        if step < reach:

            @pl.when(core == 0)
            def _():
                fill(1, odd_in.at[step], 1).start()
                fill(1, odd_in.at[step], 1).wait()

        else:

            @pl.when(core == 0)
            def _():
                sum_v[1] = jnp.zeros(sum_v.shape[1:], bf16)

        if step > 0:

            @pl.when(core == 1)
            def _():
                fill(1, odd_in.at[step - 1], 1).start()
                fill(1, odd_in.at[step - 1], 1).wait()

        else:

            @pl.when(core == 1)
            def _():
                sum_v[1] = jnp.zeros(sum_v.shape[1:], bf16)

    def hop_out(step, sum_v):
        gathered(step, sum_v)
        if step < reach:

            @pl.when(ahead)
            def _():
                hop_copy(step + 1, sum_v).wait_recv()
                came = pltpu.make_async_copy(hop_in.at[step + 1], sum_v.at[2], sum_sem.at[2])
                came.start()
                came.wait()

            @pl.when(place + 2 >= chain)
            def _():
                sum_v[2] = jnp.zeros(sum_v.shape[1:], bf16)

        small = tokens // 4

        def one(i, carry):
            at = pl.ds(pl.multiple_of((i % 4) * small, small), small)
            kind = i // 4
            total = sum_v[0, kind, at, :].astype(f32) + sum_v[1, kind, at, :].astype(f32)
            if step < reach:
                total = total + sum_v[2, kind, at, :].astype(f32)
            if step > 0:
                sum_v[3 + step % 2, kind, at, :] = total.astype(bf16)
            else:

                @pl.when(kind == 0)
                def _():
                    turned = turn(total, cos_ref[at, :], -sin_ref[at, :])
                    d_v[at, width : width + KV_WIDTH] = turned.astype(bf16)

                @pl.when(kind == 1)
                def _():
                    d_v[at, width + KV_WIDTH :] = total.astype(bf16)

            return carry

        if step > 0 and step + 2 <= reach:

            @pl.when(deep)
            def _():
                hop_copy(step + 2, sum_v).wait_send()

        lax.fori_loop(0, 8, one, 0)
        if step > 0:

            @pl.when(deep)
            def _():
                hop_copy(step, sum_v).start()

    first_load = pltpu.make_async_copy(d_attn, d_v.at[:, pl.ds(0, width)], load_sem.at[0])
    first_load.start()
    first_load.wait()
    turn_slopes("o")
    far_phase("o")
    pl.run_scoped(
        attention,
        pltpu.VMEM((KEY_VALUE_HEADS, window, HEAD_SIZE), bf16),
        pltpu.VMEM((KEY_VALUE_HEADS, window, HEAD_SIZE), bf16),
        pltpu.VMEM((window, length), f32),
        pltpu.VMEM((KEY_VALUE_HEADS, window, HEAD_SIZE), bf16),
        pltpu.VMEM((KEY_VALUE_HEADS, window, HEAD_SIZE), bf16),
        pltpu.VMEM((count, 2, length, KV_WIDTH), bf16),
        pltpu.VMEM((2, 2, length, KV_WIDTH), bf16),
    )
    def remainder(nb_q, nb_kv, sum_v, fs_load):
        kinds["q"] = (1, normed, far_q, fs_q, nb_q, z_q, grad_q)
        kinds["kv"] = (2, normed, far_kv, fs_kv, nb_kv, z_kv, grad_kv)
        for i in range(reach):
            odd_copy(i).start()
        turn_slopes("q")
        far_phase("q")
        for i in range(reach):
            odd_copy(i).wait_recv()
        hop_out(reach, sum_v)
        near_phase("q")
        for step in range(reach - 1, 0, -1):
            hop_out(step, sum_v)
        hop_out(0, sum_v)
        turn_slopes("kv")
        far_phase("kv")

        def slope_body(w_block, h_block, out):
            found = dot(d_v[...], w_block[...], NT)
            out[...] = found
            at = pl.ds(pl.multiple_of(pl.program_id(0) * 256, 256), 256)
            gain_v[0:1, at] = jnp.sum(found * h_block[...].astype(f32) * scale[...], axis=0, keepdims=True)

        pltpu.emit_pipeline(
            slope_body,
            grid=(width // 256,),
            in_specs=[
                pl.BlockSpec((256, w_in.shape[1]), lambda j: (j, 0)),
                pl.BlockSpec((tokens, 256), lambda j: (0, j)),
            ],
            out_specs=[pl.BlockSpec((tokens, 256), lambda j: (0, j))],
        )(w_in, hid, slope_out)
        gain_v[1:2, :] = gain_two[...]
        near_phase("kv")
        z_phase("o", fs_load)

        for f in range(peers):
            gain_fs[f, 0:2] = gain_v[0:2, f * rows : (f + 1) * rows]

        def gain_hop(f):
            return send(gain_fs.at[f], gain_all.at[chain + me], gf_s.at[f], gf_r.at[me], {"fs": f})

        def gain_arrival(s):
            return send(gain_fs.at[s], gain_all.at[chain + s], gf_s.at[s], gf_r.at[s], {"fs": s})

        for f in range(peers):

            @pl.when(f != me)
            def _(f=f):
                gain_hop(f).start()

        mine = gain_fs[me]
        for s in range(peers):

            @pl.when(s != me)
            def _(s=s):
                gain_arrival(s).wait_recv()

            @pl.when(s == me)
            def _(s=s):
                gain_all[chain + s] = jnp.zeros(gain_all.shape[1:], f32)

            mine = mine + gain_all[chain + s]
        gain_all[place] = mine

        def gain_spread(k):
            return send(gain_all.at[place], gain_all.at[place], ga_s.at[k], ga_r.at[k], {"ctx": toggled(place, k, chain)})

        for k in range(1, chain):
            gain_spread(k).start()
        z_phase("q", fs_load)
        for k in range(1, chain):
            gain_spread(k).wait_recv()
        total = gain_all[0]
        for c in range(1, chain):
            total = total + gain_all[c]
        gain_out[...] = total
        z_phase("kv", fs_load)
        finish("o")
        finish("q")
        finish("kv")

        settle("o")
        settle("q")
        settle("kv")
        for i in range(reach):
            odd_copy(i).wait_send()
        for step in range(min(reach, 2), 0, -1):

            @pl.when(deep)
            def _(step=step):
                hop_copy(step, sum_v).wait_send()

        for f in range(peers):

            @pl.when(f != me)
            def _(f=f):
                gain_hop(f).wait_send()

        for k in range(1, chain):
            gain_spread(k).wait_send()

    pl.run_scoped(
        remainder,
        pltpu.VMEM(nb_o.shape, bf16),
        pltpu.VMEM((nb_o.shape[0],) + z_kv.shape[1:], bf16),
        pltpu.VMEM((5, 2, tokens, KV_WIDTH), bf16),
        pltpu.VMEM((peers,) + z_o.shape[1:], bf16),
    )


def back(peers, chain, count, normed, attended, d_attn, d_att, queries, lse, low, cosine, sine, scale, gain_two, line, sib, hidden, w_in):
    tokens, width = normed.shape
    batches = low.shape[0]
    length = tokens // batches
    window = count * length
    planes, rows = chain // 2, width // peers
    own, own_kv = width // chain, 2 * KV_WIDTH // chain
    reach = (count - 1) // 2
    bf, f32 = jnp.bfloat16, jnp.float32
    S = jax.ShapeDtypeStruct
    DMA = pltpu.SemaphoreType.DMA
    far = pl.BlockSpec(memory_space=pl.ANY)
    near = pl.BlockSpec(memory_space=pltpu.VMEM)
    tiles = peers * planes
    return pl.pallas_call(
        functools.partial(back_kernel, peers, chain, count, batches),
        in_specs=[near, near, far] + [near] * 8 + [far] * 4,
        out_specs=[far] + [near] * 4 + [far] * 9,
        out_shape=[
            S((tokens, width), f32),
            S((own, rows), f32),
            S((own, rows), f32),
            S((own_kv, rows), f32),
            S((8, rows), f32),
            S((tiles, own, rows), bf),
            S((tiles, own, rows), bf),
            S((tiles, own_kv, rows), bf),
            S((peers, planes, own, rows), bf),
            S((peers, planes, own, rows), bf),
            S((peers, planes, own_kv, rows), bf),
            S((count, 2, tokens, KV_WIDTH), bf),
            S((reach, 2, tokens, KV_WIDTH), bf),
            S((reach + 1, 2, tokens, KV_WIDTH), bf),
        ],
        scratch_shapes=[
            pltpu.VMEM((tiles, own, rows), bf),
            pltpu.VMEM((planes, own, rows), bf),
            pltpu.VMEM((planes, own, rows), bf),
            pltpu.VMEM((planes, own_kv, rows), bf),
            pltpu.VMEM((2, planes, own, tokens), bf),
            pltpu.VMEM((2, own, rows), bf),
            pltpu.VMEM((tokens, width + 2 * KV_WIDTH), bf),
            pltpu.VMEM((8, width), f32),
            pltpu.VMEM((peers, 8, rows), f32),
            pltpu.VMEM((chain + peers, 8, rows), f32),
            DMA((3, tiles)), DMA((3, tiles)), DMA((3, peers, planes)), DMA((3, peers, planes)),
            DMA((3, planes)), DMA((3, planes)), DMA((2,)), DMA((peers,)), DMA((1,)),
            DMA((reach,)), DMA((reach,)), DMA((reach + 1,)), DMA((reach + 1,)), DMA((3,)), DMA((2,)),
            DMA((peers,)), DMA((peers,)), DMA((chain,)), DMA((chain,)),
        ],
        compiler_params=pltpu.CompilerParams(
            vmem_limit_bytes=FEED_VMEM, collective_id=3, has_side_effects=True
        ),
        cost_estimate=cost(2 * tokens * width * 3840 * 20, 200 * tokens * width, QUERY_HEADS * tokens * window),
    )(normed, attended, d_attn, d_att, queries, lse, low, cosine, sine, scale, gain_two, line, sib, hidden, w_in)


def boundaries(lengths, positions):
    cut_points = jnp.cumsum(lengths)[:-1]
    passed = positions[:, None] >= cut_points[None, :]
    return jnp.max(jnp.where(passed, cut_points[None, :], 0), axis=1)


def matmul(left, right):
    return dot(left, right, NN)


def matmul_back(gradient, weight):
    return dot(gradient, weight, NT)


def on_device(
    hidden_in,
    doc_lengths,
    attn_gain,
    query_weight,
    key_matrix,
    value_matrix,
    output_weight,
    mlp_gain,
    gate_weight,
    up_weight,
    down_weight,
    out_grad,
):
    owners, chain = lax.axis_size("fs"), lax.axis_size("ctx")
    owner, place = lax.axis_index("fs"), lax.axis_index("ctx")
    core = place % 2
    planes = chain // 2
    batches, length, width = hidden_in.shape
    tokens = batches * length
    rows = query_weight.shape[0]
    inner = down_weight.shape[0]
    count = min(WINDOW // length + 1, chain)

    def across(x, k):
        return lax.ppermute(x, "fs", [(i, i ^ k) for i in range(owners)])

    grads_in = out_grad.reshape(tokens, width)

    positions = place * length + jnp.arange(length, dtype=jnp.int32)
    starts = jax.vmap(lambda lengths: boundaries(lengths, positions))(doc_lengths)
    low = jnp.maximum(starts, positions[None, :] - (WINDOW - 1))
    frequency = ROPE_THETA ** (-2.0 * jnp.arange(HALF, dtype=jnp.float32) / HEAD_SIZE)
    turns = (positions[None, :] - starts).reshape(tokens).astype(jnp.float32)
    angles = turns[:, None] * frequency[None, :]
    cosine, sine = jnp.cos(angles), jnp.sin(angles)
    cosine = jnp.tile(jnp.concatenate([cosine, cosine], axis=1), (1, STRIP // HEAD_SIZE))
    sine = jnp.tile(jnp.concatenate([-sine, sine], axis=1), (1, STRIP // HEAD_SIZE))

    gains = jnp.concatenate([jnp.stack([attn_gain, mlp_gain]).astype(jnp.float32), jnp.zeros((6, rows))])
    (
        in_full, out_full, gate_full, up_full, grads_all, normed, queries, line, kin, attended_rows, lse, gain_rows
    ) = front(
        owners,
        chain,
        count,
        hidden_in.reshape(tokens, width),
        gains,
        (query_weight, key_matrix, value_matrix, output_weight, gate_weight, up_weight),
        grads_in,
        cosine,
        sine,
        low[:, :, None],
    )
    gain_one, gain_two = gain_rows[0], gain_rows[1]

    x = hidden_in.reshape(tokens, width).astype(jnp.float32)
    scale_one = lax.rsqrt(jnp.mean(x * x, axis=1, keepdims=True) + NORM_EPS)
    projected = matmul(attended_rows, out_full)
    residual = x + projected
    scale_two = lax.rsqrt(jnp.mean(residual * residual, axis=1, keepdims=True) + NORM_EPS)
    normed_two = (residual * scale_two * gain_two).astype(jnp.bfloat16)

    normed_all, gate_slopes, up_slopes, mid = feed(
        owners, normed_two, grads_all, down_weight, gate_full, up_full
    )
    gate_part, up_part = gate_fold(normed_all, gate_slopes, up_slopes)
    gate_slopes, up_slopes, gate_part, up_part = lax.optimization_barrier(
        (gate_slopes, up_slopes, gate_part, up_part)
    )
    own_part, in_parts, *out_parts = feed_back(
        owners, gate_slopes, up_slopes, mid, down_weight, gate_full, up_full
    )
    came = [across(out_parts[k], k) for k in range(1, owners)]
    normed_two_grad = own_part.astype(jnp.float32) + jnp.sum(in_parts.astype(jnp.float32), axis=0)

    spans = chain // owners
    gate_mine = lax.psum_scatter(gate_part, "ctx", scatter_dimension=0, tiled=True)
    up_mine = lax.psum_scatter(up_part, "ctx", scatter_dimension=0, tiled=True)
    mid = lax.optimization_barrier((mid, own_part))[0]
    down_part = down_fold(grads_all, mid, chain)
    down_grad = lax.psum_scatter(down_part, "ctx", scatter_dimension=0, tiled=True)[0]
    down_grad = down_grad.astype(jnp.float32)
    slot = place % spans
    strip = inner // spans
    def pieces_of(mine):
        return [
            lax.dynamic_slice_in_dim(mine, ((slot + k) % spans) * strip, strip, 1)
            for k in range(spans)
        ]

    def set_out(pieces):
        moved = []
        for k in range(spans):
            moves = [
                (f * chain + c, (c // spans) * chain + f * spans + (c % spans + k) % spans)
                for f in range(owners)
                for c in range(chain)
            ]
            moved.append(lax.ppermute(pieces[k], ("fs", "ctx"), moves))
        return moved

    def put_together(moved):
        whole = jnp.zeros((spans,) + moved[0].shape, jnp.float32)
        for k in range(spans):
            piece = moved[k].astype(jnp.float32)[None]
            whole = lax.dynamic_update_slice_in_dim(whole, piece, (slot - k) % spans, 0)
        return whole.reshape(rows, strip)

    scaled_two = normed_two_grad * gain_two
    residual_grad = grads_in.astype(jnp.float32) + scale_two * (
        scaled_two
        - residual * scale_two * scale_two * jnp.mean(scaled_two * residual, axis=1, keepdims=True)
    )
    gain_two_part = jnp.sum(normed_two_grad * residual * scale_two, axis=0)
    attn_grad = residual_grad.astype(jnp.bfloat16)
    attended_grad = matmul_back(attn_grad, out_full).astype(jnp.bfloat16)
    attended_grad, *gate_pieces = lax.optimization_barrier((attended_grad, *pieces_of(gate_mine)))
    gate_moved = set_out(gate_pieces)
    ended = back(
        owners,
        chain,
        count,
        normed,
        attended_rows,
        attn_grad,
        attended_grad,
        queries,
        lse,
        low[:, None, :],
        cosine,
        sine,
        scale_one,
        gain_two_part[None, :],
        line,
        kin,
        hidden_in.reshape(tokens, width),
        in_full,
    )
    normed_grad, output_turned, query_turned, kv_turned, gain_grads = ended[:5]
    residual_late = lax.optimization_barrier((residual, normed_grad))[0]
    hidden_out = residual_late + out_parts[0].astype(jnp.float32)
    for part in came:
        hidden_out = hidden_out + part.astype(jnp.float32)
    output_grad, query_grad = output_turned.T, query_turned.T
    kv_own = KV_WIDTH // chain
    key_grad, value_grad = kv_turned[:kv_own].T, kv_turned[kv_own:].T
    up_mine, _, *gate_moved = lax.optimization_barrier((up_mine, normed_grad, *gate_moved))
    gate_grad = put_together(gate_moved)
    up_grad = put_together(set_out(pieces_of(up_mine)))
    scaled_one = normed_grad * gain_one
    hidden_grad = residual_grad + scale_one * (
        scaled_one - x * scale_one * scale_one * jnp.mean(scaled_one * x, axis=1, keepdims=True)
    )
    return (
        hidden_out.reshape(batches, length, width),
        hidden_grad.reshape(batches, length, width),
        gain_grads[0],
        query_grad,
        key_grad,
        value_grad,
        output_grad,
        gain_grads[1],
        gate_grad,
        up_grad,
        down_grad,
    )


def solution(mesh):
    tokens_spec = P("fs", "ctx", None)
    rows_spec = P("fs", None)
    block_spec = P("fs", "ctx")
    return jax.shard_map(
        on_device,
        mesh=mesh,
        in_specs=(
            tokens_spec,
            rows_spec,
            P("fs"),
            rows_spec,
            rows_spec,
            rows_spec,
            rows_spec,
            P("fs"),
            rows_spec,
            rows_spec,
            rows_spec,
            tokens_spec,
        ),
        out_specs=(
            tokens_spec,
            tokens_spec,
            P("fs"),
            block_spec,
            block_spec,
            block_spec,
            block_spec,
            P("fs"),
            block_spec,
            block_spec,
            block_spec,
        ),
        check_vma=False,
    )
```
